512 devices in a mesh: pb: 32 (over x, y_lo, core), ka: 16 (over y_hi, z).
Axes of the slice: x: 4, y: 8 (y_hi: 2, y_lo: 4; y = y_hi * 4 + y_lo), z: 8, core: 2. Of those that a mesh axis runs over, the one named last changes fastest.
Arguments:
- query_states: bfloat16 [65536, 512], P(('pb', 'ka')), may hold values from -128 to 128
- out_grad: bfloat16 [65536, 512], P(('pb', 'ka')), may hold values from -192 to 192
- forward_out: bfloat16 [65536, 512], P(('pb', 'ka')), may hold values from -6 to 6
- key_states: bfloat16 [65536, 128], P(('ka', 'pb')), may hold values from -8 to 8
- value_states: bfloat16 [65536, 128], P(('ka', 'pb')), may hold values from -6 to 6
- block_mask: int32 [512, 512], P('pb', 'ka'), may hold values from 0 to 1, as said below
Outputs:
- query_grad: bfloat16 [65536, 512], P(('pb', 'ka'))
- key_grad: bfloat16 [65536, 128], P(('ka', 'pb'))
- value_grad: bfloat16 [65536, 128], P(('ka', 'pb'))
The draws below stay inside these ranges and needn't reach their ends.
Inputs may be any that keep to these rules, and one draw needn't show every extreme that they name: `block_mask`: the tiles of one index of pb and one index of ka (16 query tiles by 32 key tiles) hold at most 32 ones, exactly 32 for some such group; every diagonal tile is 1.
All inputs are finite; a program needn't handle non-finite values.
Results may differ from the reference program's by a relative error of at most 0.015.
Values may be sent and summed in bfloat16 or wider, within the bound.
No kernel may reach another device: no remote copies, remote signals or barrier semaphores. Data moves between devices by JAX's collectives and lax.ppermute only.
A program may use at most 64 MiB of HBM per device.

```python
import math
import jax
import jax.numpy as jnp
from jax import lax

TILE = 128
HD = 128
HQ = 4
QTILES = 16
NB = 512
KTILES = 32
SEQ = 65536
MOST = 32
N_PB = 32
N_KA = 16


def shared_keys(key):
    base = jax.random.normal(jax.random.fold_in(key, 11), (SEQ, HD), jnp.float32)
    base = jnp.clip(base, -6.0, 6.0)
    return base


def draw_key_states(key, part):
    base = shared_keys(key)
    return base.astype(jnp.bfloat16)


def draw_query_states(key, part):
    noise = jax.random.normal(jax.random.fold_in(key, 21), (SEQ, HQ * HD), jnp.float32)
    noise = jnp.clip(noise, -6.0, 6.0)
    return noise.astype(jnp.bfloat16)


def draw_block_mask(key, part):
    devices = N_PB * N_KA
    pairs = QTILES * KTILES
    drawn = jax.random.randint(jax.random.fold_in(key, 31), (N_PB, N_KA), 0, MOST // 2 + 1)
    spikes = jax.random.randint(jax.random.fold_in(key, 32), (N_PB, N_KA), 0, 16) == 0
    forced = jax.random.randint(jax.random.fold_in(key, 33), (), 0, devices)
    device_index = jnp.arange(devices, dtype=jnp.int32).reshape(N_PB, N_KA)
    wanted = jnp.where(spikes | (device_index == forced), MOST, drawn)
    owner = jnp.arange(N_PB, dtype=jnp.int32)[:, None] * QTILES // KTILES == jnp.arange(N_KA, dtype=jnp.int32)[None, :]
    on_diagonal = jnp.where(owner, QTILES, 0)
    allowed = jnp.minimum(wanted, MOST - on_diagonal)
    row_tile = jnp.arange(NB, dtype=jnp.int32)[:, None]
    col_tile = jnp.arange(NB, dtype=jnp.int32)[None, :]
    diagonal = (row_tile == col_tile).astype(jnp.int32)
    local = row_tile % QTILES * KTILES + col_tile % KTILES
    scores = jax.random.randint(jax.random.fold_in(key, 34), (NB, NB), 0, 2 ** 16) * pairs + local + diagonal * 2 ** 30
    grouped = scores.reshape(N_PB, QTILES, N_KA, KTILES).transpose(0, 2, 1, 3).reshape(N_PB, N_KA, pairs)
    ranks = jnp.argsort(jnp.argsort(grouped, axis=-1, stable=True), axis=-1, stable=True)
    picked = (ranks < allowed[:, :, None]).astype(jnp.int32)
    spread_back = picked.reshape(N_PB, N_KA, QTILES, KTILES).transpose(0, 2, 1, 3).reshape(NB, NB)
    return jnp.maximum(spread_back, diagonal).astype(jnp.int32)


def level_of(stream_key, shape, cuts, least, largest):
    def one(dim, shards_of):
        steps = jax.random.uniform(jax.random.fold_in(jax.random.fold_in(stream_key, 6), dim), (shards_of,), jnp.float32, least / len(cuts), largest / len(cuts))
        return jnp.repeat(jnp.exp(steps), shape[dim] // shards_of).reshape((-1,) + (1,) * (len(shape) - dim - 1))

    factor_of = one(*cuts[0])
    for cut in cuts[1:]:
        factor_of = factor_of * one(*cut)
    return factor_of


def scatter_about(own_key, extent, width, limit, shards=(), held_as=jnp.bfloat16):
    values = jax.random.normal(own_key, extent, jnp.float32) * width
    if len(shards) > 0:
        values = level_of(own_key, extent, shards, -0.22, 0.18) * values
    return jnp.clip(values, min=-limit, max=limit).astype(held_as)


def setup_inputs(seed: int = 0) -> dict:
    streams_of = jax.random.split(jax.random.key(seed), 7)
    query_states = draw_query_states(jax.random.fold_in(streams_of[6], 71), 0)
    out_grad = scatter_about(streams_of[1], (SEQ, HQ * HD), 32.0, 192.0, ((0, 512),))
    forward_out = scatter_about(streams_of[2], (SEQ, HQ * HD), 1.0, 6.0, ((0, 512),))
    key_states = draw_key_states(jax.random.fold_in(streams_of[6], 71), 0)
    value_states = scatter_about(streams_of[4], (SEQ, HD), 1.0, 6.0, ((0, 512),))
    block_mask = draw_block_mask(jax.random.fold_in(streams_of[6], 71), 0)
    return dict(query_states=query_states, out_grad=out_grad, forward_out=forward_out, key_states=key_states, value_states=value_states, block_mask=block_mask)


def reference(query_states, out_grad, forward_out, key_states, value_states, block_mask):
    score_scale = 1.0 / math.sqrt(HD)
    row_count = TILE * HQ
    product = out_grad.astype(jnp.float32) * forward_out.astype(jnp.float32)
    delta_half = lax.optimization_barrier(jnp.sum(product.reshape(SEQ, HQ, HD), axis=2)).astype(jnp.bfloat16)
    delta_all = lax.optimization_barrier(delta_half).astype(jnp.float32).reshape(N_PB, QTILES, row_count)

    def one_row(carried, inputs):
        key_acc, value_acc = carried
        row_tile, mask_row, delta_row = inputs
        flat = mask_row.astype(jnp.int32)
        ranked = (1 - flat) * NB + jnp.arange(NB, dtype=jnp.int32)
        pair_order = jnp.argsort(ranked, stable=True).astype(jnp.int32)
        pair_count = jnp.sum(flat).astype(jnp.int32)
        block_counts = lax.optimization_barrier(jnp.sum(flat.reshape(N_KA, KTILES), axis=1)).astype(jnp.int32)
        block_ends = jnp.cumsum(block_counts).astype(jnp.int32)
        block_starts = (block_ends - block_counts).astype(jnp.int32)
        row_start = (row_tile * TILE).astype(jnp.int32)
        query_tile = lax.dynamic_slice_in_dim(query_states, row_start, TILE, 0).reshape(row_count, HD)
        grad_tile = lax.dynamic_slice_in_dim(out_grad, row_start, TILE, 0).reshape(row_count, HD)

        def scores_of(col_tile):
            col_start = (col_tile * TILE).astype(jnp.int32)
            key_tile = lax.dynamic_slice_in_dim(key_states, col_start, TILE, 0)
            scores = jnp.dot(query_tile, key_tile.T, preferred_element_type=jnp.float32) * score_scale
            return (col_start, key_tile, scores)

        def forward(slot_index, current):
            row_max, row_sum = current
            _, _, scores = scores_of(pair_order[slot_index])
            new_max = jnp.maximum(row_max, lax.optimization_barrier(jnp.max(scores, axis=1)))
            new_sum = row_sum * jnp.exp(row_max - new_max) + lax.optimization_barrier(jnp.sum(jnp.exp(scores - new_max[:, None]), axis=1))
            return (new_max, new_sum)
        start_state = (jnp.full((row_count,), -1e+30, jnp.float32), jnp.zeros((row_count,), jnp.float32))
        row_max, row_sum = lax.fori_loop(jnp.int32(0), pair_count, forward, start_state)
        log_total = row_max + jnp.log(row_sum)

        def backward(slot_index, current):
            query_acc, key_part, value_part = current
            col_start, key_tile, scores = scores_of(pair_order[slot_index])
            value_tile = lax.dynamic_slice_in_dim(value_states, col_start, TILE, 0)
            probs = jnp.exp(scores - log_total[:, None])
            probs_half = probs.astype(jnp.bfloat16)
            grad_probs = jnp.dot(grad_tile, value_tile.T, preferred_element_type=jnp.float32)
            grad_scores = (probs * (grad_probs - delta_row[:, None])).astype(jnp.bfloat16)
            query_acc = query_acc + jnp.dot(grad_scores, key_tile, preferred_element_type=jnp.float32)
            key_piece = jnp.dot(grad_scores.T, query_tile, preferred_element_type=jnp.float32)
            value_piece = jnp.dot(probs_half.T, grad_tile, preferred_element_type=jnp.float32)
            key_old = lax.dynamic_slice_in_dim(key_part, col_start, TILE, 0)
            value_old = lax.dynamic_slice_in_dim(value_part, col_start, TILE, 0)
            key_part = lax.dynamic_update_slice_in_dim(key_part, key_old + key_piece, col_start, 0)
            value_part = lax.dynamic_update_slice_in_dim(value_part, value_old + value_piece, col_start, 0)
            return (query_acc, key_part, value_part)

        def per_block(block_index, current):
            query_total, key_part, value_part = current
            empty = jnp.zeros((row_count, HD), jnp.float32)
            query_part, key_part, value_part = lax.fori_loop(block_starts[block_index], block_ends[block_index], backward, (empty, key_part, value_part))
            rounded = lax.optimization_barrier(query_part.astype(jnp.bfloat16)).astype(jnp.float32)
            return (query_total + rounded, key_part, value_part)
        query_total, key_acc, value_acc = lax.fori_loop(jnp.int32(0), jnp.int32(N_KA), per_block, (jnp.zeros((row_count, HD), jnp.float32), key_acc, value_acc))
        return ((key_acc, value_acc), query_total)

    def one_block(carried, inputs):
        key_total, value_total = carried
        block_index, mask_rows, delta_rows = inputs
        rows = (block_index * QTILES + jnp.arange(QTILES, dtype=jnp.int32)).astype(jnp.int32)
        start_carry = (jnp.zeros((SEQ, HD), jnp.float32), jnp.zeros((SEQ, HD), jnp.float32))
        (key_acc, value_acc), query_parts = lax.scan(one_row, start_carry, (rows, mask_rows, delta_rows))
        key_total = key_total + lax.optimization_barrier(key_acc.astype(jnp.bfloat16)).astype(jnp.float32)
        value_total = value_total + lax.optimization_barrier(value_acc.astype(jnp.bfloat16)).astype(jnp.float32)
        return ((key_total, value_total), query_parts)
    outer_carry = (jnp.zeros((SEQ, HD), jnp.float32), jnp.zeros((SEQ, HD), jnp.float32))
    block_ids = jnp.arange(N_PB, dtype=jnp.int32)
    (key_sum, value_sum), query_parts = lax.scan(one_block, outer_carry, (block_ids, block_mask.reshape(N_PB, QTILES, NB), delta_all))
    query_grad = (query_parts.reshape(SEQ, HQ * HD) * score_scale).astype(jnp.bfloat16)
    key_grad = (key_sum * score_scale).astype(jnp.bfloat16)
    value_grad = value_sum.astype(jnp.bfloat16)
    return (query_grad, key_grad, value_grad)
```

```python
import math

import jax
import jax.numpy as jnp
from jax import lax
from jax.experimental import pallas as pl
from jax.experimental.pallas import tpu as pltpu
from jax.sharding import Mesh
from jax.sharding import PartitionSpec as P

TILE = 128
HD = 128
HQ = 4
ROWS = TILE * HQ
NQ = 16
NK = 32
QPAD = 272
LOW = -1e30
SCALE = 1.0 / math.sqrt(HD)
LOG2E = 1.0 / math.log(2.0)
Y = ("yl", "yh")
VMEM_LIMIT = 56 * 1024 * 1024


def dot(a, b, dims):
    return lax.dot_general(a, b, (dims, ((), ())), preferred_element_type=jnp.float32)


def heads(ref, r, first):
    return jnp.concatenate(
        [ref[r, first : first + TILE, h * HD : (h + 1) * HD] for h in range(HQ)], axis=0
    )


def stats_kernel(pairs_ref, count_ref, q_ref, kv_ref, out_ref, m_ref, l_ref):
    m_ref[...] = jnp.full(m_ref.shape, LOW, jnp.float32)
    l_ref[...] = jnp.zeros(l_ref.shape, jnp.float32)

    def visit(s, carry):
        pair = pairs_ref[s]
        r = pair // NK
        j = pair % NK
        scores = dot(kv_ref[j, :, :HD], heads(q_ref, r, 0), ((1,), (1,))) * (SCALE * LOG2E)
        old = m_ref[r]
        new = jnp.maximum(old, jnp.max(scores, axis=0, keepdims=True))
        m_ref[r] = new
        l_ref[r] = l_ref[r] * jnp.exp2(old - new) + jnp.sum(
            jnp.exp2(scores - new), axis=0, keepdims=True
        )
        return carry

    lax.fori_loop(0, count_ref[0], visit, 0)
    total = l_ref[...]
    out_ref[...] = jnp.where(
        total > 0.0, m_ref[...] + jnp.log2(jnp.maximum(total, 1e-30)), LOW
    )


def grad_kernel(pairs_ref, count_ref, q_ref, kv_ref, total_ref, dq_ref, dkv_ref, dq_acc, dkv_acc):
    dq_acc[...] = jnp.zeros(dq_acc.shape, jnp.float32)
    dkv_acc[...] = jnp.zeros(dkv_acc.shape, jnp.float32)

    def visit(s, carry):
        pair = pairs_ref[s]
        r = pair // NK
        j = pair % NK
        k = kv_ref[j, :, :HD]
        v = kv_ref[j, :, HD:]
        q = heads(q_ref, r, 0)
        g = heads(q_ref, r, TILE)
        delta = q_ref[r, 2 * TILE : 2 * TILE + 16, :].astype(jnp.float32)[0:1, :]
        scores = dot(k, q, ((1,), (1,))) * (SCALE * LOG2E)
        probs = jnp.exp2(scores - total_ref[r])
        grad_probs = dot(v, g, ((1,), (1,)))
        grad_scores = (probs * (grad_probs - delta)).astype(jnp.bfloat16)
        dq_acc[r] += dot(k, grad_scores, ((0,), (0,)))
        dkv_acc[j, :, :HD] += dot(grad_scores, q, ((1,), (0,)))
        dkv_acc[j, :, HD:] += dot(probs.astype(jnp.bfloat16), g, ((1,), (0,)))
        return carry

    lax.fori_loop(0, count_ref[0], visit, 0)
    dq_ref[...] = dq_acc[...].astype(jnp.bfloat16)
    dkv_ref[...] = dkv_acc[...].astype(jnp.bfloat16)


def vmem():
    return pl.BlockSpec(memory_space=pltpu.VMEM)


def smem():
    return pl.BlockSpec(memory_space=pltpu.SMEM)


def call_stats(pairs, count, q, kv):
    return pl.pallas_call(
        stats_kernel,
        out_shape=jax.ShapeDtypeStruct((NQ, 1, ROWS), jnp.float32),
        in_specs=[smem(), smem(), vmem(), vmem()],
        out_specs=vmem(),
        scratch_shapes=[
            pltpu.VMEM((NQ, 1, ROWS), jnp.float32),
            pltpu.VMEM((NQ, 1, ROWS), jnp.float32),
        ],
        compiler_params=pltpu.CompilerParams(vmem_limit_bytes=VMEM_LIMIT),
        name="row_statistics",
    )(pairs, count, q, kv)


def call_grad(pairs, count, q, kv, total):
    return pl.pallas_call(
        grad_kernel,
        out_shape=(
            jax.ShapeDtypeStruct((NQ, HD, ROWS), jnp.bfloat16),
            jax.ShapeDtypeStruct((NK, TILE, 2 * HD), jnp.bfloat16),
        ),
        in_specs=[smem(), smem(), vmem(), vmem(), vmem()],
        out_specs=(vmem(), vmem()),
        scratch_shapes=[
            pltpu.VMEM((NQ, HD, ROWS), jnp.float32),
            pltpu.VMEM((NK, TILE, 2 * HD), jnp.float32),
        ],
        compiler_params=pltpu.CompilerParams(vmem_limit_bytes=VMEM_LIMIT),
        name="gradients",
    )(pairs, count, q, kv, total)


def to_everyone(value, axis):
    peers = lax.axis_size(axis)
    return lax.all_to_all(
        jnp.broadcast_to(value[None], (peers, *value.shape)), axis, 0, 0, tiled=True
    )


def swap_cores(value):
    return lax.ppermute(value, "c", [(0, 1), (1, 0)])


def list_pairs(tile_mask):
    flat = tile_mask.reshape(-1) > 0
    number = flat.shape[0]
    place = jnp.arange(number, dtype=jnp.int32)
    ones = flat.astype(jnp.int32)
    before = jnp.sum(
        jnp.where(place[None, :] < place[:, None], ones[None, :], 0), axis=1
    )
    here = (before[None, :] == place[:, None]) & flat[None, :]
    return jnp.sum(jnp.where(here, place[None, :], 0), axis=1), jnp.sum(ones)[None]


def body(query_states, out_grad, forward_out, key_states, value_states, block_mask):
    core = lax.axis_index("c")
    y_hi = lax.axis_index("yh")
    y_lo = lax.axis_index("yl")
    product = out_grad.astype(jnp.float32) * forward_out.astype(jnp.float32)
    delta = jnp.sum(product.reshape(TILE, HQ, HD), axis=2).astype(jnp.bfloat16)
    delta_rows = jnp.pad(delta.T.reshape(1, ROWS), ((0, 15), (0, 0)))
    q_own = jnp.concatenate([query_states, out_grad, delta_rows], axis=0)
    q_all = lax.all_gather(q_own, ("c", "z"), axis=0, tiled=False)

    mask_rows = jnp.pad(block_mask.astype(jnp.bfloat16).reshape(2, 2 * HD), ((0, 6), (0, 0)))
    kv_own = jnp.concatenate(
        [jnp.concatenate([key_states, value_states], axis=1), mask_rows], axis=0
    )
    kv_y = to_everyone(kv_own, Y)
    kv_all = to_everyone(kv_y[:, :TILE], "x").reshape(NK, TILE, 2 * HD)

    mine = lax.dynamic_slice_in_dim(kv_y[:, TILE : TILE + 2], y_lo * 2, 2, 0)
    mine = mine.reshape(2, 16, 32)
    other = swap_cores(mine)
    first = jnp.where(core == 0, mine, other)
    second = jnp.where(core == 0, other, mine)
    both = jnp.stack([first, second])
    both = lax.dynamic_slice_in_dim(both, y_hi * 8, 8, 2)
    both = both.reshape(2, 2, 8, 16, 2)
    both = jnp.where(core == 0, both[..., 0], both[..., 1])
    mask = both.transpose(0, 2, 3, 1).reshape(NQ, NK)
    pairs, count = list_pairs(mask)

    part = call_stats(pairs, count, q_all, kv_all)
    parts = to_everyone(part.reshape(NQ * ROWS // HD, HD), ("c", "z"))
    top = jnp.max(parts, axis=0)
    total = top + jnp.log2(jnp.sum(jnp.exp2(parts - top[None]), axis=0))
    total = total.reshape(NQ, 1, ROWS)
    dq, dkv = call_grad(pairs, count, q_all, kv_all, total)

    dq = dq.reshape(2, 8, HD, ROWS)
    kept = jnp.where(core == 0, dq[0], dq[1])
    sent = jnp.where(core == 0, dq[1], dq[0])
    got = swap_cores(sent)
    chip = (kept.astype(jnp.float32) + got.astype(jnp.float32)).astype(jnp.bfloat16)
    dq_own = lax.psum_scatter(chip, "z", scatter_dimension=0, tiled=True)[0]
    dq_own = (dq_own.astype(jnp.float32) * SCALE).astype(jnp.bfloat16)
    query_grad = dq_own.reshape(HD, HQ, TILE).transpose(2, 1, 0).reshape(TILE, HQ * HD)

    over_x = lax.all_to_all(dkv.reshape(4, 8 * TILE, 2 * HD), "x", 0, 0, tiled=True)
    over_x = over_x.astype(jnp.float32).sum(axis=0).astype(jnp.bfloat16)
    over_y = lax.all_to_all(over_x.reshape(8, TILE, 2 * HD), Y, 0, 0, tiled=True)
    sums = over_y.astype(jnp.float32).sum(axis=0)
    key_grad = (sums[:, :HD] * SCALE).astype(jnp.bfloat16)
    value_grad = sums[:, HD:].astype(jnp.bfloat16)
    return query_grad, key_grad, value_grad


def solution(mesh):
    torus = Mesh(mesh.devices.reshape(4, 4, 2, 2, 8), ("x", "yl", "c", "yh", "z"))
    queries = P(("x", "yl", "c", "yh", "z"), None)
    keys = P(("yh", "z", "x", "yl", "c"), None)
    return jax.shard_map(
        body,
        mesh=torus,
        in_specs=(queries, queries, queries, keys, keys, P(("x", "yl", "c"), ("yh", "z"))),
        out_specs=(queries, keys, keys),
        check_vma=False,
    )
```

```python
import math

import jax
import jax.numpy as jnp
from jax import lax
from jax.experimental import pallas as pl
from jax.experimental.pallas import tpu as pltpu
from jax.sharding import Mesh
from jax.sharding import PartitionSpec as P

TILE = 128
HD = 128
HQ = 4
ROWS = TILE * HQ
NQ = 16
NK = 32
QPAD = 272
LOW = -1e30
SCALE = 1.0 / math.sqrt(HD)
LOG2E = 1.0 / math.log(2.0)
Y = ("yl", "yh")
STEP = 4


def dot(a, b, dims):
    return lax.dot_general(a, b, (dims, ((), ())), preferred_element_type=jnp.float32)


def heads(ref, r, first):
    return jnp.concatenate(
        [ref[r, first : first + TILE, h * HD : (h + 1) * HD] for h in range(HQ)], axis=0
    )


def unpack(pairs_ref, s):
    pair = pairs_ref[s]
    r, j = pair >> 6, pair & 63
    return r, j, jnp.minimum(r, NQ - 1), jnp.minimum(j, NK - 1)


def blocks_of(count_ref, per_step):
    return (count_ref[0] + (per_step - 1)) // per_step


def stats_kernel(pairs_ref, count_ref, q_hbm, kv_hbm, out_ref, q_ref, k_ref, m_ref, l_ref, sems):
    copies = (
        pltpu.make_async_copy(q_hbm.at[:, pl.ds(0, TILE), :], q_ref, sems.at[0]),
        pltpu.make_async_copy(kv_hbm.at[:, :, pl.ds(0, HD)], k_ref, sems.at[1]),
    )
    for copy in copies:
        copy.start()
    m_ref[...] = jnp.full(m_ref.shape, LOW, jnp.float32)
    l_ref[...] = jnp.zeros(l_ref.shape, jnp.float32)
    for copy in copies:
        copy.wait()

    def visit(i, carry):
        found = []
        for u in range(STEP):
            r, _, rq, jk = unpack(pairs_ref, i * STEP + u)
            scores = dot(k_ref[jk], heads(q_ref, rq, 0), ((1,), (1,))) * (SCALE * LOG2E)
            top = jnp.max(scores, axis=0, keepdims=True)
            found.append((r, top, jnp.sum(jnp.exp2(scores - top), axis=0, keepdims=True)))
        for r, top, total in found:
            old = m_ref[r]
            new = jnp.maximum(old, top)
            m_ref[r] = new
            l_ref[r] = l_ref[r] * jnp.exp2(old - new) + total * jnp.exp2(top - new)
        return carry

    lax.fori_loop(0, blocks_of(count_ref, STEP), visit, 0)
    total = l_ref[...][:NQ]
    out_ref[...] = jnp.where(
        total > 0.0, m_ref[...][:NQ] + jnp.log2(jnp.maximum(total, 1e-30)), LOW
    )


def weights_of(q_ref, kv_ref, total_ref, rq, jk):
    scores = dot(kv_ref[jk, :, :HD], heads(q_ref, rq, 0), ((1,), (1,))) * (SCALE * LOG2E)
    probs = jnp.exp2(scores - total_ref[rq])
    grad_probs = dot(kv_ref[jk, :, HD:], heads(q_ref, rq, TILE), ((1,), (1,)))
    delta = q_ref[rq, 2 * TILE : 2 * TILE + 16, :].astype(jnp.float32)[0:1, :]
    return probs, (probs * (grad_probs - delta)).astype(jnp.bfloat16)


def load(q_hbm, kv_hbm, total_hbm, q_ref, kv_ref, total_ref, sems):
    copies = (
        pltpu.make_async_copy(q_hbm, q_ref, sems.at[0]),
        pltpu.make_async_copy(kv_hbm, kv_ref, sems.at[1]),
        pltpu.make_async_copy(total_hbm, total_ref, sems.at[2]),
    )
    for copy in copies:
        copy.start()
    return copies


def query_kernel(
    pairs_ref, count_ref, core_ref, q_hbm, kv_hbm, total_hbm, out_ref,
    q_ref, kv_ref, total_ref, acc, ds_ref, sems,
):
    copies = load(q_hbm, kv_hbm, total_hbm, q_ref, kv_ref, total_ref, sems)
    acc[...] = jnp.zeros(acc.shape, jnp.float32)
    for copy in copies:
        copy.wait()

    def visit(i, carry):
        where = [unpack(pairs_ref, i * STEP + u) for u in range(STEP)]
        for u, (_, _, rq, jk) in enumerate(where):
            ds_ref[u] = weights_of(q_ref, kv_ref, total_ref, rq, jk)[1]
        parts = [dot(kv_ref[w[3], :, :HD], ds_ref[u], ((0,), (0,))) for u, w in enumerate(where)]
        for (r, _, _, _), part in zip(where, parts):
            acc[r] += part
        return carry

    lax.fori_loop(0, blocks_of(count_ref, STEP), visit, 0)
    core = core_ref[0]
    for r in range(NQ):
        out_ref[(r // 8) ^ core, r % 8] = acc[r].astype(jnp.bfloat16)


def key_kernel(
    pairs_ref, count_ref, q_hbm, kv_hbm, total_hbm, out_ref,
    q_ref, kv_ref, total_ref, acc, p_ref, ds_ref, sems,
):
    copies = load(q_hbm, kv_hbm, total_hbm, q_ref, kv_ref, total_ref, sems)
    acc[...] = jnp.zeros(acc.shape, jnp.float32)
    for copy in copies:
        copy.wait()

    def visit(i, carry):
        where = [unpack(pairs_ref, i * STEP + u) for u in range(STEP)]
        for u, (_, _, rq, jk) in enumerate(where):
            probs, grad_scores = weights_of(q_ref, kv_ref, total_ref, rq, jk)
            p_ref[u] = probs.astype(jnp.bfloat16)
            ds_ref[u] = grad_scores
        parts = [
            (
                dot(ds_ref[u], heads(q_ref, w[2], 0), ((1,), (0,))),
                dot(p_ref[u], heads(q_ref, w[2], TILE), ((1,), (0,))),
            )
            for u, w in enumerate(where)
        ]
        for (_, j, _, _), (of_key, of_value) in zip(where, parts):
            acc[j, :, :HD] += of_key
            acc[j, :, HD:] += of_value
        return carry

    lax.fori_loop(0, blocks_of(count_ref, STEP), visit, 0)
    out_ref[...] = acc[:NK].astype(jnp.bfloat16)


def vmem():
    return pl.BlockSpec(memory_space=pltpu.VMEM)


def smem():
    return pl.BlockSpec(memory_space=pltpu.SMEM)


def anywhere():
    return pl.BlockSpec(memory_space=pl.ANY)


def params(mib):
    return pltpu.CompilerParams(vmem_limit_bytes=mib * 1024 * 1024)


def loaded():
    return [
        pltpu.VMEM((NQ, QPAD, ROWS), jnp.bfloat16),
        pltpu.VMEM((NK, TILE, 2 * HD), jnp.bfloat16),
        pltpu.VMEM((NQ, 1, ROWS), jnp.float32),
    ]


def call_stats(pairs, count, q, kv):
    return pl.pallas_call(
        stats_kernel,
        out_shape=jax.ShapeDtypeStruct((NQ, 1, ROWS), jnp.float32),
        in_specs=[smem(), smem(), anywhere(), anywhere()],
        out_specs=vmem(),
        scratch_shapes=[
            pltpu.VMEM((NQ, TILE, ROWS), jnp.bfloat16),
            pltpu.VMEM((NK, TILE, HD), jnp.bfloat16),
            pltpu.VMEM((NQ + 1, 1, ROWS), jnp.float32),
            pltpu.VMEM((NQ + 1, 1, ROWS), jnp.float32),
            pltpu.SemaphoreType.DMA((2,)),
        ],
        compiler_params=params(60),
        cost_estimate=pl.CostEstimate(
            flops=10_000_000_000, bytes_accessed=4 << 20, transcendentals=0
        ),
        name="row_statistics",
    )(pairs, count, q, kv)


def call_query(pairs, count, core, q, kv, total):
    return pl.pallas_call(
        query_kernel,
        out_shape=jax.ShapeDtypeStruct((2, NQ // 2, HD, ROWS), jnp.bfloat16),
        in_specs=[smem(), smem(), smem(), anywhere(), anywhere(), anywhere()],
        out_specs=vmem(),
        scratch_shapes=loaded()
        + [
            pltpu.VMEM((NQ + 1, HD, ROWS), jnp.float32),
            pltpu.VMEM((STEP, TILE, ROWS), jnp.bfloat16),
            pltpu.SemaphoreType.DMA((3,)),
        ],
        compiler_params=params(60),
        cost_estimate=pl.CostEstimate(
            flops=10_000_000_000, bytes_accessed=8 << 20, transcendentals=0
        ),
        name="query_gradient",
    )(pairs, count, core, q, kv, total)


def call_key(pairs, count, q, kv, total):
    return pl.pallas_call(
        key_kernel,
        out_shape=jax.ShapeDtypeStruct((NK, TILE, 2 * HD), jnp.bfloat16),
        in_specs=[smem(), smem(), anywhere(), anywhere(), anywhere()],
        out_specs=vmem(),
        scratch_shapes=loaded()
        + [
            pltpu.VMEM((NK + 1, TILE, 2 * HD), jnp.float32),
            pltpu.VMEM((STEP, TILE, ROWS), jnp.bfloat16),
            pltpu.VMEM((STEP, TILE, ROWS), jnp.bfloat16),
            pltpu.SemaphoreType.DMA((3,)),
        ],
        compiler_params=params(60),
        cost_estimate=pl.CostEstimate(
            flops=10_000_000_000, bytes_accessed=8 << 20, transcendentals=0
        ),
        name="key_gradient",
    )(pairs, count, q, kv, total)


def to_everyone(value, axis):
    peers = lax.axis_size(axis)
    return lax.all_to_all(
        jnp.broadcast_to(value[None], (peers, *value.shape)), axis, 0, 0, tiled=True
    )


def swap_cores(value):
    return lax.ppermute(value, "c", [(0, 1), (1, 0)])


def list_pairs(tile_mask):
    flat = tile_mask.reshape(-1) > 0
    number = flat.shape[0]
    place = jnp.arange(number, dtype=jnp.int32)
    ones = flat.astype(jnp.int32)
    before = jnp.sum(
        jnp.where(place[None, :] < place[:, None], ones[None, :], 0), axis=1
    )
    here = (before[None, :] == place[:, None]) & flat[None, :]
    spare = jnp.where(place < jnp.sum(ones), 0, NQ * 64 + NK)
    code = place // NK * 64 + place % NK
    pairs = jnp.sum(jnp.where(here, code[None, :], 0), axis=1) + spare
    return jnp.pad(pairs, (0, STEP), constant_values=NQ * 64 + NK), jnp.sum(ones)[None]


def body(query_states, out_grad, forward_out, key_states, value_states, block_mask):
    core = lax.axis_index("c")
    y_hi = lax.axis_index("yh")
    y_lo = lax.axis_index("yl")
    product = out_grad.astype(jnp.float32) * forward_out.astype(jnp.float32)
    delta = jnp.sum(product.reshape(TILE, HQ, HD), axis=2).astype(jnp.bfloat16)
    delta_rows = jnp.pad(delta.T.reshape(1, ROWS), ((0, 15), (0, 0)))
    q_own = jnp.concatenate([query_states, out_grad, delta_rows], axis=0)
    q_all = lax.all_gather(q_own, ("c", "z"), axis=0, tiled=False)

    mask_rows = jnp.pad(block_mask.astype(jnp.bfloat16).reshape(2, 2 * HD), ((0, 6), (0, 0)))
    kv_own = jnp.concatenate(
        [jnp.concatenate([key_states, value_states], axis=1), mask_rows], axis=0
    )
    kv_y = to_everyone(kv_own, Y)
    kv_all = to_everyone(kv_y[:, :TILE], "x").reshape(NK, TILE, 2 * HD)

    mine = lax.dynamic_slice_in_dim(kv_y[:, TILE : TILE + 2], y_lo * 2, 2, 0)
    mine = mine.reshape(2, 16, 32)
    other = swap_cores(mine)
    first = jnp.where(core == 0, mine, other)
    second = jnp.where(core == 0, other, mine)
    both = jnp.stack([first, second])
    both = lax.dynamic_slice_in_dim(both, y_hi * 8, 8, 2)
    both = both.reshape(2, 2, 8, 16, 2)
    both = jnp.where(core == 0, both[..., 0], both[..., 1])
    mask = both.transpose(0, 2, 3, 1).reshape(NQ, NK)
    pairs, count = list_pairs(mask)

    part = call_stats(pairs, count, q_all, kv_all)
    parts = to_everyone(part.reshape(NQ * ROWS // HD, HD), ("c", "z"))
    dq = call_query(pairs, count, core[None], q_all, kv_all, part)
    kept, got = dq[0], swap_cores(dq[1])

    top = jnp.max(parts, axis=0)
    total = top + jnp.log2(jnp.sum(jnp.exp2(parts - top[None]), axis=0))
    dkv = call_key(pairs, count, q_all, kv_all, total.reshape(NQ, 1, ROWS))

    own_part = lax.dynamic_index_in_dim(parts, core * 8 + lax.axis_index("z"), 0, False)
    far_part = lax.dynamic_index_in_dim(parts, (1 - core) * 8 + lax.axis_index("z"), 0, False)
    own_w, far_w = (
        lax.dynamic_slice_in_dim(jnp.exp2(p - total), core * 32, 32, 0).reshape(8, 1, ROWS)
        for p in (own_part, far_part)
    )
    chip = (kept.astype(jnp.float32) * own_w + got.astype(jnp.float32) * far_w).astype(
        jnp.bfloat16
    )
    dq_own = lax.psum_scatter(chip, "z", scatter_dimension=0, tiled=True)[0]
    dq_own = (dq_own.astype(jnp.float32) * SCALE).astype(jnp.bfloat16)
    query_grad = dq_own.reshape(HD, HQ, TILE).transpose(2, 1, 0).reshape(TILE, HQ * HD)

    over_x = lax.all_to_all(dkv.reshape(4, 8 * TILE, 2 * HD), "x", 0, 0, tiled=True)
    over_x = over_x.astype(jnp.float32).sum(axis=0).astype(jnp.bfloat16)
    over_y = lax.all_to_all(over_x.reshape(8, TILE, 2 * HD), Y, 0, 0, tiled=True)
    sums = over_y.astype(jnp.float32).sum(axis=0)
    key_grad = (sums[:, :HD] * SCALE).astype(jnp.bfloat16)
    value_grad = sums[:, HD:].astype(jnp.bfloat16)
    return query_grad, key_grad, value_grad


def solution(mesh):
    torus = Mesh(mesh.devices.reshape(4, 4, 2, 2, 8), ("x", "yl", "c", "yh", "z"))
    queries = P(("x", "yl", "c", "yh", "z"), None)
    keys = P(("yh", "z", "x", "yl", "c"), None)
    return jax.shard_map(
        body,
        mesh=torus,
        in_specs=(queries, queries, queries, keys, keys, P(("x", "yl", "c"), ("yh", "z"))),
        out_specs=(queries, keys, keys),
        check_vma=False,
    )
```

```python
import math

import jax
import jax.numpy as jnp
from jax import lax
from jax.experimental import pallas as pl
from jax.experimental.pallas import tpu as pltpu
from jax.sharding import Mesh
from jax.sharding import PartitionSpec as P

TILE = 128
HD = 128
HQ = 4
ROWS = TILE * HQ
NQ = 16
NK = 32
NY = 8
NZ = 8
QPAD = 272
LOW = -1e30
SCALE = 1.0 / math.sqrt(HD)
LOG2E = 1.0 / math.log(2.0)
Y = ("yl", "yh")
STEP = 4


def dot(a, b, dims):
    return lax.dot_general(a, b, (dims, ((), ())), preferred_element_type=jnp.float32)


def heads(ref, r, first):
    return jnp.concatenate(
        [ref[r, first : first + TILE, h * HD : (h + 1) * HD] for h in range(HQ)], axis=0
    )


def unpack(pairs_ref, s):
    pair = pairs_ref[s]
    r, j = pair >> 6, pair & 63
    return r, j, jnp.minimum(r, NQ - 1), jnp.minimum(j, NK - 1)


def blocks_of(count_ref, per_step):
    return (count_ref[0] + (per_step - 1)) // per_step


def stats_kernel(
    pairs_ref, count_ref, q_hbm, kv0, kv1, kv2, kv3, out_ref, q_ref, k_ref, m_ref, l_ref, sems
):
    copies = [pltpu.make_async_copy(q_hbm.at[:, pl.ds(0, TILE), :], q_ref, sems.at[0])]
    for n, piece in enumerate((kv0, kv1, kv2, kv3)):
        source = piece.at[:, pl.ds(0, TILE), pl.ds(0, HD)]
        copies.append(
            pltpu.make_async_copy(source, k_ref.at[pl.ds(n * NY, NY)], sems.at[n + 1])
        )
    for copy in copies:
        copy.start()
    m_ref[...] = jnp.full(m_ref.shape, LOW, jnp.float32)
    l_ref[...] = jnp.zeros(l_ref.shape, jnp.float32)
    for copy in copies:
        copy.wait()

    def visit(i, carry):
        found = []
        for u in range(STEP):
            r, _, rq, jk = unpack(pairs_ref, i * STEP + u)
            scores = dot(k_ref[jk], heads(q_ref, rq, 0), ((1,), (1,))) * (SCALE * LOG2E)
            top = jnp.max(scores, axis=0, keepdims=True)
            found.append((r, top, jnp.sum(jnp.exp2(scores - top), axis=0, keepdims=True)))
        for r, top, total in found:
            old = m_ref[r]
            new = jnp.maximum(old, top)
            m_ref[r] = new
            l_ref[r] = l_ref[r] * jnp.exp2(old - new) + total * jnp.exp2(top - new)
        return carry

    lax.fori_loop(0, blocks_of(count_ref, STEP), visit, 0)
    total = l_ref[...][:NQ]
    out_ref[...] = jnp.where(
        total > 0.0, m_ref[...][:NQ] + jnp.log2(jnp.maximum(total, 1e-30)), LOW
    )


def weights_of(q_ref, kv_ref, total_ref, rq, jk):
    scores = dot(kv_ref[jk, :, :HD], heads(q_ref, rq, 0), ((1,), (1,))) * (SCALE * LOG2E)
    probs = jnp.exp2(scores - total_ref[rq])
    grad_probs = dot(kv_ref[jk, :, HD:], heads(q_ref, rq, TILE), ((1,), (1,)))
    delta = q_ref[rq, 2 * TILE : 2 * TILE + 16, :].astype(jnp.float32)[0:1, :]
    return probs, (probs * (grad_probs - delta)).astype(jnp.bfloat16)


def load(q_hbm, pieces, q_ref, kv_ref, sems):
    copies = [pltpu.make_async_copy(q_hbm, q_ref, sems.at[0])]
    for n, piece in enumerate(pieces):
        source = piece.at[:, pl.ds(0, TILE), :]
        copies.append(
            pltpu.make_async_copy(source, kv_ref.at[pl.ds(n * NY, NY)], sems.at[n + 1])
        )
    for copy in copies:
        copy.start()
    return copies


def query_kernel(
    pairs_ref, count_ref, core_ref, q_hbm, kv0, kv1, kv2, kv3, total_ref, kept_ref, sent_ref,
    q_ref, kv_ref, acc, ds_ref, sems,
):
    copies = load(q_hbm, (kv0, kv1, kv2, kv3), q_ref, kv_ref, sems)
    acc[...] = jnp.zeros(acc.shape, jnp.float32)
    for copy in copies:
        copy.wait()

    def visit(i, carry):
        where = [unpack(pairs_ref, i * STEP + u) for u in range(STEP)]
        for u, (_, _, rq, jk) in enumerate(where):
            ds_ref[u] = weights_of(q_ref, kv_ref, total_ref, rq, jk)[1]
        parts = [dot(kv_ref[w[3], :, :HD], ds_ref[u], ((0,), (0,))) for u, w in enumerate(where)]
        for (r, _, _, _), part in zip(where, parts):
            acc[r] += part
        return carry

    lax.fori_loop(0, blocks_of(count_ref, STEP), visit, 0)
    mine = core_ref[0] * NZ
    for n in range(NZ):
        kept_ref[n] = acc[mine + n].astype(jnp.bfloat16)
        sent_ref[n] = acc[NZ - mine + n].astype(jnp.bfloat16)


def key_kernel(
    pairs_ref, count_ref, core_ref, q_hbm, kv0, kv1, kv2, kv3, total_ref, own_ref, far_ref,
    kept_hbm, got_hbm, chip_hbm, out0, out1, out2, out3,
    q_ref, kv_ref, acc, p_ref, ds_ref, kept_ref, got_ref, chip_ref, sems,
):
    two = (
        pltpu.make_async_copy(kept_hbm, kept_ref, sems.at[5]),
        pltpu.make_async_copy(got_hbm, got_ref, sems.at[6]),
    )
    for copy in two:
        copy.start()
    copies = load(q_hbm, (kv0, kv1, kv2, kv3), q_ref, kv_ref, sems)
    acc[...] = jnp.zeros(acc.shape, jnp.float32)
    for copy in two:
        copy.wait()
    for n in range(NZ):
        r = core_ref[0] * NZ + n
        own = jnp.exp2(own_ref[r] - total_ref[r])
        far = jnp.exp2(far_ref[r] - total_ref[r])
        chip_ref[n] = (
            kept_ref[n].astype(jnp.float32) * own + got_ref[n].astype(jnp.float32) * far
        ).astype(jnp.bfloat16)
    leave = pltpu.make_async_copy(chip_ref, chip_hbm, sems.at[7])
    leave.start()
    for copy in copies:
        copy.wait()

    def visit(i, carry):
        where = [unpack(pairs_ref, i * STEP + u) for u in range(STEP)]
        for u, (_, _, rq, jk) in enumerate(where):
            probs, grad_scores = weights_of(q_ref, kv_ref, total_ref, rq, jk)
            p_ref[u] = probs.astype(jnp.bfloat16)
            ds_ref[u] = grad_scores
        parts = [
            (
                dot(ds_ref[u], heads(q_ref, w[2], 0), ((1,), (0,))),
                dot(p_ref[u], heads(q_ref, w[2], TILE), ((1,), (0,))),
            )
            for u, w in enumerate(where)
        ]
        for (_, j, _, _), (of_key, of_value) in zip(where, parts):
            acc[j, :, :HD] += of_key
            acc[j, :, HD:] += of_value
        return carry

    lax.fori_loop(0, blocks_of(count_ref, STEP), visit, 0)
    for n, out_ref in enumerate((out0, out1, out2, out3)):
        out_ref[...] = acc[n * NY : (n + 1) * NY].astype(jnp.bfloat16)
    leave.wait()


def vmem():
    return pl.BlockSpec(memory_space=pltpu.VMEM)


def smem():
    return pl.BlockSpec(memory_space=pltpu.SMEM)


def anywhere():
    return pl.BlockSpec(memory_space=pl.ANY)


def params():
    return pltpu.CompilerParams(vmem_limit_bytes=60 * 1024 * 1024)


def cost(mib):
    return pl.CostEstimate(flops=10_000_000_000, bytes_accessed=mib << 20, transcendentals=0)


def loaded():
    return [
        pltpu.VMEM((NQ, QPAD, ROWS), jnp.bfloat16),
        pltpu.VMEM((NK, TILE, 2 * HD), jnp.bfloat16),
    ]


def call_stats(pairs, count, q, kv):
    return pl.pallas_call(
        stats_kernel,
        out_shape=jax.ShapeDtypeStruct((NQ, 1, ROWS), jnp.float32),
        in_specs=[smem(), smem()] + [anywhere()] * 5,
        out_specs=vmem(),
        scratch_shapes=[
            pltpu.VMEM((NQ, TILE, ROWS), jnp.bfloat16),
            pltpu.VMEM((NK, TILE, HD), jnp.bfloat16),
            pltpu.VMEM((NQ + 1, 1, ROWS), jnp.float32),
            pltpu.VMEM((NQ + 1, 1, ROWS), jnp.float32),
            pltpu.SemaphoreType.DMA((5,)),
        ],
        compiler_params=params(),
        cost_estimate=cost(4),
        name="row_statistics",
    )(pairs, count, q, *kv)


def call_query(pairs, count, core, q, kv, part):
    half = jax.ShapeDtypeStruct((NZ, HD, ROWS), jnp.bfloat16)
    return pl.pallas_call(
        query_kernel,
        out_shape=(half, half),
        in_specs=[smem()] * 3 + [anywhere()] * 5 + [vmem()],
        out_specs=(vmem(), vmem()),
        scratch_shapes=loaded()
        + [
            pltpu.VMEM((NQ + 1, HD, ROWS), jnp.float32),
            pltpu.VMEM((STEP, TILE, ROWS), jnp.bfloat16),
            pltpu.SemaphoreType.DMA((5,)),
        ],
        compiler_params=params(),
        cost_estimate=cost(8),
        name="query_gradient",
    )(pairs, count, core, q, *kv, part)


def call_key(pairs, count, core, q, kv, total, own, far, kept, got):
    quarter = jax.ShapeDtypeStruct((NY, TILE, 2 * HD), jnp.bfloat16)
    half = pltpu.VMEM((NZ, HD, ROWS), jnp.bfloat16)
    return pl.pallas_call(
        key_kernel,
        out_shape=(jax.ShapeDtypeStruct((NZ, HD, ROWS), jnp.bfloat16),) + (quarter,) * 4,
        in_specs=[smem()] * 3 + [anywhere()] * 5 + [vmem()] * 3 + [anywhere()] * 2,
        out_specs=(anywhere(),) + (vmem(),) * 4,
        scratch_shapes=loaded()
        + [
            pltpu.VMEM((NK + 1, TILE, 2 * HD), jnp.float32),
            pltpu.VMEM((STEP, TILE, ROWS), jnp.bfloat16),
            pltpu.VMEM((STEP, TILE, ROWS), jnp.bfloat16),
            half,
            half,
            half,
            pltpu.SemaphoreType.DMA((8,)),
        ],
        compiler_params=params(),
        cost_estimate=cost(8),
        name="key_gradient",
    )(pairs, count, core, q, *kv, total, own, far, kept, got)


def to_everyone(value, axis):
    peers = lax.axis_size(axis)
    return lax.all_to_all(
        jnp.broadcast_to(value[None], (peers, *value.shape)), axis, 0, 0, tiled=True
    )


def along_x(value, by):
    return lax.ppermute(value, "x", [(n, (n + by) % 4) for n in range(4)])


def swap_cores(value):
    return lax.ppermute(value, "c", [(0, 1), (1, 0)])


def list_pairs(tile_mask):
    flat = tile_mask.reshape(-1) > 0
    number = flat.shape[0]
    place = jnp.arange(number, dtype=jnp.int32)
    ones = flat.astype(jnp.int32)
    before = jnp.sum(
        jnp.where(place[None, :] < place[:, None], ones[None, :], 0), axis=1
    )
    here = (before[None, :] == place[:, None]) & flat[None, :]
    spare = jnp.where(place < jnp.sum(ones), 0, NQ * 64 + NK)
    code = place // NK * 64 + place % NK
    pairs = jnp.sum(jnp.where(here, code[None, :], 0), axis=1) + spare
    return jnp.pad(pairs, (0, STEP), constant_values=NQ * 64 + NK), jnp.sum(ones)[None]


def body(query_states, out_grad, forward_out, key_states, value_states, block_mask):
    core = lax.axis_index("c")
    y_hi = lax.axis_index("yh")
    y_lo = lax.axis_index("yl")
    product = out_grad.astype(jnp.float32) * forward_out.astype(jnp.float32)
    delta = jnp.sum(product.reshape(TILE, HQ, HD), axis=2).astype(jnp.bfloat16)
    delta_rows = jnp.pad(delta.T.reshape(1, ROWS), ((0, 15), (0, 0)))
    q_own = jnp.concatenate([query_states, out_grad, delta_rows], axis=0)
    q_all = lax.all_gather(q_own, ("c", "z"), axis=0, tiled=False)

    mask_rows = jnp.pad(block_mask.astype(jnp.bfloat16).reshape(2, 2 * HD), ((0, 14), (0, 0)))
    kv_own = jnp.concatenate(
        [jnp.concatenate([key_states, value_states], axis=1), mask_rows], axis=0
    )
    kv_y = to_everyone(kv_own, Y)
    kv_all = (kv_y, along_x(kv_y, 1), along_x(kv_y, -1), along_x(kv_y, 2))

    mine = lax.dynamic_slice_in_dim(kv_y[:, TILE : TILE + 2], y_lo * 2, 2, 0)
    mine = mine.reshape(2, 16, 32)
    other = swap_cores(mine)
    first = jnp.where(core == 0, mine, other)
    second = jnp.where(core == 0, other, mine)
    both = jnp.stack([first, second])
    both = lax.dynamic_slice_in_dim(both, y_hi * 8, 8, 2)
    both = both.reshape(2, 2, 8, 16, 2)
    both = jnp.where(core == 0, both[..., 0], both[..., 1])
    mask = both.transpose(0, 2, 3, 1).reshape(NQ, 4, NY)
    turned = lax.dynamic_slice_in_dim(jnp.concatenate([mask, mask], 1), lax.axis_index("x"), 4, 1)
    mask = jnp.concatenate([turned[:, :1], turned[:, 3:], turned[:, 1:3]], axis=1).reshape(NQ, NK)
    pairs, count = list_pairs(mask)

    part = call_stats(pairs, count, q_all, kv_all)
    parts = to_everyone(part.reshape(NQ * ROWS // HD, HD), ("c", "z"))
    kept, sent = call_query(pairs, count, core[None], q_all, kv_all, part)
    got = swap_cores(sent)

    top = jnp.max(parts, axis=0)
    total = top + jnp.log2(jnp.sum(jnp.exp2(parts - top[None]), axis=0))
    total = total.reshape(NQ, 1, ROWS)
    far = lax.dynamic_index_in_dim(parts, (1 - core) * NZ + lax.axis_index("z"), 0, False)
    far = far.reshape(NQ, 1, ROWS)
    chip, here, back, ahead, across = call_key(
        pairs, count, core[None], q_all, kv_all, total, part, far, kept, got
    )

    dq_own = lax.psum_scatter(chip, "z", scatter_dimension=0, tiled=True)[0]
    dq_own = (dq_own.astype(jnp.float32) * SCALE).astype(jnp.bfloat16)
    query_grad = dq_own.reshape(HD, HQ, TILE).transpose(2, 1, 0).reshape(TILE, HQ * HD)

    over_x = (here, along_x(across, 2), along_x(back, -1), along_x(ahead, 1))
    over_x = sum(p.astype(jnp.float32) for p in over_x).astype(jnp.bfloat16)
    over_y = lax.all_to_all(over_x, Y, 0, 0, tiled=True)
    sums = over_y.astype(jnp.float32).sum(axis=0)
    key_grad = (sums[:, :HD] * SCALE).astype(jnp.bfloat16)
    value_grad = sums[:, HD:].astype(jnp.bfloat16)
    return query_grad, key_grad, value_grad


def solution(mesh):
    torus = Mesh(mesh.devices.reshape(4, 4, 2, 2, 8), ("x", "yl", "c", "yh", "z"))
    queries = P(("x", "yl", "c", "yh", "z"), None)
    keys = P(("yh", "z", "x", "yl", "c"), None)
    return jax.shard_map(
        body,
        mesh=torus,
        in_specs=(queries, queries, queries, keys, keys, P(("x", "yl", "c"), ("yh", "z"))),
        out_specs=(queries, keys, keys),
        check_vma=False,
    )
```

```python
import math

import jax
import jax.numpy as jnp
from jax import lax
from jax.experimental import pallas as pl
from jax.experimental.pallas import tpu as pltpu
from jax.sharding import Mesh
from jax.sharding import PartitionSpec as P

TILE = 128
HD = 128
HQ = 4
ROWS = TILE * HQ
NQ = 16
NK = 32
NY = 8
NZ = 8
QPAD = 272
KPAD = 144
LOW = -1e30
SCALE = 1.0 / math.sqrt(HD)
LOG2E = 1.0 / math.log(2.0)
Y = ("yl", "yh")
STEP = 4


def dot(a, b, dims):
    return lax.dot_general(a, b, (dims, ((), ())), preferred_element_type=jnp.float32)


def heads(ref, r, first):
    return jnp.concatenate(
        [ref[r, first : first + TILE, h * HD : (h + 1) * HD] for h in range(HQ)], axis=0
    )


def unpack(pairs_ref, s):
    pair = pairs_ref[s]
    r, j = pair >> 6, pair & 63
    return r, j, jnp.minimum(r, NQ - 1), jnp.minimum(j, NK - 1)


def blocks_of(count_ref, per_step):
    return (count_ref[0] + (per_step - 1)) // per_step


def stats_kernel(
    pairs_ref, count_ref, q_hbm, kv_hbm, out_ref, sent_hbm, q_ref, k_ref, m_ref, l_ref, sems
):
    copies = (
        pltpu.make_async_copy(q_hbm.at[:, pl.ds(0, TILE), :], q_ref, sems.at[0]),
        pltpu.make_async_copy(kv_hbm.at[:, :, pl.ds(0, HD)], k_ref, sems.at[1]),
    )
    for copy in copies:
        copy.start()
    m_ref[...] = jnp.full(m_ref.shape, LOW, jnp.float32)
    l_ref[...] = jnp.zeros(l_ref.shape, jnp.float32)
    for copy in copies:
        copy.wait()

    def visit(i, carry):
        found = []
        for u in range(STEP):
            r, _, rq, jk = unpack(pairs_ref, i * STEP + u)
            scores = dot(k_ref[jk], heads(q_ref, rq, 0), ((1,), (1,))) * (SCALE * LOG2E)
            top = jnp.max(scores, axis=0, keepdims=True)
            found.append((r, top, jnp.sum(jnp.exp2(scores - top), axis=0, keepdims=True)))
        for r, top, total in found:
            old = m_ref[r]
            new = jnp.maximum(old, top)
            m_ref[r] = new
            l_ref[r] = l_ref[r] * jnp.exp2(old - new) + total * jnp.exp2(top - new)
        return carry

    lax.fori_loop(0, blocks_of(count_ref, STEP), visit, 0)
    total = l_ref[...][:NQ]
    out_ref[...] = jnp.where(
        total > 0.0, m_ref[...][:NQ] + jnp.log2(jnp.maximum(total, 1e-30)), LOW
    )
    copies = [pltpu.make_async_copy(out_ref, sent_hbm.at[n], sems.at[n]) for n in range(NQ)]
    for copy in copies:
        copy.start()
    for copy in copies:
        copy.wait()


def weights_of(q_ref, kv_ref, total_ref, rq, jk):
    scores = dot(kv_ref[jk, :, :HD], heads(q_ref, rq, 0), ((1,), (1,))) * (SCALE * LOG2E)
    probs = jnp.exp2(scores - total_ref[rq])
    grad_probs = dot(kv_ref[jk, :, HD:], heads(q_ref, rq, TILE), ((1,), (1,)))
    delta = q_ref[rq, 2 * TILE : 2 * TILE + 16, :].astype(jnp.float32)[0:1, :]
    return probs, (probs * (grad_probs - delta)).astype(jnp.bfloat16)


def load(q_hbm, kv_hbm, q_ref, kv_ref, sems):
    copies = (
        pltpu.make_async_copy(q_hbm, q_ref, sems.at[0]),
        pltpu.make_async_copy(kv_hbm, kv_ref, sems.at[1]),
    )
    for copy in copies:
        copy.start()
    return copies


def query_kernel(
    pairs_ref, count_ref, core_ref, q_hbm, kv_hbm, total_ref, kept_ref, sent_ref,
    q_ref, kv_ref, acc, ds_ref, sems,
):
    copies = load(q_hbm, kv_hbm, q_ref, kv_ref, sems)
    acc[...] = jnp.zeros(acc.shape, jnp.float32)
    for copy in copies:
        copy.wait()

    def visit(i, carry):
        where = [unpack(pairs_ref, i * STEP + u) for u in range(STEP)]
        for u, (_, _, rq, jk) in enumerate(where):
            ds_ref[u] = weights_of(q_ref, kv_ref, total_ref, rq, jk)[1]
        parts = [dot(kv_ref[w[3], :, :HD], ds_ref[u], ((0,), (0,))) for u, w in enumerate(where)]
        for (r, _, _, _), part in zip(where, parts):
            acc[r] += part
        return carry

    lax.fori_loop(0, blocks_of(count_ref, STEP), visit, 0)
    mine = core_ref[0] * NZ
    for n in range(NZ):
        kept_ref[n] = acc[mine + n].astype(jnp.bfloat16)
        sent_ref[n] = acc[NZ - mine + n].astype(jnp.bfloat16)


def key_kernel(
    pairs_ref, count_ref, core_ref, x_ref, q_hbm, kv_hbm, total_ref, own_ref, far_ref,
    kept_hbm, got_hbm, chip_hbm, out0, out1, out2, out3,
    q_ref, kv_ref, acc, p_ref, ds_ref, kept_ref, got_ref, chip_ref, sems,
):
    two = (
        pltpu.make_async_copy(kept_hbm, kept_ref, sems.at[2]),
        pltpu.make_async_copy(got_hbm, got_ref, sems.at[3]),
    )
    for copy in two:
        copy.start()
    copies = load(q_hbm, kv_hbm, q_ref, kv_ref, sems)
    acc[...] = jnp.zeros(acc.shape, jnp.float32)
    for copy in two:
        copy.wait()
    for n in range(NZ):
        r = core_ref[0] * NZ + n
        own = jnp.exp2(own_ref[r] - total_ref[r])
        far = jnp.exp2(far_ref[r] - total_ref[r])
        chip_ref[n] = (
            kept_ref[n].astype(jnp.float32) * own + got_ref[n].astype(jnp.float32) * far
        ).astype(jnp.bfloat16)
    leave = pltpu.make_async_copy(chip_ref, chip_hbm, sems.at[4])
    leave.start()
    for copy in copies:
        copy.wait()

    def visit(i, carry):
        where = [unpack(pairs_ref, i * STEP + u) for u in range(STEP)]
        for u, (_, _, rq, jk) in enumerate(where):
            probs, grad_scores = weights_of(q_ref, kv_ref, total_ref, rq, jk)
            p_ref[u] = probs.astype(jnp.bfloat16)
            ds_ref[u] = grad_scores
        parts = [
            (
                dot(ds_ref[u], heads(q_ref, w[2], 0), ((1,), (0,))),
                dot(p_ref[u], heads(q_ref, w[2], TILE), ((1,), (0,))),
            )
            for u, w in enumerate(where)
        ]
        for (_, j, _, _), (of_key, of_value) in zip(where, parts):
            acc[j, :, :HD] += of_key
            acc[j, :, HD:] += of_value
        return carry

    lax.fori_loop(0, blocks_of(count_ref, STEP), visit, 0)
    for n, out_ref in enumerate((out0, out1, out2, out3)):
        first = pl.multiple_of(((x_ref[0] + n) & 3) * NY, NY)
        out_ref[...] = acc[pl.ds(first, NY)].astype(jnp.bfloat16)
    leave.wait()


def prepare_kernel(q_in, g_in, o_in, k_in, v_in, mask_in, q_ref, kv_hbm, kv_ref, sems):
    kv_ref[:TILE, :HD] = k_in[...]
    kv_ref[:TILE, HD:] = v_in[...]
    kv_ref[TILE:, :] = jnp.zeros((KPAD - TILE, 2 * HD), jnp.bfloat16)
    kv_ref[TILE:, :NK] = mask_in[...].astype(jnp.float32).astype(jnp.bfloat16)
    copies = [pltpu.make_async_copy(kv_ref, kv_hbm.at[n], sems.at[n]) for n in range(NY)]
    for copy in copies:
        copy.start()
    q_ref[:TILE] = q_in[...]
    q_ref[TILE : 2 * TILE] = g_in[...]
    for h in range(HQ):
        cols = slice(h * HD, (h + 1) * HD)
        product = g_in[:, cols].astype(jnp.float32) * o_in[:, cols].astype(jnp.float32)
        delta = jnp.sum(product.T, axis=0, keepdims=True).astype(jnp.bfloat16)
        q_ref[2 * TILE :, cols] = jnp.broadcast_to(delta, (QPAD - 2 * TILE, HD))
    for copy in copies:
        copy.wait()


def finish_kernel(dq_ref, over_y_ref, query_ref, key_ref, value_ref):
    for h in range(HQ):
        cols = slice(h * TILE, (h + 1) * TILE)
        query_ref[:, cols] = (dq_ref[:, cols].astype(jnp.float32).T * SCALE).astype(jnp.bfloat16)
    sums = over_y_ref[0].astype(jnp.float32)
    for n in range(1, NY):
        sums += over_y_ref[n].astype(jnp.float32)
    key_ref[...] = (sums[:, :HD] * SCALE).astype(jnp.bfloat16)
    value_ref[...] = sums[:, HD:].astype(jnp.bfloat16)


def vmem():
    return pl.BlockSpec(memory_space=pltpu.VMEM)


def smem():
    return pl.BlockSpec(memory_space=pltpu.SMEM)


def anywhere():
    return pl.BlockSpec(memory_space=pl.ANY)


def params():
    return pltpu.CompilerParams(vmem_limit_bytes=50 * 1024 * 1024)


def cost(mib):
    return pl.CostEstimate(flops=10_000_000_000, bytes_accessed=mib << 20, transcendentals=0)


def loaded():
    return [
        pltpu.VMEM((NQ, QPAD, ROWS), jnp.bfloat16),
        pltpu.VMEM((NK, TILE, 2 * HD), jnp.bfloat16),
    ]


def call_prepare(q, g, o, k, v, mask):
    return pl.pallas_call(
        prepare_kernel,
        out_shape=(
            jax.ShapeDtypeStruct((QPAD, ROWS), jnp.bfloat16),
            jax.ShapeDtypeStruct((NY, KPAD, 2 * HD), jnp.bfloat16),
        ),
        in_specs=[vmem()] * 6,
        out_specs=(vmem(), anywhere()),
        scratch_shapes=[
            pltpu.VMEM((KPAD, 2 * HD), jnp.bfloat16),
            pltpu.SemaphoreType.DMA((NY,)),
        ],
        name="prepare",
    )(q, g, o, k, v, mask)


def call_finish(dq, over_y):
    tile = jax.ShapeDtypeStruct((TILE, HD), jnp.bfloat16)
    return pl.pallas_call(
        finish_kernel,
        out_shape=(jax.ShapeDtypeStruct((TILE, ROWS), jnp.bfloat16), tile, tile),
        in_specs=[vmem()] * 2,
        out_specs=(vmem(),) * 3,
        name="finish",
    )(dq, over_y)


def call_stats(pairs, count, q, kv):
    return pl.pallas_call(
        stats_kernel,
        out_shape=(
            jax.ShapeDtypeStruct((NQ, 1, ROWS), jnp.float32),
            jax.ShapeDtypeStruct((NQ, NQ, 1, ROWS), jnp.float32),
        ),
        in_specs=[smem()] * 2 + [anywhere()] * 2,
        out_specs=(vmem(), anywhere()),
        scratch_shapes=[
            pltpu.VMEM((NQ, TILE, ROWS), jnp.bfloat16),
            pltpu.VMEM((NK, TILE, HD), jnp.bfloat16),
            pltpu.VMEM((NQ + 1, 1, ROWS), jnp.float32),
            pltpu.VMEM((NQ + 1, 1, ROWS), jnp.float32),
            pltpu.SemaphoreType.DMA((NQ,)),
        ],
        compiler_params=params(),
        cost_estimate=cost(4),
        name="row_statistics",
    )(pairs, count, q, kv)


def call_query(pairs, count, core, q, kv, part):
    half = jax.ShapeDtypeStruct((NZ, HD, ROWS), jnp.bfloat16)
    return pl.pallas_call(
        query_kernel,
        out_shape=(half, half),
        in_specs=[smem()] * 3 + [anywhere()] * 2 + [vmem()],
        out_specs=(vmem(), vmem()),
        scratch_shapes=loaded()
        + [
            pltpu.VMEM((NQ + 1, HD, ROWS), jnp.float32),
            pltpu.VMEM((STEP, TILE, ROWS), jnp.bfloat16),
            pltpu.SemaphoreType.DMA((2,)),
        ],
        compiler_params=params(),
        cost_estimate=cost(8),
        name="query_gradient",
    )(pairs, count, core, q, kv, part)


def call_key(pairs, count, core, x, q, kv, total, own, far, kept, got):
    quarter = jax.ShapeDtypeStruct((NY, TILE, 2 * HD), jnp.bfloat16)
    half = pltpu.VMEM((NZ, HD, ROWS), jnp.bfloat16)
    return pl.pallas_call(
        key_kernel,
        out_shape=(jax.ShapeDtypeStruct((NZ, HD, ROWS), jnp.bfloat16),) + (quarter,) * 4,
        in_specs=[smem()] * 4 + [anywhere()] * 2 + [vmem()] * 3 + [anywhere()] * 2,
        out_specs=(anywhere(),) + (vmem(),) * 4,
        scratch_shapes=loaded()
        + [
            pltpu.VMEM((NK + 1, TILE, 2 * HD), jnp.float32),
            pltpu.VMEM((STEP, TILE, ROWS), jnp.bfloat16),
            pltpu.VMEM((STEP, TILE, ROWS), jnp.bfloat16),
            half,
            half,
            half,
            pltpu.SemaphoreType.DMA((5,)),
        ],
        compiler_params=params(),
        cost_estimate=cost(8),
        name="key_gradient",
    )(pairs, count, core, x, q, kv, total, own, far, kept, got)


def to_everyone(value, axis):
    peers = lax.axis_size(axis)
    return lax.all_to_all(
        jnp.broadcast_to(value[None], (peers, *value.shape)), axis, 0, 0, tiled=True
    )


def along_x(value, by):
    return lax.ppermute(value, "x", [(n, (n + by) % 4) for n in range(4)])


def swap_cores(value):
    return lax.ppermute(value, "c", [(0, 1), (1, 0)])


def list_pairs(tile_mask):
    flat = tile_mask.reshape(-1) > 0
    number = flat.shape[0]
    place = jnp.arange(number, dtype=jnp.int32)
    ones = flat.astype(jnp.int32)
    before = jnp.sum(
        jnp.where(place[None, :] < place[:, None], ones[None, :], 0), axis=1
    )
    here = (before[None, :] == place[:, None]) & flat[None, :]
    spare = jnp.where(place < jnp.sum(ones), 0, NQ * 64 + NK)
    code = place // NK * 64 + place % NK
    pairs = jnp.sum(jnp.where(here, code[None, :], 0), axis=1) + spare
    return jnp.pad(pairs, (0, STEP), constant_values=NQ * 64 + NK), jnp.sum(ones)[None]


def body(query_states, out_grad, forward_out, key_states, value_states, block_mask):
    core = lax.axis_index("c")
    y_hi = lax.axis_index("yh")
    y_lo = lax.axis_index("yl")
    q_own, kv_own = call_prepare(
        query_states, out_grad, forward_out, key_states, value_states, block_mask
    )
    q_all = lax.all_gather(q_own, ("c", "z"), axis=0, tiled=False)
    kv_y = lax.all_to_all(kv_own, Y, 0, 0, tiled=True)
    kv_all = to_everyone(kv_y[:, :TILE], "x").reshape(NK, TILE, 2 * HD)

    mine = lax.dynamic_slice_in_dim(kv_y[:, TILE:, :NK], y_lo * 2, 2, 0)
    other = swap_cores(mine)
    first = jnp.where(core == 0, mine, other)
    second = jnp.where(core == 0, other, mine)
    both = jnp.stack([first, second])
    both = lax.dynamic_slice_in_dim(both, y_hi * 8, 8, 2)
    both = both.reshape(2, 2, 8, 16, 2)
    both = jnp.where(core == 0, both[..., 0], both[..., 1])
    mask = both.transpose(0, 2, 3, 1).reshape(NQ, NK)
    pairs, count = list_pairs(mask)

    part, parts = call_stats(pairs, count, q_all, kv_all)
    parts = parts.reshape(NQ, NQ * ROWS // HD, HD)
    parts = lax.all_to_all(parts, ("c", "z"), 0, 0, tiled=True)
    kept, sent = call_query(pairs, count, core[None], q_all, kv_all, part)
    got = swap_cores(sent)

    top = jnp.max(parts, axis=0)
    total = top + jnp.log2(jnp.sum(jnp.exp2(parts - top[None]), axis=0))
    total = total.reshape(NQ, 1, ROWS)
    far = lax.dynamic_index_in_dim(parts, (1 - core) * NZ + lax.axis_index("z"), 0, False)
    far = far.reshape(NQ, 1, ROWS)
    x = lax.axis_index("x")
    chip, here, ahead, across, back = call_key(
        pairs, count, core[None], x[None], q_all, kv_all, total, part, far, kept, got
    )

    dq_own = lax.psum_scatter(chip, "z", scatter_dimension=0, tiled=True)[0]
    over_x = (here, along_x(across, 2), along_x(back, -1), along_x(ahead, 1))
    over_x = sum(p.astype(jnp.float32) for p in over_x).astype(jnp.bfloat16)
    over_y = lax.all_to_all(over_x, Y, 0, 0, tiled=True)
    return call_finish(dq_own, over_y)


def solution(mesh):
    torus = Mesh(mesh.devices.reshape(4, 4, 2, 2, 8), ("x", "yl", "c", "yh", "z"))
    queries = P(("x", "yl", "c", "yh", "z"), None)
    keys = P(("yh", "z", "x", "yl", "c"), None)
    return jax.shard_map(
        body,
        mesh=torus,
        in_specs=(queries, queries, queries, keys, keys, P(("x", "yl", "c"), ("yh", "z"))),
        out_specs=(queries, keys, keys),
        check_vma=False,
    )
```

```python
import math

import jax
import jax.numpy as jnp
from jax import lax
from jax.experimental import pallas as pl
from jax.experimental.pallas import tpu as pltpu
from jax.sharding import Mesh
from jax.sharding import PartitionSpec as P

TILE = 128
HD = 128
HQ = 4
ROWS = TILE * HQ
NQ = 16
NK = 32
NY = 8
NZ = 8
QPAD = 272
KPAD = 144
LOW = -1e30
SCALE = 1.0 / math.sqrt(HD)
LOG2E = 1.0 / math.log(2.0)
Y = ("yl", "yh")
STEP = 4


def dot(a, b, dims):
    return lax.dot_general(a, b, (dims, ((), ())), preferred_element_type=jnp.float32)


def heads(ref, r, first):
    return jnp.concatenate(
        [ref[r, first : first + TILE, h * HD : (h + 1) * HD] for h in range(HQ)], axis=0
    )


def unpack(pairs_ref, s):
    pair = pairs_ref[s]
    r, j = pair >> 6, pair & 63
    return r, j, jnp.minimum(r, NQ - 1), jnp.minimum(j, NK - 1)


def blocks_of(count_ref, per_step):
    return (count_ref[0] + (per_step - 1)) // per_step


def stats_kernel(
    pairs_ref, count_ref, q_hbm, k_hbm, out_ref, sent_hbm, q_ref, k_ref, m_ref, l_ref, sems
):
    copies = (
        pltpu.make_async_copy(q_hbm.at[:, pl.ds(0, TILE), :], q_ref, sems.at[0]),
        pltpu.make_async_copy(k_hbm, k_ref, sems.at[1]),
    )
    for copy in copies:
        copy.start()
    m_ref[...] = jnp.full(m_ref.shape, LOW, jnp.float32)
    l_ref[...] = jnp.zeros(l_ref.shape, jnp.float32)
    for copy in copies:
        copy.wait()

    def visit(i, carry):
        found = []
        for u in range(STEP):
            r, _, rq, jk = unpack(pairs_ref, i * STEP + u)
            scores = dot(k_ref[jk], heads(q_ref, rq, 0), ((1,), (1,))) * (SCALE * LOG2E)
            top = jnp.max(scores, axis=0, keepdims=True)
            found.append((r, top, jnp.sum(jnp.exp2(scores - top), axis=0, keepdims=True)))
        for r, top, total in found:
            old = m_ref[r]
            new = jnp.maximum(old, top)
            m_ref[r] = new
            l_ref[r] = l_ref[r] * jnp.exp2(old - new) + total * jnp.exp2(top - new)
        return carry

    lax.fori_loop(0, blocks_of(count_ref, STEP), visit, 0)
    total = l_ref[...][:NQ]
    out_ref[...] = jnp.where(
        total > 0.0, m_ref[...][:NQ] + jnp.log2(jnp.maximum(total, 1e-30)), LOW
    )
    copies = [pltpu.make_async_copy(out_ref, sent_hbm.at[n], sems.at[n]) for n in range(NQ)]
    for copy in copies:
        copy.start()
    for copy in copies:
        copy.wait()


def weights_of(q_ref, k_ref, v_ref, total_ref, rq, jk):
    scores = dot(k_ref[jk], heads(q_ref, rq, 0), ((1,), (1,))) * (SCALE * LOG2E)
    probs = jnp.exp2(scores - total_ref[rq])
    grad_probs = dot(v_ref[jk], heads(q_ref, rq, TILE), ((1,), (1,)))
    delta = q_ref[rq, 2 * TILE : 2 * TILE + 16, :].astype(jnp.float32)[0:1, :]
    return probs, (probs * (grad_probs - delta)).astype(jnp.bfloat16)


def of_x(x_ref, by):
    return pl.ds(pl.multiple_of(((x_ref[0] + by) & 3) * NY, NY), NY)


def load(x_ref, q_hbm, k_hbm, values, q_ref, k_ref, v_ref, sems):
    copies = [
        pltpu.make_async_copy(q_hbm, q_ref, sems.at[0]),
        pltpu.make_async_copy(k_hbm, k_ref, sems.at[1]),
    ]
    for n, piece in enumerate(values):
        copies.append(pltpu.make_async_copy(piece, v_ref.at[of_x(x_ref, n)], sems.at[2 + n]))
    for copy in copies:
        copy.start()
    return copies


def query_kernel(
    pairs_ref, count_ref, core_ref, x_ref, q_hbm, k_hbm, v0, v1, v2, v3, total_ref,
    kept_ref, sent_ref, q_ref, k_ref, v_ref, acc, ds_ref, sems,
):
    copies = load(x_ref, q_hbm, k_hbm, (v0, v1, v2, v3), q_ref, k_ref, v_ref, sems)
    acc[...] = jnp.zeros(acc.shape, jnp.float32)
    for copy in copies:
        copy.wait()

    def visit(i, carry):
        where = [unpack(pairs_ref, i * STEP + u) for u in range(STEP)]
        for u, (_, _, rq, jk) in enumerate(where):
            ds_ref[u] = weights_of(q_ref, k_ref, v_ref, total_ref, rq, jk)[1]
        parts = [dot(k_ref[w[3]], ds_ref[u], ((0,), (0,))) for u, w in enumerate(where)]
        for (r, _, _, _), part in zip(where, parts):
            acc[r] += part
        return carry

    lax.fori_loop(0, blocks_of(count_ref, STEP), visit, 0)
    mine = core_ref[0] * NZ
    for n in range(NZ):
        kept_ref[n] = acc[mine + n].astype(jnp.bfloat16)
        sent_ref[n] = acc[NZ - mine + n].astype(jnp.bfloat16)


def key_kernel(
    pairs_ref, count_ref, core_ref, x_ref, q_hbm, k_hbm, v0, v1, v2, v3, total_ref, own_ref,
    far_ref, kept_hbm, got_hbm, chip_hbm, dk0, dk1, dk2, dk3, dv0, dv1, dv2, dv3,
    q_ref, k_ref, v_ref, k_acc, v_acc, p_ref, ds_ref, kept_ref, got_ref, chip_ref, sems,
):
    two = (
        pltpu.make_async_copy(kept_hbm, kept_ref, sems.at[6]),
        pltpu.make_async_copy(got_hbm, got_ref, sems.at[7]),
    )
    for copy in two:
        copy.start()
    copies = load(x_ref, q_hbm, k_hbm, (v0, v1, v2, v3), q_ref, k_ref, v_ref, sems)
    k_acc[...] = jnp.zeros(k_acc.shape, jnp.float32)
    v_acc[...] = jnp.zeros(v_acc.shape, jnp.float32)
    for copy in two:
        copy.wait()
    for n in range(NZ):
        r = core_ref[0] * NZ + n
        own = jnp.exp2(own_ref[r] - total_ref[r])
        far = jnp.exp2(far_ref[r] - total_ref[r])
        chip_ref[n] = (
            kept_ref[n].astype(jnp.float32) * own + got_ref[n].astype(jnp.float32) * far
        ).astype(jnp.bfloat16)
    leave = pltpu.make_async_copy(chip_ref, chip_hbm, sems.at[8])
    leave.start()
    for copy in copies:
        copy.wait()

    def visit(i, carry):
        where = [unpack(pairs_ref, i * STEP + u) for u in range(STEP)]
        for u, (_, _, rq, jk) in enumerate(where):
            probs, grad_scores = weights_of(q_ref, k_ref, v_ref, total_ref, rq, jk)
            p_ref[u] = probs.astype(jnp.bfloat16)
            ds_ref[u] = grad_scores
        parts = [
            (
                dot(ds_ref[u], heads(q_ref, w[2], 0), ((1,), (0,))),
                dot(p_ref[u], heads(q_ref, w[2], TILE), ((1,), (0,))),
            )
            for u, w in enumerate(where)
        ]
        for (_, j, _, _), (of_key, of_value) in zip(where, parts):
            k_acc[j] += of_key
            v_acc[j] += of_value
        return carry

    lax.fori_loop(0, blocks_of(count_ref, STEP), visit, 0)
    for n, (dk_ref, dv_ref) in enumerate(((dk0, dv0), (dk1, dv1), (dk2, dv2), (dk3, dv3))):
        dk_ref[...] = k_acc[of_x(x_ref, n)].astype(jnp.bfloat16)
        dv_ref[...] = v_acc[of_x(x_ref, n)].astype(jnp.bfloat16)
    leave.wait()


def prepare_kernel(q_in, g_in, o_in, k_in, v_in, mask_in, q_ref, kv_hbm, kv_ref, sems):
    kv_ref[:TILE, :HD] = k_in[...]
    kv_ref[:TILE, HD:] = v_in[...]
    kv_ref[TILE:, :] = jnp.zeros((KPAD - TILE, 2 * HD), jnp.bfloat16)
    kv_ref[TILE:, :NK] = mask_in[...].astype(jnp.float32).astype(jnp.bfloat16)
    copies = [pltpu.make_async_copy(kv_ref, kv_hbm.at[n], sems.at[n]) for n in range(NY)]
    for copy in copies:
        copy.start()
    q_ref[:TILE] = q_in[...]
    q_ref[TILE : 2 * TILE] = g_in[...]
    for h in range(HQ):
        cols = slice(h * HD, (h + 1) * HD)
        product = g_in[:, cols].astype(jnp.float32) * o_in[:, cols].astype(jnp.float32)
        delta = jnp.sum(product.T, axis=0, keepdims=True).astype(jnp.bfloat16)
        q_ref[2 * TILE :, cols] = jnp.broadcast_to(delta, (QPAD - 2 * TILE, HD))
    for copy in copies:
        copy.wait()


def finish_kernel(dq_ref, dk_ref, dv_ref, query_ref, key_ref, value_ref):
    for h in range(HQ):
        cols = slice(h * TILE, (h + 1) * TILE)
        query_ref[:, cols] = (dq_ref[:, cols].astype(jnp.float32).T * SCALE).astype(jnp.bfloat16)
    for parts_ref, out_ref, scale in ((dk_ref, key_ref, SCALE), (dv_ref, value_ref, 1.0)):
        total = parts_ref[0].astype(jnp.float32)
        for n in range(1, NY):
            total += parts_ref[n].astype(jnp.float32)
        out_ref[...] = (total * scale).astype(jnp.bfloat16)


def vmem():
    return pl.BlockSpec(memory_space=pltpu.VMEM)


def smem():
    return pl.BlockSpec(memory_space=pltpu.SMEM)


def anywhere():
    return pl.BlockSpec(memory_space=pl.ANY)


def params():
    return pltpu.CompilerParams(vmem_limit_bytes=50 * 1024 * 1024)


def cost(mib):
    return pl.CostEstimate(flops=10_000_000_000, bytes_accessed=mib << 20, transcendentals=0)


def loaded():
    return [
        pltpu.VMEM((NQ, QPAD, ROWS), jnp.bfloat16),
        pltpu.VMEM((NK, TILE, HD), jnp.bfloat16),
        pltpu.VMEM((NK, TILE, HD), jnp.bfloat16),
    ]


def call_prepare(q, g, o, k, v, mask):
    return pl.pallas_call(
        prepare_kernel,
        out_shape=(
            jax.ShapeDtypeStruct((QPAD, ROWS), jnp.bfloat16),
            jax.ShapeDtypeStruct((NY, KPAD, 2 * HD), jnp.bfloat16),
        ),
        in_specs=[vmem()] * 6,
        out_specs=(vmem(), anywhere()),
        scratch_shapes=[
            pltpu.VMEM((KPAD, 2 * HD), jnp.bfloat16),
            pltpu.SemaphoreType.DMA((NY,)),
        ],
        name="prepare",
    )(q, g, o, k, v, mask)


def call_finish(dq, dk, dv):
    tile = jax.ShapeDtypeStruct((TILE, HD), jnp.bfloat16)
    return pl.pallas_call(
        finish_kernel,
        out_shape=(jax.ShapeDtypeStruct((TILE, ROWS), jnp.bfloat16), tile, tile),
        in_specs=[vmem()] * 3,
        out_specs=(vmem(),) * 3,
        name="finish",
    )(dq, dk, dv)


def call_stats(pairs, count, q, k):
    return pl.pallas_call(
        stats_kernel,
        out_shape=(
            jax.ShapeDtypeStruct((NQ, 1, ROWS), jnp.float32),
            jax.ShapeDtypeStruct((NQ, NQ, 1, ROWS), jnp.float32),
        ),
        in_specs=[smem()] * 2 + [anywhere()] * 2,
        out_specs=(vmem(), anywhere()),
        scratch_shapes=[
            pltpu.VMEM((NQ, TILE, ROWS), jnp.bfloat16),
            pltpu.VMEM((NK, TILE, HD), jnp.bfloat16),
            pltpu.VMEM((NQ + 1, 1, ROWS), jnp.float32),
            pltpu.VMEM((NQ + 1, 1, ROWS), jnp.float32),
            pltpu.SemaphoreType.DMA((NQ,)),
        ],
        compiler_params=params(),
        cost_estimate=cost(4),
        name="row_statistics",
    )(pairs, count, q, k)


def call_query(pairs, count, core, x, q, k, values, part):
    half = jax.ShapeDtypeStruct((NZ, HD, ROWS), jnp.bfloat16)
    return pl.pallas_call(
        query_kernel,
        out_shape=(half, half),
        in_specs=[smem()] * 4 + [anywhere()] * 6 + [vmem()],
        out_specs=(vmem(), vmem()),
        scratch_shapes=loaded()
        + [
            pltpu.VMEM((NQ + 1, HD, ROWS), jnp.float32),
            pltpu.VMEM((STEP, TILE, ROWS), jnp.bfloat16),
            pltpu.SemaphoreType.DMA((6,)),
        ],
        compiler_params=params(),
        cost_estimate=cost(8),
        name="query_gradient",
    )(pairs, count, core, x, q, k, *values, part)


def call_key(pairs, count, core, x, q, k, values, total, own, far, kept, got):
    quarter = jax.ShapeDtypeStruct((NY, TILE, HD), jnp.bfloat16)
    half = pltpu.VMEM((NZ, HD, ROWS), jnp.bfloat16)
    return pl.pallas_call(
        key_kernel,
        out_shape=(jax.ShapeDtypeStruct((NZ, HD, ROWS), jnp.bfloat16),) + (quarter,) * 8,
        in_specs=[smem()] * 4 + [anywhere()] * 6 + [vmem()] * 3 + [anywhere()] * 2,
        out_specs=(anywhere(),) + (vmem(),) * 8,
        scratch_shapes=loaded()
        + [
            pltpu.VMEM((NK + 1, TILE, HD), jnp.float32),
            pltpu.VMEM((NK + 1, TILE, HD), jnp.float32),
            pltpu.VMEM((STEP, TILE, ROWS), jnp.bfloat16),
            pltpu.VMEM((STEP, TILE, ROWS), jnp.bfloat16),
            half,
            half,
            half,
            pltpu.SemaphoreType.DMA((9,)),
        ],
        compiler_params=params(),
        cost_estimate=cost(8),
        name="key_gradient",
    )(pairs, count, core, x, q, k, *values, total, own, far, kept, got)


def to_everyone(value, axis):
    peers = lax.axis_size(axis)
    return lax.all_to_all(
        jnp.broadcast_to(value[None], (peers, *value.shape)), axis, 0, 0, tiled=True
    )


def along_x(value, by):
    return lax.ppermute(value, "x", [(n, (n + by) % 4) for n in range(4)])


def swap_cores(value):
    return lax.ppermute(value, "c", [(0, 1), (1, 0)])


def sum_over_keys(here, ahead, across, back):
    arrived = (here, along_x(across, 2), along_x(ahead, 1), along_x(back, -1))
    over_x = sum(p.astype(jnp.float32) for p in arrived).astype(jnp.bfloat16)
    return lax.all_to_all(over_x, Y, 0, 0, tiled=True)


def list_pairs(tile_mask):
    flat = tile_mask.reshape(-1) > 0
    number = flat.shape[0]
    place = jnp.arange(number, dtype=jnp.int32)
    ones = flat.astype(jnp.int32)
    before = jnp.sum(
        jnp.where(place[None, :] < place[:, None], ones[None, :], 0), axis=1
    )
    here = (before[None, :] == place[:, None]) & flat[None, :]
    spare = jnp.where(place < jnp.sum(ones), 0, NQ * 64 + NK)
    code = place // NK * 64 + place % NK
    pairs = jnp.sum(jnp.where(here, code[None, :], 0), axis=1) + spare
    return jnp.pad(pairs, (0, STEP), constant_values=NQ * 64 + NK), jnp.sum(ones)[None]


def body(query_states, out_grad, forward_out, key_states, value_states, block_mask):
    core, x = lax.axis_index("c"), lax.axis_index("x")
    y_hi = lax.axis_index("yh")
    y_lo = lax.axis_index("yl")
    q_own, kv_own = call_prepare(
        query_states, out_grad, forward_out, key_states, value_states, block_mask
    )
    q_all = lax.all_gather(q_own, ("c", "z"), axis=0, tiled=False)
    kv_y = lax.all_to_all(kv_own, Y, 0, 0, tiled=True)
    k_all = to_everyone(kv_y[:, :TILE, :HD], "x").reshape(NK, TILE, HD)
    mine = lax.dynamic_slice_in_dim(kv_y[:, TILE:, :NK], y_lo * 2, 2, 0)
    other = swap_cores(mine)
    v_y, other = lax.optimization_barrier((kv_y[:, :TILE, HD:], other))
    v_all = (v_y, along_x(v_y, -1), along_x(v_y, 2), along_x(v_y, 1))
    first = jnp.where(core == 0, mine, other)
    second = jnp.where(core == 0, other, mine)
    both = jnp.stack([first, second])
    both = lax.dynamic_slice_in_dim(both, y_hi * 8, 8, 2)
    both = both.reshape(2, 2, 8, 16, 2)
    both = jnp.where(core == 0, both[..., 0], both[..., 1])
    mask = both.transpose(0, 2, 3, 1).reshape(NQ, NK)
    pairs, count = list_pairs(mask)

    part, parts = call_stats(pairs, count, q_all, k_all)
    parts = parts.reshape(NQ, NQ * ROWS // HD, HD)
    parts = lax.all_to_all(parts, ("c", "z"), 0, 0, tiled=True)
    kept, sent = call_query(pairs, count, core[None], x[None], q_all, k_all, v_all, part)
    got = swap_cores(sent)

    top = jnp.max(parts, axis=0)
    total = top + jnp.log2(jnp.sum(jnp.exp2(parts - top[None]), axis=0))
    total = total.reshape(NQ, 1, ROWS)
    far = lax.dynamic_index_in_dim(parts, (1 - core) * NZ + lax.axis_index("z"), 0, False)
    far = far.reshape(NQ, 1, ROWS)
    chip, *parts = call_key(
        pairs, count, core[None], x[None], q_all, k_all, v_all, total, part, far, kept, got
    )
    dq_own = lax.psum_scatter(chip, "z", scatter_dimension=0, tiled=True)[0]
    dv_own, dk_own = sum_over_keys(*parts[4:]), sum_over_keys(*parts[:4])
    return call_finish(dq_own, dk_own, dv_own)


def solution(mesh):
    torus = Mesh(mesh.devices.reshape(4, 4, 2, 2, 8), ("x", "yl", "c", "yh", "z"))
    queries = P(("x", "yl", "c", "yh", "z"), None)
    keys = P(("yh", "z", "x", "yl", "c"), None)
    return jax.shard_map(
        body,
        mesh=torus,
        in_specs=(queries, queries, queries, keys, keys, P(("x", "yl", "c"), ("yh", "z"))),
        out_specs=(queries, keys, keys),
        check_vma=False,
    )
```

```python
import math

import jax
import jax.numpy as jnp
from jax import lax
from jax.experimental import pallas as pl
from jax.experimental.pallas import tpu as pltpu
from jax.sharding import Mesh
from jax.sharding import PartitionSpec as P

TILE = 128
HD = 128
HQ = 4
ROWS = TILE * HQ
NQ = 16
NK = 32
NY = 8
NZ = 8
QPAD = 272
KPAD = 144
LOW = -1e30
SCALE = 1.0 / math.sqrt(HD)
LOG2E = 1.0 / math.log(2.0)
Y = ("yl", "yh")
STEP = 4


def dot(a, b, dims):
    return lax.dot_general(a, b, (dims, ((), ())), preferred_element_type=jnp.float32)


def heads(ref, r, first):
    return jnp.concatenate(
        [ref[r, first : first + TILE, h * HD : (h + 1) * HD] for h in range(HQ)], axis=0
    )


def unpack(pairs_ref, s):
    pair = pairs_ref[s]
    r, j = pair >> 6, pair & 63
    return r, j, jnp.minimum(r, NQ - 1), jnp.minimum(j, NK - 1)


def blocks_of(count_ref, per_step):
    return (count_ref[0] + (per_step - 1)) // per_step


def stats_kernel(
    pairs_ref, count_ref, q_hbm, k_hbm, out_ref, sent_hbm, q_ref, k_ref, m_ref, l_ref, sems
):
    copies = (
        pltpu.make_async_copy(q_hbm.at[:, pl.ds(0, TILE), :], q_ref, sems.at[0]),
        pltpu.make_async_copy(k_hbm, k_ref, sems.at[1]),
    )
    for copy in copies:
        copy.start()
    m_ref[...] = jnp.full(m_ref.shape, LOW, jnp.float32)
    l_ref[...] = jnp.zeros(l_ref.shape, jnp.float32)
    for copy in copies:
        copy.wait()

    def visit(i, carry):
        found = []
        for u in range(STEP):
            r, _, rq, jk = unpack(pairs_ref, i * STEP + u)
            scores = dot(k_ref[jk], heads(q_ref, rq, 0), ((1,), (1,))) * (SCALE * LOG2E)
            top = jnp.max(scores, axis=0, keepdims=True)
            found.append((r, top, jnp.sum(jnp.exp2(scores - top), axis=0, keepdims=True)))
        for r, top, total in found:
            old = m_ref[r]
            new = jnp.maximum(old, top)
            m_ref[r] = new
            l_ref[r] = l_ref[r] * jnp.exp2(old - new) + total * jnp.exp2(top - new)
        return carry

    lax.fori_loop(0, blocks_of(count_ref, STEP), visit, 0)
    total = l_ref[...][:NQ]
    out_ref[...] = jnp.where(
        total > 0.0, m_ref[...][:NQ] + jnp.log2(jnp.maximum(total, 1e-30)), LOW
    )
    copies = [pltpu.make_async_copy(out_ref, sent_hbm.at[n], sems.at[n]) for n in range(NQ)]
    for copy in copies:
        copy.start()
    for copy in copies:
        copy.wait()


def weights_of(q_ref, k_ref, v_ref, total_ref, rq, jk):
    scores = dot(k_ref[jk], heads(q_ref, rq, 0), ((1,), (1,))) * (SCALE * LOG2E)
    probs = jnp.exp2(scores - total_ref[rq])
    grad_probs = dot(v_ref[jk], heads(q_ref, rq, TILE), ((1,), (1,)))
    delta = q_ref[rq, 2 * TILE : 2 * TILE + 16, :].astype(jnp.float32)[0:1, :]
    return probs, (probs * (grad_probs - delta)).astype(jnp.bfloat16)


def of_x(x_ref, by):
    return pl.ds(pl.multiple_of(((x_ref[0] + by) & 3) * NY, NY), NY)


def load(x_ref, q_hbm, k_hbm, values, q_ref, k_ref, v_ref, sems):
    copies = [
        pltpu.make_async_copy(q_hbm, q_ref, sems.at[0]),
        pltpu.make_async_copy(k_hbm, k_ref, sems.at[1]),
    ]
    for n, piece in enumerate(values):
        copies.append(pltpu.make_async_copy(piece, v_ref.at[of_x(x_ref, n)], sems.at[2 + n]))
    for copy in copies:
        copy.start()
    return copies


def query_kernel(
    pairs_ref, count_ref, core_ref, x_ref, q_hbm, k_hbm, v0, v1, v2, v3, total_ref,
    kept_ref, sent_ref, q_ref, k_ref, v_ref, acc, ds_ref, sems,
):
    copies = load(x_ref, q_hbm, k_hbm, (v0, v1, v2, v3), q_ref, k_ref, v_ref, sems)
    acc[...] = jnp.zeros(acc.shape, jnp.float32)
    for copy in copies:
        copy.wait()

    def visit(i, carry):
        where = [unpack(pairs_ref, i * STEP + u) for u in range(STEP)]
        for u, (_, _, rq, jk) in enumerate(where):
            ds_ref[u] = weights_of(q_ref, k_ref, v_ref, total_ref, rq, jk)[1]
        parts = [dot(k_ref[w[3]], ds_ref[u], ((0,), (0,))) for u, w in enumerate(where)]
        for (r, _, _, _), part in zip(where, parts):
            acc[r] += part
        return carry

    lax.fori_loop(0, blocks_of(count_ref, STEP), visit, 0)
    mine = core_ref[0] * NZ
    for n in range(NZ):
        kept_ref[n] = acc[mine + n].astype(jnp.bfloat16)
        sent_ref[n] = acc[NZ - mine + n].astype(jnp.bfloat16)


def key_kernel(
    pairs_ref, count_ref, core_ref, x_ref, q_hbm, k_hbm, v0, v1, v2, v3, total_ref, own_ref,
    far_ref, kept_hbm, got_hbm, chip_hbm, out0, out1, out2, out3,
    q_ref, k_ref, v_ref, k_acc, v_acc, p_ref, ds_ref, kept_ref, got_ref, chip_ref, sems,
):
    two = (
        pltpu.make_async_copy(kept_hbm, kept_ref, sems.at[6]),
        pltpu.make_async_copy(got_hbm, got_ref, sems.at[7]),
    )
    for copy in two:
        copy.start()
    copies = load(x_ref, q_hbm, k_hbm, (v0, v1, v2, v3), q_ref, k_ref, v_ref, sems)
    k_acc[...] = jnp.zeros(k_acc.shape, jnp.float32)
    v_acc[...] = jnp.zeros(v_acc.shape, jnp.float32)
    for copy in two:
        copy.wait()
    for n in range(NZ):
        r = core_ref[0] * NZ + n
        own = jnp.exp2(own_ref[r] - total_ref[r])
        far = jnp.exp2(far_ref[r] - total_ref[r])
        chip_ref[n] = (
            kept_ref[n].astype(jnp.float32) * own + got_ref[n].astype(jnp.float32) * far
        ).astype(jnp.bfloat16)
    leave = pltpu.make_async_copy(chip_ref, chip_hbm, sems.at[8])
    leave.start()
    for copy in copies:
        copy.wait()

    def visit(i, carry):
        where = [unpack(pairs_ref, i * STEP + u) for u in range(STEP)]
        for u, (_, _, rq, jk) in enumerate(where):
            probs, grad_scores = weights_of(q_ref, k_ref, v_ref, total_ref, rq, jk)
            p_ref[u] = probs.astype(jnp.bfloat16)
            ds_ref[u] = grad_scores
        parts = [
            (
                dot(ds_ref[u], heads(q_ref, w[2], 0), ((1,), (0,))),
                dot(p_ref[u], heads(q_ref, w[2], TILE), ((1,), (0,))),
            )
            for u, w in enumerate(where)
        ]
        for (_, j, _, _), (of_key, of_value) in zip(where, parts):
            k_acc[j] += of_key
            v_acc[j] += of_value
        return carry

    lax.fori_loop(0, blocks_of(count_ref, STEP), visit, 0)
    for n, out_ref in enumerate((out0, out1, out2, out3)):
        out_ref[:, :, :HD] = k_acc[of_x(x_ref, n)].astype(jnp.bfloat16)
        out_ref[:, :, HD:] = v_acc[of_x(x_ref, n)].astype(jnp.bfloat16)
    leave.wait()


def prepare_kernel(q_in, g_in, o_in, k_in, v_in, mask_in, q_ref, kv_hbm, kv_ref, sems):
    kv_ref[:TILE, :HD] = k_in[...]
    kv_ref[:TILE, HD:] = v_in[...]
    kv_ref[TILE:, :] = jnp.zeros((KPAD - TILE, 2 * HD), jnp.bfloat16)
    kv_ref[TILE:, :NK] = mask_in[...].astype(jnp.float32).astype(jnp.bfloat16)
    copies = [pltpu.make_async_copy(kv_ref, kv_hbm.at[n], sems.at[n]) for n in range(NY)]
    for copy in copies:
        copy.start()
    q_ref[:TILE] = q_in[...]
    q_ref[TILE : 2 * TILE] = g_in[...]
    for h in range(HQ):
        cols = slice(h * HD, (h + 1) * HD)
        product = g_in[:, cols].astype(jnp.float32) * o_in[:, cols].astype(jnp.float32)
        delta = jnp.sum(product.T, axis=0, keepdims=True).astype(jnp.bfloat16)
        q_ref[2 * TILE :, cols] = jnp.broadcast_to(delta, (QPAD - 2 * TILE, HD))
    for copy in copies:
        copy.wait()


def finish_queries_kernel(dq_ref, query_ref):
    for h in range(HQ):
        cols = slice(h * TILE, (h + 1) * TILE)
        query_ref[:, cols] = (dq_ref[:, cols].astype(jnp.float32).T * SCALE).astype(jnp.bfloat16)


def finish_keys_kernel(over_y_ref, key_ref, value_ref):
    sums = over_y_ref[0].astype(jnp.float32)
    for n in range(1, NY):
        sums += over_y_ref[n].astype(jnp.float32)
    key_ref[...] = (sums[:, :HD] * SCALE).astype(jnp.bfloat16)
    value_ref[...] = sums[:, HD:].astype(jnp.bfloat16)


def vmem():
    return pl.BlockSpec(memory_space=pltpu.VMEM)


def smem():
    return pl.BlockSpec(memory_space=pltpu.SMEM)


def anywhere():
    return pl.BlockSpec(memory_space=pl.ANY)


def params():
    return pltpu.CompilerParams(vmem_limit_bytes=50 * 1024 * 1024)


def cost(mib):
    return pl.CostEstimate(flops=10_000_000_000, bytes_accessed=mib << 20, transcendentals=0)


def loaded():
    return [
        pltpu.VMEM((NQ, QPAD, ROWS), jnp.bfloat16),
        pltpu.VMEM((NK, TILE, HD), jnp.bfloat16),
        pltpu.VMEM((NK, TILE, HD), jnp.bfloat16),
    ]


def call_prepare(q, g, o, k, v, mask):
    return pl.pallas_call(
        prepare_kernel,
        out_shape=(
            jax.ShapeDtypeStruct((QPAD, ROWS), jnp.bfloat16),
            jax.ShapeDtypeStruct((NY, KPAD, 2 * HD), jnp.bfloat16),
        ),
        in_specs=[vmem()] * 6,
        out_specs=(vmem(), anywhere()),
        scratch_shapes=[
            pltpu.VMEM((KPAD, 2 * HD), jnp.bfloat16),
            pltpu.SemaphoreType.DMA((NY,)),
        ],
        name="prepare",
    )(q, g, o, k, v, mask)


def call_finish_queries(dq):
    return pl.pallas_call(
        finish_queries_kernel,
        out_shape=jax.ShapeDtypeStruct((TILE, ROWS), jnp.bfloat16),
        in_specs=[vmem()],
        out_specs=vmem(),
        name="finish_queries",
    )(dq)


def call_finish_keys(over_y):
    tile = jax.ShapeDtypeStruct((TILE, HD), jnp.bfloat16)
    return pl.pallas_call(
        finish_keys_kernel,
        out_shape=(tile, tile),
        in_specs=[vmem()],
        out_specs=(vmem(),) * 2,
        name="finish_keys",
    )(over_y)


def call_stats(pairs, count, q, k):
    return pl.pallas_call(
        stats_kernel,
        out_shape=(
            jax.ShapeDtypeStruct((NQ, 1, ROWS), jnp.float32),
            jax.ShapeDtypeStruct((NQ, NQ, 1, ROWS), jnp.float32),
        ),
        in_specs=[smem()] * 2 + [anywhere()] * 2,
        out_specs=(vmem(), anywhere()),
        scratch_shapes=[
            pltpu.VMEM((NQ, TILE, ROWS), jnp.bfloat16),
            pltpu.VMEM((NK, TILE, HD), jnp.bfloat16),
            pltpu.VMEM((NQ + 1, 1, ROWS), jnp.float32),
            pltpu.VMEM((NQ + 1, 1, ROWS), jnp.float32),
            pltpu.SemaphoreType.DMA((NQ,)),
        ],
        compiler_params=params(),
        cost_estimate=cost(4),
        name="row_statistics",
    )(pairs, count, q, k)


def call_query(pairs, count, core, x, q, k, values, part):
    half = jax.ShapeDtypeStruct((NZ, HD, ROWS), jnp.bfloat16)
    return pl.pallas_call(
        query_kernel,
        out_shape=(half, half),
        in_specs=[smem()] * 4 + [anywhere()] * 6 + [vmem()],
        out_specs=(vmem(), vmem()),
        scratch_shapes=loaded()
        + [
            pltpu.VMEM((NQ + 1, HD, ROWS), jnp.float32),
            pltpu.VMEM((STEP, TILE, ROWS), jnp.bfloat16),
            pltpu.SemaphoreType.DMA((6,)),
        ],
        compiler_params=params(),
        cost_estimate=cost(8),
        name="query_gradient",
    )(pairs, count, core, x, q, k, *values, part)


def call_key(pairs, count, core, x, q, k, values, total, own, far, kept, got):
    quarter = jax.ShapeDtypeStruct((NY, TILE, 2 * HD), jnp.bfloat16)
    half = pltpu.VMEM((NZ, HD, ROWS), jnp.bfloat16)
    return pl.pallas_call(
        key_kernel,
        out_shape=(jax.ShapeDtypeStruct((NZ, HD, ROWS), jnp.bfloat16),) + (quarter,) * 4,
        in_specs=[smem()] * 4 + [anywhere()] * 6 + [vmem()] * 3 + [anywhere()] * 2,
        out_specs=(anywhere(),) + (vmem(),) * 4,
        scratch_shapes=loaded()
        + [
            pltpu.VMEM((NK + 1, TILE, HD), jnp.float32),
            pltpu.VMEM((NK + 1, TILE, HD), jnp.float32),
            pltpu.VMEM((STEP, TILE, ROWS), jnp.bfloat16),
            pltpu.VMEM((STEP, TILE, ROWS), jnp.bfloat16),
            half,
            half,
            half,
            pltpu.SemaphoreType.DMA((9,)),
        ],
        compiler_params=params(),
        cost_estimate=cost(8),
        name="key_gradient",
    )(pairs, count, core, x, q, k, *values, total, own, far, kept, got)


def to_everyone(value, axis):
    peers = lax.axis_size(axis)
    return lax.all_to_all(
        jnp.broadcast_to(value[None], (peers, *value.shape)), axis, 0, 0, tiled=True
    )


def along_x(value, by):
    return lax.ppermute(value, "x", [(n, (n + by) % 4) for n in range(4)])


def swap_cores(value):
    return lax.ppermute(value, "c", [(0, 1), (1, 0)])


def sum_over_keys(here, ahead, across, back):
    arrived = (here, along_x(across, 2), along_x(ahead, 1), along_x(back, -1))
    over_x = sum(p.astype(jnp.float32) for p in arrived).astype(jnp.bfloat16)
    return lax.all_to_all(over_x, Y, 0, 0, tiled=True)


def list_pairs(tile_mask):
    flat = tile_mask.reshape(-1) > 0
    number = flat.shape[0]
    place = jnp.arange(number, dtype=jnp.int32)
    ones = flat.astype(jnp.int32)
    before = jnp.sum(
        jnp.where(place[None, :] < place[:, None], ones[None, :], 0), axis=1
    )
    here = (before[None, :] == place[:, None]) & flat[None, :]
    spare = jnp.where(place < jnp.sum(ones), 0, NQ * 64 + NK)
    code = place // NK * 64 + place % NK
    pairs = jnp.sum(jnp.where(here, code[None, :], 0), axis=1) + spare
    return jnp.pad(pairs, (0, STEP), constant_values=NQ * 64 + NK), jnp.sum(ones)[None]


def body(query_states, out_grad, forward_out, key_states, value_states, block_mask):
    core, x = lax.axis_index("c"), lax.axis_index("x")
    y_hi = lax.axis_index("yh")
    y_lo = lax.axis_index("yl")
    q_own, kv_own = call_prepare(
        query_states, out_grad, forward_out, key_states, value_states, block_mask
    )
    q_all = lax.all_gather(q_own, ("c", "z"), axis=0, tiled=False)
    kv_y = lax.all_to_all(kv_own, Y, 0, 0, tiled=True)
    k_all = to_everyone(kv_y[:, :TILE, :HD], "x").reshape(NK, TILE, HD)
    mine = lax.dynamic_slice_in_dim(kv_y[:, TILE:, :NK], y_lo * 2, 2, 0)
    other = swap_cores(mine)
    v_y, other = lax.optimization_barrier((kv_y[:, :TILE, HD:], other))
    v_all = (v_y, along_x(v_y, -1), along_x(v_y, 2), along_x(v_y, 1))
    first = jnp.where(core == 0, mine, other)
    second = jnp.where(core == 0, other, mine)
    both = jnp.stack([first, second])
    both = lax.dynamic_slice_in_dim(both, y_hi * 8, 8, 2)
    both = both.reshape(2, 2, 8, 16, 2)
    both = jnp.where(core == 0, both[..., 0], both[..., 1])
    mask = both.transpose(0, 2, 3, 1).reshape(NQ, NK)
    pairs, count = list_pairs(mask)

    part, parts = call_stats(pairs, count, q_all, k_all)
    parts = parts.reshape(NQ, NQ * ROWS // HD, HD)
    parts = lax.all_to_all(parts, ("c", "z"), 0, 0, tiled=True)
    kept, sent = call_query(pairs, count, core[None], x[None], q_all, k_all, v_all, part)
    got = swap_cores(sent)

    top = jnp.max(parts, axis=0)
    total = top + jnp.log2(jnp.sum(jnp.exp2(parts - top[None]), axis=0))
    total = total.reshape(NQ, 1, ROWS)
    far = lax.dynamic_index_in_dim(parts, (1 - core) * NZ + lax.axis_index("z"), 0, False)
    far = far.reshape(NQ, 1, ROWS)
    chip, *parts = call_key(
        pairs, count, core[None], x[None], q_all, k_all, v_all, total, part, far, kept, got
    )
    dq_own = lax.psum_scatter(chip, "z", scatter_dimension=0, tiled=True)[0]
    query_grad, over_y = lax.optimization_barrier(
        (call_finish_queries(dq_own), sum_over_keys(*parts))
    )
    return query_grad, *call_finish_keys(over_y)


def solution(mesh):
    torus = Mesh(mesh.devices.reshape(4, 4, 2, 2, 8), ("x", "yl", "c", "yh", "z"))
    queries = P(("x", "yl", "c", "yh", "z"), None)
    keys = P(("yh", "z", "x", "yl", "c"), None)
    return jax.shard_map(
        body,
        mesh=torus,
        in_specs=(queries, queries, queries, keys, keys, P(("x", "yl", "c"), ("yh", "z"))),
        out_specs=(queries, keys, keys),
        check_vma=False,
    )
```

```python
import math

import jax
import jax.numpy as jnp
from jax import lax
from jax.experimental import pallas as pl
from jax.experimental.pallas import tpu as pltpu
from jax.sharding import Mesh
from jax.sharding import PartitionSpec as P

TILE = 128
HD = 128
HQ = 4
ROWS = TILE * HQ
NQ = 16
NK = 32
NY = 8
NZ = 8
QPAD = 272
KPAD = 144
LOW = -1e30
SCALE = 1.0 / math.sqrt(HD)
LOG2E = 1.0 / math.log(2.0)
Y = ("yl", "yh")
STEP = 4


def dot(a, b, dims):
    return lax.dot_general(a, b, (dims, ((), ())), preferred_element_type=jnp.float32)


def heads(ref, r, first):
    return jnp.concatenate(
        [ref[r, first : first + TILE, h * HD : (h + 1) * HD] for h in range(HQ)], axis=0
    )


def unpack(pairs_ref, s):
    pair = pairs_ref[s]
    r, j = pair >> 6, pair & 63
    return r, j, jnp.minimum(r, NQ - 1), jnp.minimum(j, NK - 1)


def blocks_of(count_ref, per_step):
    return (count_ref[0] + (per_step - 1)) // per_step


def stats_kernel(
    pairs_ref, count_ref, q_hbm, k_hbm, out_ref, sent_hbm, q_ref, k_ref, m_ref, l_ref, sent_ref, sems
):
    copies = (
        pltpu.make_async_copy(q_hbm.at[:, pl.ds(0, TILE), :], q_ref, sems.at[0]),
        pltpu.make_async_copy(k_hbm, k_ref, sems.at[1]),
    )
    for copy in copies:
        copy.start()
    m_ref[...] = jnp.full(m_ref.shape, LOW, jnp.float32)
    l_ref[...] = jnp.zeros(l_ref.shape, jnp.float32)
    for copy in copies:
        copy.wait()

    def visit(i, carry):
        found = []
        for u in range(STEP):
            r, _, rq, jk = unpack(pairs_ref, i * STEP + u)
            scores = dot(k_ref[jk], heads(q_ref, rq, 0), ((1,), (1,))) * (SCALE * LOG2E)
            top = jnp.max(scores, axis=0, keepdims=True)
            found.append((r, top, jnp.sum(jnp.exp2(scores - top), axis=0, keepdims=True)))
        for r, top, total in found:
            old = m_ref[r]
            new = jnp.maximum(old, top)
            m_ref[r] = new
            l_ref[r] = l_ref[r] * jnp.exp2(old - new) + total * jnp.exp2(top - new)
        return carry

    lax.fori_loop(0, blocks_of(count_ref, STEP), visit, 0)
    total = l_ref[...][:NQ]
    out_ref[...] = jnp.where(
        total > 0.0, m_ref[...][:NQ] + jnp.log2(jnp.maximum(total, 1e-30)), LOW
    )
    for n in range(NQ * HQ):
        sent_ref[n : n + 1] = out_ref[n // HQ, :, n % HQ * TILE : (n % HQ + 1) * TILE]
    copies = [pltpu.make_async_copy(sent_ref, sent_hbm.at[n], sems.at[n]) for n in range(NQ)]
    for copy in copies:
        copy.start()
    for copy in copies:
        copy.wait()


def weights_of(q_ref, k_ref, v_ref, total_ref, rq, jk):
    scores = dot(k_ref[jk], heads(q_ref, rq, 0), ((1,), (1,))) * (SCALE * LOG2E)
    probs = jnp.exp2(scores - total_ref[rq])
    grad_probs = dot(v_ref[jk], heads(q_ref, rq, TILE), ((1,), (1,)))
    delta = q_ref[rq, 2 * TILE : 2 * TILE + 16, :].astype(jnp.float32)[0:1, :]
    return probs, (probs * (grad_probs - delta)).astype(jnp.bfloat16)


def of_x(x_ref, by):
    return pl.ds(pl.multiple_of(((x_ref[0] + by) & 3) * NY, NY), NY)


def load(x_ref, q_hbm, k_hbm, values, q_ref, k_ref, v_ref, sems):
    copies = [
        pltpu.make_async_copy(q_hbm, q_ref, sems.at[0]),
        pltpu.make_async_copy(k_hbm, k_ref, sems.at[1]),
    ]
    for n, piece in enumerate(values):
        copies.append(pltpu.make_async_copy(piece, v_ref.at[of_x(x_ref, n)], sems.at[2 + n]))
    for copy in copies:
        copy.start()
    return copies


def query_kernel(
    pairs_ref, count_ref, core_ref, x_ref, q_hbm, k_hbm, v0, v1, v2, v3, total_ref,
    kept_ref, sent_ref, q_ref, k_ref, v_ref, acc, ds_ref, sems,
):
    copies = load(x_ref, q_hbm, k_hbm, (v0, v1, v2, v3), q_ref, k_ref, v_ref, sems)
    acc[...] = jnp.zeros(acc.shape, jnp.float32)
    for copy in copies:
        copy.wait()

    def visit(i, carry):
        where = [unpack(pairs_ref, i * STEP + u) for u in range(STEP)]
        for u, (_, _, rq, jk) in enumerate(where):
            ds_ref[u] = weights_of(q_ref, k_ref, v_ref, total_ref, rq, jk)[1]
        parts = [dot(k_ref[w[3]], ds_ref[u], ((0,), (0,))) for u, w in enumerate(where)]
        for (r, _, _, _), part in zip(where, parts):
            acc[r] += part
        return carry

    lax.fori_loop(0, blocks_of(count_ref, STEP), visit, 0)
    mine = core_ref[0] * NZ
    for n in range(NZ):
        kept_ref[n] = acc[mine + n].astype(jnp.bfloat16)
        sent_ref[n] = acc[NZ - mine + n].astype(jnp.bfloat16)


def key_kernel(
    pairs_ref, count_ref, core_ref, x_ref, z_ref, q_hbm, k_hbm, v0, v1, v2, v3, parts_ref,
    kept_hbm, got_hbm, chip_hbm, out0, out1, out2, out3, q_ref, k_ref, v_ref, k_acc, v_acc,
    p_ref, ds_ref, kept_ref, got_ref, chip_ref, total_ref, own_ref, far_ref, sems,
):
    two = (
        pltpu.make_async_copy(kept_hbm, kept_ref, sems.at[6]),
        pltpu.make_async_copy(got_hbm, got_ref, sems.at[7]),
    )
    for copy in two:
        copy.start()
    copies = load(x_ref, q_hbm, k_hbm, (v0, v1, v2, v3), q_ref, k_ref, v_ref, sems)
    k_acc[...] = jnp.zeros(k_acc.shape, jnp.float32)
    v_acc[...] = jnp.zeros(v_acc.shape, jnp.float32)
    top = parts_ref[0]
    for n in range(1, NQ):
        top = jnp.maximum(top, parts_ref[n])
    summed = jnp.exp2(parts_ref[0] - top)
    for n in range(1, NQ):
        summed += jnp.exp2(parts_ref[n] - top)
    total = top + jnp.log2(summed)
    for n in range(NQ * HQ):
        total_ref[n // HQ, :, n % HQ * TILE : (n % HQ + 1) * TILE] = total[n : n + 1]
    own_ref[...] = jnp.exp2(parts_ref[core_ref[0] * NZ + z_ref[0]] - total)
    far_ref[...] = jnp.exp2(parts_ref[(1 - core_ref[0]) * NZ + z_ref[0]] - total)
    for copy in two:
        copy.wait()
    for n in range(NZ):
        for h in range(HQ):
            row = pl.ds((core_ref[0] * NZ + n) * HQ + h, 1)
            cols = slice(h * TILE, (h + 1) * TILE)
            chip_ref[n, :, cols] = (
                kept_ref[n, :, cols].astype(jnp.float32) * own_ref[row]
                + got_ref[n, :, cols].astype(jnp.float32) * far_ref[row]
            ).astype(jnp.bfloat16)
    leave = pltpu.make_async_copy(chip_ref, chip_hbm, sems.at[8])
    leave.start()
    for copy in copies:
        copy.wait()

    def visit(i, carry):
        where = [unpack(pairs_ref, i * STEP + u) for u in range(STEP)]
        for u, (_, _, rq, jk) in enumerate(where):
            probs, grad_scores = weights_of(q_ref, k_ref, v_ref, total_ref, rq, jk)
            p_ref[u] = probs.astype(jnp.bfloat16)
            ds_ref[u] = grad_scores
        parts = [
            (
                dot(ds_ref[u], heads(q_ref, w[2], 0), ((1,), (0,))),
                dot(p_ref[u], heads(q_ref, w[2], TILE), ((1,), (0,))),
            )
            for u, w in enumerate(where)
        ]
        for (_, j, _, _), (of_key, of_value) in zip(where, parts):
            k_acc[j] += of_key
            v_acc[j] += of_value
        return carry

    lax.fori_loop(0, blocks_of(count_ref, STEP), visit, 0)
    for n, out_ref in enumerate((out0, out1, out2, out3)):
        out_ref[:, :, :HD] = k_acc[of_x(x_ref, n)].astype(jnp.bfloat16)
        out_ref[:, :, HD:] = v_acc[of_x(x_ref, n)].astype(jnp.bfloat16)
    leave.wait()


def prepare_kernel(
    q_in, g_in, o_in, k_in, v_in, mask_in, q_hbm, kv_hbm, kv_ref, delta_ref, sems
):
    rows = (pl.ds(0, TILE), pl.ds(TILE, TILE), pl.ds(2 * TILE, QPAD - 2 * TILE))
    copies = [
        pltpu.make_async_copy(source, q_hbm.at[row], sems.at[NY + n])
        for n, (source, row) in enumerate(zip((q_in, g_in, delta_ref), rows))
    ]
    copies[0].start()
    copies[1].start()
    kv_ref[:TILE, :HD] = k_in[...]
    kv_ref[:TILE, HD:] = v_in[...]
    kv_ref[TILE:, :] = jnp.zeros((KPAD - TILE, 2 * HD), jnp.bfloat16)
    kv_ref[TILE:, :NK] = mask_in[...].astype(jnp.float32).astype(jnp.bfloat16)
    for n in range(NY):
        copies.append(pltpu.make_async_copy(kv_ref, kv_hbm.at[n], sems.at[n]))
        copies[-1].start()
    for h in range(HQ):
        cols = slice(h * HD, (h + 1) * HD)
        product = g_in[:, cols].astype(jnp.float32) * o_in[:, cols].astype(jnp.float32)
        delta = jnp.sum(product.T, axis=0, keepdims=True).astype(jnp.bfloat16)
        delta_ref[:, cols] = jnp.broadcast_to(delta, (QPAD - 2 * TILE, HD))
    copies[2].start()
    for copy in copies:
        copy.wait()


def finish_queries_kernel(dq_ref, query_ref):
    for h in range(HQ):
        cols = slice(h * TILE, (h + 1) * TILE)
        query_ref[:, cols] = (dq_ref[:, cols].astype(jnp.float32).T * SCALE).astype(jnp.bfloat16)


def finish_keys_kernel(over_y_ref, key_ref, value_ref):
    sums = over_y_ref[0].astype(jnp.float32)
    for n in range(1, NY):
        sums += over_y_ref[n].astype(jnp.float32)
    key_ref[...] = (sums[:, :HD] * SCALE).astype(jnp.bfloat16)
    value_ref[...] = sums[:, HD:].astype(jnp.bfloat16)


def vmem():
    return pl.BlockSpec(memory_space=pltpu.VMEM)


def smem():
    return pl.BlockSpec(memory_space=pltpu.SMEM)


def anywhere():
    return pl.BlockSpec(memory_space=pl.ANY)


def params(mib=50):
    return pltpu.CompilerParams(vmem_limit_bytes=mib * 1024 * 1024)


def cost(mib):
    return pl.CostEstimate(flops=10_000_000_000, bytes_accessed=mib << 20, transcendentals=0)


def loaded():
    return [
        pltpu.VMEM((NQ, QPAD, ROWS), jnp.bfloat16),
        pltpu.VMEM((NK, TILE, HD), jnp.bfloat16),
        pltpu.VMEM((NK, TILE, HD), jnp.bfloat16),
    ]


def call_prepare(q, g, o, k, v, mask):
    return pl.pallas_call(
        prepare_kernel,
        out_shape=(
            jax.ShapeDtypeStruct((QPAD, ROWS), jnp.bfloat16),
            jax.ShapeDtypeStruct((NY, KPAD, 2 * HD), jnp.bfloat16),
        ),
        in_specs=[vmem()] * 6,
        out_specs=(anywhere(), anywhere()),
        scratch_shapes=[
            pltpu.VMEM((KPAD, 2 * HD), jnp.bfloat16),
            pltpu.VMEM((QPAD - 2 * TILE, ROWS), jnp.bfloat16),
            pltpu.SemaphoreType.DMA((NY + 3,)),
        ],
        compiler_params=params(8),
        name="prepare",
    )(q, g, o, k, v, mask)


def call_finish_queries(dq):
    return pl.pallas_call(
        finish_queries_kernel,
        out_shape=jax.ShapeDtypeStruct((TILE, ROWS), jnp.bfloat16),
        in_specs=[vmem()],
        out_specs=vmem(),
        compiler_params=params(8),
        name="finish_queries",
    )(dq)


def call_finish_keys(over_y):
    tile = jax.ShapeDtypeStruct((TILE, HD), jnp.bfloat16)
    return pl.pallas_call(
        finish_keys_kernel,
        out_shape=(tile, tile),
        in_specs=[vmem()],
        out_specs=(vmem(),) * 2,
        compiler_params=params(8),
        name="finish_keys",
    )(over_y)


def call_stats(pairs, count, q, k):
    return pl.pallas_call(
        stats_kernel,
        out_shape=(
            jax.ShapeDtypeStruct((NQ, 1, ROWS), jnp.float32),
            jax.ShapeDtypeStruct((NQ, NQ * HQ, TILE), jnp.float32),
        ),
        in_specs=[smem()] * 2 + [anywhere()] * 2,
        out_specs=(vmem(), anywhere()),
        scratch_shapes=[
            pltpu.VMEM((NQ, TILE, ROWS), jnp.bfloat16),
            pltpu.VMEM((NK, TILE, HD), jnp.bfloat16),
            pltpu.VMEM((NQ + 1, 1, ROWS), jnp.float32),
            pltpu.VMEM((NQ + 1, 1, ROWS), jnp.float32),
            pltpu.VMEM((NQ * HQ, TILE), jnp.float32),
            pltpu.SemaphoreType.DMA((NQ,)),
        ],
        compiler_params=params(),
        cost_estimate=cost(4),
        name="row_statistics",
    )(pairs, count, q, k)


def call_query(pairs, count, core, x, q, k, values, part):
    half = jax.ShapeDtypeStruct((NZ, HD, ROWS), jnp.bfloat16)
    return pl.pallas_call(
        query_kernel,
        out_shape=(half, half),
        in_specs=[smem()] * 4 + [anywhere()] * 6 + [vmem()],
        out_specs=(vmem(), vmem()),
        scratch_shapes=loaded()
        + [
            pltpu.VMEM((NQ + 1, HD, ROWS), jnp.float32),
            pltpu.VMEM((STEP, TILE, ROWS), jnp.bfloat16),
            pltpu.SemaphoreType.DMA((6,)),
        ],
        compiler_params=params(),
        cost_estimate=cost(8),
        name="query_gradient",
    )(pairs, count, core, x, q, k, *values, part)


def call_key(pairs, count, core, x, z, q, k, values, parts, kept, got):
    quarter = jax.ShapeDtypeStruct((NY, TILE, 2 * HD), jnp.bfloat16)
    half = pltpu.VMEM((NZ, HD, ROWS), jnp.bfloat16)
    return pl.pallas_call(
        key_kernel,
        out_shape=(jax.ShapeDtypeStruct((NZ, HD, ROWS), jnp.bfloat16),) + (quarter,) * 4,
        in_specs=[smem()] * 5 + [anywhere()] * 6 + [vmem()] + [anywhere()] * 2,
        out_specs=(anywhere(),) + (vmem(),) * 4,
        scratch_shapes=loaded()
        + [
            pltpu.VMEM((NK + 1, TILE, HD), jnp.float32),
            pltpu.VMEM((NK + 1, TILE, HD), jnp.float32),
            pltpu.VMEM((STEP, TILE, ROWS), jnp.bfloat16),
            pltpu.VMEM((STEP, TILE, ROWS), jnp.bfloat16),
            half,
            half,
            half,
            pltpu.VMEM((NQ, 1, ROWS), jnp.float32),
            pltpu.VMEM((NQ * HQ, TILE), jnp.float32),
            pltpu.VMEM((NQ * HQ, TILE), jnp.float32),
            pltpu.SemaphoreType.DMA((9,)),
        ],
        compiler_params=params(),
        cost_estimate=cost(8),
        name="key_gradient",
    )(pairs, count, core, x, z, q, k, *values, parts, kept, got)


def to_everyone(value, axis):
    peers = lax.axis_size(axis)
    return lax.all_to_all(
        jnp.broadcast_to(value[None], (peers, *value.shape)), axis, 0, 0, tiled=True
    )


def along_x(value, by):
    return lax.ppermute(value, "x", [(n, (n + by) % 4) for n in range(4)])


def swap_cores(value):
    return lax.ppermute(value, "c", [(0, 1), (1, 0)])


def sum_over_keys(here, ahead, across, back):
    arrived = (here, along_x(across, 2), along_x(ahead, 1), along_x(back, -1))
    over_x = sum(p.astype(jnp.float32) for p in arrived).astype(jnp.bfloat16)
    return lax.all_to_all(over_x, Y, 0, 0, tiled=True)


def list_pairs(tile_mask):
    flat = tile_mask.reshape(-1) > 0
    number = flat.shape[0]
    place = jnp.arange(number, dtype=jnp.int32)
    ones = flat.astype(jnp.int32)
    before = jnp.sum(
        jnp.where(place[None, :] < place[:, None], ones[None, :], 0), axis=1
    )
    here = (before[None, :] == place[:, None]) & flat[None, :]
    spare = jnp.where(place < jnp.sum(ones), 0, NQ * 64 + NK)
    code = place // NK * 64 + place % NK
    pairs = jnp.sum(jnp.where(here, code[None, :], 0), axis=1) + spare
    return jnp.pad(pairs, (0, STEP), constant_values=NQ * 64 + NK), jnp.sum(ones)[None]


def body(query_states, out_grad, forward_out, key_states, value_states, block_mask):
    core, x, z = (lax.axis_index(a) for a in ("c", "x", "z"))
    y_hi = lax.axis_index("yh")
    y_lo = lax.axis_index("yl")
    q_own, kv_own = call_prepare(
        query_states, out_grad, forward_out, key_states, value_states, block_mask
    )
    q_all = lax.all_gather(q_own, ("c", "z"), axis=0, tiled=False)
    kv_y = lax.all_to_all(kv_own, Y, 0, 0, tiled=True)
    k_all = to_everyone(kv_y[:, :TILE, :HD], "x").reshape(NK, TILE, HD)
    mine = lax.dynamic_slice_in_dim(kv_y[:, TILE:, :NK], y_lo * 2, 2, 0)
    other = swap_cores(mine)
    v_y, other = lax.optimization_barrier((kv_y[:, :TILE, HD:], other))
    v_all = (v_y, along_x(v_y, -1), along_x(v_y, 2), along_x(v_y, 1))
    first = jnp.where(core == 0, mine, other)
    second = jnp.where(core == 0, other, mine)
    both = jnp.stack([first, second])
    both = lax.dynamic_slice_in_dim(both, y_hi * 8, 8, 2)
    both = both.reshape(2, 2, 8, 16, 2)
    both = jnp.where(core == 0, both[..., 0], both[..., 1])
    mask = both.transpose(0, 2, 3, 1).reshape(NQ, NK)
    pairs, count = list_pairs(mask)

    part, parts = call_stats(pairs, count, q_all, k_all)
    parts = lax.all_to_all(parts, ("c", "z"), 0, 0, tiled=True)
    kept, sent = call_query(pairs, count, core[None], x[None], q_all, k_all, v_all, part)
    got = swap_cores(sent)

    parts = jnp.maximum(parts, LOW)
    chip, *parts = call_key(
        pairs, count, core[None], x[None], z[None], q_all, k_all, v_all, parts, kept, got
    )
    dq_own = lax.psum_scatter(chip, "z", scatter_dimension=0, tiled=True)[0]
    query_grad, over_y = lax.optimization_barrier(
        (call_finish_queries(dq_own), sum_over_keys(*parts))
    )
    return query_grad, *call_finish_keys(over_y)


def solution(mesh):
    torus = Mesh(mesh.devices.reshape(4, 4, 2, 2, 8), ("x", "yl", "c", "yh", "z"))
    queries = P(("x", "yl", "c", "yh", "z"), None)
    keys = P(("yh", "z", "x", "yl", "c"), None)
    return jax.shard_map(
        body,
        mesh=torus,
        in_specs=(queries, queries, queries, keys, keys, P(("x", "yl", "c"), ("yh", "z"))),
        out_specs=(queries, keys, keys),
        check_vma=False,
    )
```

```python
import math

import jax
import jax.numpy as jnp
from jax import lax
from jax.experimental import pallas as pl
from jax.experimental.pallas import tpu as pltpu
from jax.sharding import Mesh
from jax.sharding import PartitionSpec as P

TILE = 128
HD = 128
HQ = 4
ROWS = TILE * HQ
NQ = 16
NK = 32
NY = 8
NZ = 8
QPAD = 272
KPAD = 144
LOW = -1e30
SCALE = 1.0 / math.sqrt(HD)
LOG2E = 1.0 / math.log(2.0)
Y = ("yl", "yh")
SCALARS = 4
STEP = 4


def dot(a, b, dims):
    return lax.dot_general(a, b, (dims, ((), ())), preferred_element_type=jnp.float32)


def heads(ref, r, first):
    return jnp.concatenate(
        [ref[r, first : first + TILE, h * HD : (h + 1) * HD] for h in range(HQ)], axis=0
    )


def unpack(info_ref, s):
    pair = info_ref[SCALARS + s]
    r, j = pair >> 6, pair & 63
    return r, j, jnp.minimum(r, NQ - 1), jnp.minimum(j, NK - 1)


def steps_of(info_ref):
    return (info_ref[0] + (STEP - 1)) // STEP


def stats_kernel(
    info_ref, q_hbm, k_hbm, out_ref, sent_hbm, q_ref, k_ref, m_ref, l_ref, sent_ref, sems
):
    copies = (
        pltpu.make_async_copy(q_hbm.at[:, pl.ds(0, TILE), :], q_ref, sems.at[0]),
        pltpu.make_async_copy(k_hbm, k_ref, sems.at[1]),
    )
    for copy in copies:
        copy.start()
    m_ref[...] = jnp.full(m_ref.shape, LOW, jnp.float32)
    l_ref[...] = jnp.zeros(l_ref.shape, jnp.float32)
    for copy in copies:
        copy.wait()

    def visit(i, carry):
        found = []
        for u in range(STEP):
            r, _, rq, jk = unpack(info_ref, i * STEP + u)
            scores = dot(k_ref[jk], heads(q_ref, rq, 0), ((1,), (1,))) * (SCALE * LOG2E)
            top = jnp.max(scores, axis=0, keepdims=True)
            found.append((r, top, jnp.sum(jnp.exp2(scores - top), axis=0, keepdims=True)))
        for r, top, total in found:
            old = m_ref[r]
            new = jnp.maximum(old, top)
            m_ref[r] = new
            l_ref[r] = l_ref[r] * jnp.exp2(old - new) + total * jnp.exp2(top - new)
        return carry

    lax.fori_loop(0, steps_of(info_ref), visit, 0)
    total = l_ref[...][:NQ]
    out_ref[...] = jnp.where(
        total > 0.0, m_ref[...][:NQ] + jnp.log2(jnp.maximum(total, 1e-30)), LOW
    )
    for n in range(NQ * HQ):
        sent_ref[n : n + 1] = out_ref[n // HQ, :, n % HQ * TILE : (n % HQ + 1) * TILE]
    copies = [pltpu.make_async_copy(sent_ref, sent_hbm.at[n], sems.at[n]) for n in range(NQ)]
    for copy in copies:
        copy.start()
    for copy in copies:
        copy.wait()


def weights_of(q_ref, k_ref, v_ref, total_ref, rq, jk):
    scores = dot(k_ref[jk], heads(q_ref, rq, 0), ((1,), (1,))) * (SCALE * LOG2E)
    probs = jnp.exp2(scores - total_ref[rq])
    grad_probs = dot(v_ref[jk], heads(q_ref, rq, TILE), ((1,), (1,)))
    delta = q_ref[rq, 2 * TILE : 2 * TILE + 16, :].astype(jnp.float32)[0:1, :]
    return probs, (probs * (grad_probs - delta)).astype(jnp.bfloat16)


def of_x(info_ref, by):
    return pl.ds(pl.multiple_of(((info_ref[2] + by) & 3) * NY, NY), NY)


def load(info_ref, q_hbm, k_hbm, values, q_ref, k_ref, v_ref, sems):
    copies = [
        pltpu.make_async_copy(q_hbm, q_ref, sems.at[0]),
        pltpu.make_async_copy(k_hbm, k_ref, sems.at[1]),
    ]
    for n, piece in enumerate(values):
        copies.append(pltpu.make_async_copy(piece, v_ref.at[of_x(info_ref, n)], sems.at[2 + n]))
    for copy in copies:
        copy.start()
    return copies


def query_kernel(
    info_ref, q_hbm, k_hbm, v0, v1, v2, v3, total_ref,
    kept_ref, sent_ref, q_ref, k_ref, v_ref, acc, ds_ref, sems,
):
    copies = load(info_ref, q_hbm, k_hbm, (v0, v1, v2, v3), q_ref, k_ref, v_ref, sems)
    acc[...] = jnp.zeros(acc.shape, jnp.float32)
    for copy in copies:
        copy.wait()

    def visit(i, carry):
        where = [unpack(info_ref, i * STEP + u) for u in range(STEP)]
        for u, (_, _, rq, jk) in enumerate(where):
            ds_ref[u] = weights_of(q_ref, k_ref, v_ref, total_ref, rq, jk)[1]
        parts = [dot(k_ref[w[3]], ds_ref[u], ((0,), (0,))) for u, w in enumerate(where)]
        for (r, _, _, _), part in zip(where, parts):
            acc[r] += part
        return carry

    lax.fori_loop(0, steps_of(info_ref), visit, 0)
    mine = info_ref[1] * NZ
    for n in range(NZ):
        kept_ref[n] = acc[mine + n].astype(jnp.bfloat16)
        sent_ref[n] = acc[NZ - mine + n].astype(jnp.bfloat16)


def key_kernel(
    info_ref, q_hbm, k_hbm, v0, v1, v2, v3, parts_ref,
    kept_hbm, got_hbm, chip_hbm, out0, out1, out2, out3, q_ref, k_ref, v_ref, k_acc, v_acc,
    p_ref, ds_ref, kept_ref, got_ref, chip_ref, total_ref, own_ref, far_ref, sems,
):
    two = (
        pltpu.make_async_copy(kept_hbm, kept_ref, sems.at[6]),
        pltpu.make_async_copy(got_hbm, got_ref, sems.at[7]),
    )
    for copy in two:
        copy.start()
    copies = load(info_ref, q_hbm, k_hbm, (v0, v1, v2, v3), q_ref, k_ref, v_ref, sems)
    k_acc[...] = jnp.zeros(k_acc.shape, jnp.float32)
    v_acc[...] = jnp.zeros(v_acc.shape, jnp.float32)
    top = parts_ref[0]
    for n in range(1, NQ):
        top = jnp.maximum(top, parts_ref[n])
    summed = jnp.exp2(parts_ref[0] - top)
    for n in range(1, NQ):
        summed += jnp.exp2(parts_ref[n] - top)
    total = top + jnp.log2(summed)
    for n in range(NQ * HQ):
        total_ref[n // HQ, :, n % HQ * TILE : (n % HQ + 1) * TILE] = total[n : n + 1]
    own_ref[...] = jnp.exp2(parts_ref[info_ref[1] * NZ + info_ref[3]] - total)
    far_ref[...] = jnp.exp2(parts_ref[(1 - info_ref[1]) * NZ + info_ref[3]] - total)
    for copy in two:
        copy.wait()
    for n in range(NZ):
        for h in range(HQ):
            row = pl.ds((info_ref[1] * NZ + n) * HQ + h, 1)
            cols = slice(h * TILE, (h + 1) * TILE)
            chip_ref[n, :, cols] = (
                kept_ref[n, :, cols].astype(jnp.float32) * own_ref[row]
                + got_ref[n, :, cols].astype(jnp.float32) * far_ref[row]
            ).astype(jnp.bfloat16)
    leave = pltpu.make_async_copy(chip_ref, chip_hbm, sems.at[8])
    leave.start()
    for copy in copies:
        copy.wait()

    def visit(i, carry):
        where = [unpack(info_ref, i * STEP + u) for u in range(STEP)]
        for u, (_, _, rq, jk) in enumerate(where):
            probs, grad_scores = weights_of(q_ref, k_ref, v_ref, total_ref, rq, jk)
            p_ref[u] = probs.astype(jnp.bfloat16)
            ds_ref[u] = grad_scores
        parts = [
            (
                dot(ds_ref[u], heads(q_ref, w[2], 0), ((1,), (0,))),
                dot(p_ref[u], heads(q_ref, w[2], TILE), ((1,), (0,))),
            )
            for u, w in enumerate(where)
        ]
        for (_, j, _, _), (of_key, of_value) in zip(where, parts):
            k_acc[j] += of_key
            v_acc[j] += of_value
        return carry

    lax.fori_loop(0, steps_of(info_ref), visit, 0)
    for n, out_ref in enumerate((out0, out1, out2, out3)):
        out_ref[:, :, :HD] = k_acc[of_x(info_ref, n)].astype(jnp.bfloat16)
        out_ref[:, :, HD:] = v_acc[of_x(info_ref, n)].astype(jnp.bfloat16)
    leave.wait()


def prepare_kernel(
    q_in, g_in, o_in, k_in, v_in, mask_in, q_hbm, kv_hbm,
    q_ref, g_ref, o_ref, mask_ref, kv_ref, delta_ref, sems,
):
    k_part, v_part = (kv_ref.at[pl.ds(0, TILE), pl.ds(n * HD, HD)] for n in range(2))
    ends = (q_ref, g_ref, o_ref, k_part, v_part, mask_ref)
    starts = (q_in, g_in, o_in, k_in, v_in, mask_in)
    q_get, g_get, o_get, k_get, v_get, mask_get = (
        pltpu.make_async_copy(start, end, sems.at[n])
        for n, (start, end) in enumerate(zip(starts, ends))
    )
    for copy in (g_get, o_get, q_get, k_get, v_get, mask_get):
        copy.start()
    kv_ref[TILE:, :] = jnp.zeros((KPAD - TILE, 2 * HD), jnp.bfloat16)
    rows = (pl.ds(0, TILE), pl.ds(TILE, TILE), pl.ds(2 * TILE, QPAD - 2 * TILE))
    q_put, g_put, delta_put = (
        pltpu.make_async_copy(start, q_hbm.at[row], sems.at[6 + n])
        for n, (start, row) in enumerate(zip((q_ref, g_ref, delta_ref), rows))
    )
    g_get.wait()
    g_put.start()
    o_get.wait()
    for h in range(HQ):
        cols = slice(h * HD, (h + 1) * HD)
        product = g_ref[:, cols].astype(jnp.float32) * o_ref[:, cols].astype(jnp.float32)
        delta = jnp.sum(product.T, axis=0, keepdims=True).astype(jnp.bfloat16)
        delta_ref[:, cols] = jnp.broadcast_to(delta, (QPAD - 2 * TILE, HD))
    delta_put.start()
    q_get.wait()
    q_put.start()
    k_get.wait()
    v_get.wait()
    mask_get.wait()
    kv_ref[TILE:, :NK] = mask_ref[...].astype(jnp.float32).astype(jnp.bfloat16)
    puts = [pltpu.make_async_copy(kv_ref, kv_hbm.at[n], sems.at[9 + n]) for n in range(NY)]
    for copy in puts:
        copy.start()
    for copy in (g_put, q_put, delta_put, *puts):
        copy.wait()


def finish_queries_kernel(dq_ref, query_ref):
    for h in range(HQ):
        cols = slice(h * TILE, (h + 1) * TILE)
        query_ref[:, cols] = (dq_ref[:, cols].astype(jnp.float32).T * SCALE).astype(jnp.bfloat16)


def finish_keys_kernel(over_y_ref, key_ref, value_ref):
    sums = over_y_ref[0].astype(jnp.float32)
    for n in range(1, NY):
        sums += over_y_ref[n].astype(jnp.float32)
    key_ref[...] = (sums[:, :HD] * SCALE).astype(jnp.bfloat16)
    value_ref[...] = sums[:, HD:].astype(jnp.bfloat16)


def vmem():
    return pl.BlockSpec(memory_space=pltpu.VMEM)


def smem():
    return pl.BlockSpec(memory_space=pltpu.SMEM)


def anywhere():
    return pl.BlockSpec(memory_space=pl.ANY)


def params(mib=50):
    return pltpu.CompilerParams(vmem_limit_bytes=mib * 1024 * 1024)


def cost(mib):
    return pl.CostEstimate(flops=10_000_000_000, bytes_accessed=mib << 20, transcendentals=0)


def loaded():
    return [
        pltpu.VMEM((NQ, QPAD, ROWS), jnp.bfloat16),
        pltpu.VMEM((NK, TILE, HD), jnp.bfloat16),
        pltpu.VMEM((NK, TILE, HD), jnp.bfloat16),
    ]


def call_prepare(q, g, o, k, v, mask):
    return pl.pallas_call(
        prepare_kernel,
        out_shape=(
            jax.ShapeDtypeStruct((QPAD, ROWS), jnp.bfloat16),
            jax.ShapeDtypeStruct((NY, KPAD, 2 * HD), jnp.bfloat16),
        ),
        in_specs=[anywhere()] * 6,
        out_specs=(anywhere(), anywhere()),
        scratch_shapes=[
            pltpu.VMEM((TILE, ROWS), jnp.bfloat16),
            pltpu.VMEM((TILE, ROWS), jnp.bfloat16),
            pltpu.VMEM((TILE, ROWS), jnp.bfloat16),
            pltpu.VMEM((2 * NZ, NK), jnp.int32),
            pltpu.VMEM((KPAD, 2 * HD), jnp.bfloat16),
            pltpu.VMEM((QPAD - 2 * TILE, ROWS), jnp.bfloat16),
            pltpu.SemaphoreType.DMA((9 + NY,)),
        ],
        compiler_params=params(60),
        name="prepare",
    )(q, g, o, k, v, mask)


def call_finish_queries(dq):
    return pl.pallas_call(
        finish_queries_kernel,
        out_shape=jax.ShapeDtypeStruct((TILE, ROWS), jnp.bfloat16),
        in_specs=[vmem()],
        out_specs=vmem(),
        compiler_params=params(8),
        name="finish_queries",
    )(dq)


def call_finish_keys(over_y):
    tile = jax.ShapeDtypeStruct((TILE, HD), jnp.bfloat16)
    return pl.pallas_call(
        finish_keys_kernel,
        out_shape=(tile, tile),
        in_specs=[vmem()],
        out_specs=(vmem(),) * 2,
        compiler_params=params(8),
        name="finish_keys",
    )(over_y)


def call_stats(info, q, k):
    return pl.pallas_call(
        stats_kernel,
        out_shape=(
            jax.ShapeDtypeStruct((NQ, 1, ROWS), jnp.float32),
            jax.ShapeDtypeStruct((NQ, NQ * HQ, TILE), jnp.float32),
        ),
        in_specs=[smem()] + [anywhere()] * 2,
        out_specs=(vmem(), anywhere()),
        scratch_shapes=[
            pltpu.VMEM((NQ, TILE, ROWS), jnp.bfloat16),
            pltpu.VMEM((NK, TILE, HD), jnp.bfloat16),
            pltpu.VMEM((NQ + 1, 1, ROWS), jnp.float32),
            pltpu.VMEM((NQ + 1, 1, ROWS), jnp.float32),
            pltpu.VMEM((NQ * HQ, TILE), jnp.float32),
            pltpu.SemaphoreType.DMA((NQ,)),
        ],
        compiler_params=params(),
        cost_estimate=cost(4),
        name="row_statistics",
    )(info, q, k)


def call_query(info, q, k, values, part):
    half = jax.ShapeDtypeStruct((NZ, HD, ROWS), jnp.bfloat16)
    return pl.pallas_call(
        query_kernel,
        out_shape=(half, half),
        in_specs=[smem()] + [anywhere()] * 6 + [vmem()],
        out_specs=(vmem(), vmem()),
        scratch_shapes=loaded()
        + [
            pltpu.VMEM((NQ + 1, HD, ROWS), jnp.float32),
            pltpu.VMEM((STEP, TILE, ROWS), jnp.bfloat16),
            pltpu.SemaphoreType.DMA((6,)),
        ],
        compiler_params=params(),
        cost_estimate=cost(8),
        name="query_gradient",
    )(info, q, k, *values, part)


def call_key(info, q, k, values, parts, kept, got):
    quarter = jax.ShapeDtypeStruct((NY, TILE, 2 * HD), jnp.bfloat16)
    half = pltpu.VMEM((NZ, HD, ROWS), jnp.bfloat16)
    return pl.pallas_call(
        key_kernel,
        out_shape=(jax.ShapeDtypeStruct((NZ, HD, ROWS), jnp.bfloat16),) + (quarter,) * 4,
        in_specs=[smem()] + [anywhere()] * 6 + [vmem()] + [anywhere()] * 2,
        out_specs=(anywhere(),) + (vmem(),) * 4,
        scratch_shapes=loaded()
        + [
            pltpu.VMEM((NK + 1, TILE, HD), jnp.float32),
            pltpu.VMEM((NK + 1, TILE, HD), jnp.float32),
            pltpu.VMEM((STEP, TILE, ROWS), jnp.bfloat16),
            pltpu.VMEM((STEP, TILE, ROWS), jnp.bfloat16),
            half,
            half,
            half,
            pltpu.VMEM((NQ, 1, ROWS), jnp.float32),
            pltpu.VMEM((NQ * HQ, TILE), jnp.float32),
            pltpu.VMEM((NQ * HQ, TILE), jnp.float32),
            pltpu.SemaphoreType.DMA((9,)),
        ],
        compiler_params=params(),
        cost_estimate=cost(8),
        name="key_gradient",
    )(info, q, k, *values, parts, kept, got)


def to_everyone(value, axis):
    peers = lax.axis_size(axis)
    return lax.all_to_all(
        jnp.broadcast_to(value[None], (peers, *value.shape)), axis, 0, 0, tiled=True
    )


def along_x(value, by):
    return lax.ppermute(value, "x", [(n, (n + by) % 4) for n in range(4)])


def swap_cores(value):
    return lax.ppermute(value, "c", [(0, 1), (1, 0)])


def sum_over_keys(here, ahead, across, back):
    arrived = (here, along_x(across, 2), along_x(ahead, 1), along_x(back, -1))
    over_x = sum(p.astype(jnp.float32) for p in arrived).astype(jnp.bfloat16)
    return lax.all_to_all(over_x, Y, 0, 0, tiled=True)


def list_pairs(tile_mask):
    flat = tile_mask.reshape(-1) > 0
    number = flat.shape[0]
    place = jnp.arange(number, dtype=jnp.int32)
    ones = flat.astype(jnp.int32)
    before = jnp.sum(
        jnp.where(place[None, :] < place[:, None], ones[None, :], 0), axis=1
    )
    here = (before[None, :] == place[:, None]) & flat[None, :]
    spare = jnp.where(place < jnp.sum(ones), 0, NQ * 64 + NK)
    code = place // NK * 64 + place % NK
    pairs = jnp.sum(jnp.where(here, code[None, :], 0), axis=1) + spare
    return jnp.pad(pairs, (0, STEP), constant_values=NQ * 64 + NK), jnp.sum(ones)


def body(query_states, out_grad, forward_out, key_states, value_states, block_mask):
    core, x, z = (lax.axis_index(a) for a in ("c", "x", "z"))
    y_hi = lax.axis_index("yh")
    y_lo = lax.axis_index("yl")
    q_own, kv_own = call_prepare(
        query_states, out_grad, forward_out, key_states, value_states, block_mask
    )
    q_all = lax.all_gather(q_own, ("c", "z"), axis=0, tiled=False)
    kv_y = lax.all_to_all(kv_own, Y, 0, 0, tiled=True)
    k_all = to_everyone(kv_y[:, :TILE, :HD], "x").reshape(NK, TILE, HD)
    mine = lax.dynamic_slice_in_dim(kv_y[:, TILE:, :NK], y_lo * 2, 2, 0)
    other = swap_cores(mine)
    v_y, other = lax.optimization_barrier((kv_y[:, :TILE, HD:], other))
    v_all = (v_y, along_x(v_y, -1), along_x(v_y, 2), along_x(v_y, 1))
    first = jnp.where(core == 0, mine, other)
    second = jnp.where(core == 0, other, mine)
    both = jnp.stack([first, second])
    both = lax.dynamic_slice_in_dim(both, y_hi * 8, 8, 2)
    both = both.reshape(2, 2, 8, 16, 2)
    both = jnp.where(core == 0, both[..., 0], both[..., 1])
    mask = both.transpose(0, 2, 3, 1).reshape(NQ, NK)
    pairs, count = list_pairs(mask)
    info = jnp.concatenate([jnp.stack([count, core, x, z]), pairs])

    part, parts = call_stats(info, q_all, k_all)
    parts = lax.all_to_all(parts, ("c", "z"), 0, 0, tiled=True)
    kept, sent = call_query(info, q_all, k_all, v_all, part)
    got = swap_cores(sent)

    parts = jnp.maximum(parts, LOW)
    chip, *parts = call_key(
        info, q_all, k_all, v_all, parts, kept, got
    )
    dq_own = lax.psum_scatter(chip, "z", scatter_dimension=0, tiled=True)[0]
    query_grad, over_y = lax.optimization_barrier(
        (call_finish_queries(dq_own), sum_over_keys(*parts))
    )
    return query_grad, *call_finish_keys(over_y)


def solution(mesh):
    torus = Mesh(mesh.devices.reshape(4, 4, 2, 2, 8), ("x", "yl", "c", "yh", "z"))
    queries = P(("x", "yl", "c", "yh", "z"), None)
    keys = P(("yh", "z", "x", "yl", "c"), None)
    return jax.shard_map(
        body,
        mesh=torus,
        in_specs=(queries, queries, queries, keys, keys, P(("x", "yl", "c"), ("yh", "z"))),
        out_specs=(queries, keys, keys),
        check_vma=False,
    )
```

```python
import math

import jax
import jax.numpy as jnp
from jax import lax
from jax.experimental import pallas as pl
from jax.experimental.pallas import tpu as pltpu
from jax.sharding import Mesh
from jax.sharding import PartitionSpec as P

TILE = 128
HD = 128
HQ = 4
ROWS = TILE * HQ
NQ = 16
NK = 32
NY = 8
NZ = 8
QPAD = 272
KPAD = 144
LOW = -1e30
SCALE = 1.0 / math.sqrt(HD)
LOG2E = 1.0 / math.log(2.0)
Y = ("yl", "yh")
SCALARS = 4
STEP = 4


def dot(a, b, dims):
    return lax.dot_general(a, b, (dims, ((), ())), preferred_element_type=jnp.float32)


def heads(ref, r, first):
    return jnp.concatenate(
        [ref[r, first : first + TILE, h * HD : (h + 1) * HD] for h in range(HQ)], axis=0
    )


def unpack(info_ref, s):
    pair = info_ref[SCALARS + s]
    r, j = pair >> 6, pair & 63
    return r, j, jnp.minimum(r, NQ - 1), jnp.minimum(j, NK - 1)


def steps_of(info_ref):
    return (info_ref[0] + (STEP - 1)) // STEP


def stats_kernel(
    info_ref, q_hbm, k_hbm, out_ref, sent_hbm, q_ref, k_ref, m_ref, l_ref, sent_ref, sems
):
    copies = (
        pltpu.make_async_copy(q_hbm.at[:, pl.ds(0, TILE), :], q_ref, sems.at[0]),
        pltpu.make_async_copy(k_hbm, k_ref, sems.at[1]),
    )
    for copy in copies:
        copy.start()
    m_ref[...] = jnp.full(m_ref.shape, LOW, jnp.float32)
    l_ref[...] = jnp.zeros(l_ref.shape, jnp.float32)
    for copy in copies:
        copy.wait()

    def visit(i, carry):
        found = []
        for u in range(STEP):
            r, _, rq, jk = unpack(info_ref, i * STEP + u)
            scores = dot(k_ref[jk], heads(q_ref, rq, 0), ((1,), (1,))) * (SCALE * LOG2E)
            top = jnp.max(scores, axis=0, keepdims=True)
            found.append((r, top, jnp.sum(jnp.exp2(scores - top), axis=0, keepdims=True)))
        for r, top, total in found:
            old = m_ref[r]
            new = jnp.maximum(old, top)
            m_ref[r] = new
            l_ref[r] = l_ref[r] * jnp.exp2(old - new) + total * jnp.exp2(top - new)
        return carry

    lax.fori_loop(0, steps_of(info_ref), visit, 0)
    total = l_ref[...][:NQ]
    out_ref[...] = jnp.where(
        total > 0.0, m_ref[...][:NQ] + jnp.log2(jnp.maximum(total, 1e-30)), LOW
    )
    for n in range(NQ * HQ):
        sent_ref[n : n + 1] = out_ref[n // HQ, :, n % HQ * TILE : (n % HQ + 1) * TILE]
    copies = [pltpu.make_async_copy(sent_ref, sent_hbm.at[n], sems.at[n]) for n in range(NQ)]
    for copy in copies:
        copy.start()
    for copy in copies:
        copy.wait()


def weights_of(q_ref, k_ref, v_ref, total_ref, rq, jk):
    scores = dot(k_ref[jk], heads(q_ref, rq, 0), ((1,), (1,))) * (SCALE * LOG2E)
    probs = jnp.exp2(scores - total_ref[rq])
    grad_probs = dot(v_ref[jk], heads(q_ref, rq, TILE), ((1,), (1,)))
    delta = q_ref[rq, 2 * TILE : 2 * TILE + 16, :].astype(jnp.float32)[0:1, :]
    return probs, (probs * (grad_probs - delta)).astype(jnp.bfloat16)


def of_x(info_ref, by):
    return pl.ds(pl.multiple_of(((info_ref[2] + by) & 3) * NY, NY), NY)


def load(info_ref, q_hbm, k_hbm, values, q_ref, k_ref, v_ref, sems):
    copies = [
        pltpu.make_async_copy(q_hbm, q_ref, sems.at[0]),
        pltpu.make_async_copy(k_hbm, k_ref, sems.at[1]),
    ]
    for n, piece in enumerate(values):
        copies.append(pltpu.make_async_copy(piece, v_ref.at[of_x(info_ref, n)], sems.at[2 + n]))
    for copy in copies:
        copy.start()
    return copies


def query_kernel(
    info_ref, q_hbm, k_hbm, v0, v1, v2, v3, total_ref,
    kept_ref, sent_ref, q_ref, k_ref, v_ref, acc, ds_ref, sems,
):
    copies = load(info_ref, q_hbm, k_hbm, (v0, v1, v2, v3), q_ref, k_ref, v_ref, sems)
    acc[...] = jnp.zeros(acc.shape, jnp.float32)
    for copy in copies:
        copy.wait()

    def visit(i, carry):
        where = [unpack(info_ref, i * STEP + u) for u in range(STEP)]
        for u, (_, _, rq, jk) in enumerate(where):
            ds_ref[u] = weights_of(q_ref, k_ref, v_ref, total_ref, rq, jk)[1]
        parts = [dot(k_ref[w[3]], ds_ref[u], ((0,), (0,))) for u, w in enumerate(where)]
        for (r, _, _, _), part in zip(where, parts):
            acc[r] += part
        return carry

    lax.fori_loop(0, steps_of(info_ref), visit, 0)
    mine = info_ref[1] * NZ
    for n in range(NZ):
        kept_ref[n] = acc[mine + n].astype(jnp.bfloat16)
        sent_ref[n] = acc[NZ - mine + n].astype(jnp.bfloat16)


def combine_kernel(info_ref, parts_ref, total_ref, own_ref, far_ref):
    top = parts_ref[0]
    for n in range(1, NQ):
        top = jnp.maximum(top, parts_ref[n])
    summed = jnp.exp2(parts_ref[0] - top)
    for n in range(1, NQ):
        summed += jnp.exp2(parts_ref[n] - top)
    total = top + jnp.log2(summed)
    for n in range(NQ * HQ):
        total_ref[n // HQ, :, n % HQ * TILE : (n % HQ + 1) * TILE] = total[n : n + 1]
    own_ref[...] = jnp.exp2(parts_ref[info_ref[1] * NZ + info_ref[3]] - total)
    far_ref[...] = jnp.exp2(parts_ref[(1 - info_ref[1]) * NZ + info_ref[3]] - total)


def weigh_kernel(info_ref, own_ref, far_ref, kept_ref, got_ref, chip_ref):
    for n in range(NZ):
        for h in range(HQ):
            row = pl.ds((info_ref[1] * NZ + n) * HQ + h, 1)
            cols = slice(h * TILE, (h + 1) * TILE)
            chip_ref[n, :, cols] = (
                kept_ref[n, :, cols].astype(jnp.float32) * own_ref[row]
                + got_ref[n, :, cols].astype(jnp.float32) * far_ref[row]
            ).astype(jnp.bfloat16)


def key_kernel(
    info_ref, q_hbm, k_hbm, v0, v1, v2, v3, total_ref, out0, out1, out2, out3,
    q_ref, k_ref, v_ref, k_acc, v_acc, p_ref, ds_ref, sems,
):
    copies = load(info_ref, q_hbm, k_hbm, (v0, v1, v2, v3), q_ref, k_ref, v_ref, sems)
    k_acc[...] = jnp.zeros(k_acc.shape, jnp.float32)
    v_acc[...] = jnp.zeros(v_acc.shape, jnp.float32)
    for copy in copies:
        copy.wait()

    def visit(i, carry):
        where = [unpack(info_ref, i * STEP + u) for u in range(STEP)]
        for u, (_, _, rq, jk) in enumerate(where):
            probs, grad_scores = weights_of(q_ref, k_ref, v_ref, total_ref, rq, jk)
            p_ref[u] = probs.astype(jnp.bfloat16)
            ds_ref[u] = grad_scores
        parts = [
            (
                dot(ds_ref[u], heads(q_ref, w[2], 0), ((1,), (0,))),
                dot(p_ref[u], heads(q_ref, w[2], TILE), ((1,), (0,))),
            )
            for u, w in enumerate(where)
        ]
        for (_, j, _, _), (of_key, of_value) in zip(where, parts):
            k_acc[j] += of_key
            v_acc[j] += of_value
        return carry

    lax.fori_loop(0, steps_of(info_ref), visit, 0)
    for n, out_ref in enumerate((out0, out1, out2, out3)):
        out_ref[:, :, :HD] = k_acc[of_x(info_ref, n)].astype(jnp.bfloat16)
        out_ref[:, :, HD:] = v_acc[of_x(info_ref, n)].astype(jnp.bfloat16)


def prepare_kernel(
    q_in, g_in, o_in, k_in, v_in, mask_in, q_hbm, kv_hbm,
    q_ref, g_ref, o_ref, mask_ref, kv_ref, delta_ref, sems,
):
    k_part, v_part = (kv_ref.at[pl.ds(0, TILE), pl.ds(n * HD, HD)] for n in range(2))
    ends = (q_ref, g_ref, o_ref, k_part, v_part, mask_ref)
    starts = (q_in, g_in, o_in, k_in, v_in, mask_in)
    q_get, g_get, o_get, k_get, v_get, mask_get = (
        pltpu.make_async_copy(start, end, sems.at[n])
        for n, (start, end) in enumerate(zip(starts, ends))
    )
    for copy in (g_get, o_get, q_get, k_get, v_get, mask_get):
        copy.start()
    kv_ref[TILE:, :] = jnp.zeros((KPAD - TILE, 2 * HD), jnp.bfloat16)
    rows = (pl.ds(0, TILE), pl.ds(TILE, TILE), pl.ds(2 * TILE, QPAD - 2 * TILE))
    q_put, g_put, delta_put = (
        pltpu.make_async_copy(start, q_hbm.at[row], sems.at[6 + n])
        for n, (start, row) in enumerate(zip((q_ref, g_ref, delta_ref), rows))
    )
    g_get.wait()
    g_put.start()
    o_get.wait()
    for h in range(HQ):
        cols = slice(h * HD, (h + 1) * HD)
        product = g_ref[:, cols].astype(jnp.float32) * o_ref[:, cols].astype(jnp.float32)
        delta = jnp.sum(product.T, axis=0, keepdims=True).astype(jnp.bfloat16)
        delta_ref[:, cols] = jnp.broadcast_to(delta, (QPAD - 2 * TILE, HD))
    delta_put.start()
    q_get.wait()
    q_put.start()
    k_get.wait()
    v_get.wait()
    mask_get.wait()
    kv_ref[TILE:, :NK] = mask_ref[...].astype(jnp.float32).astype(jnp.bfloat16)
    puts = [pltpu.make_async_copy(kv_ref, kv_hbm.at[n], sems.at[9 + n]) for n in range(NY)]
    for copy in puts:
        copy.start()
    for copy in (g_put, q_put, delta_put, *puts):
        copy.wait()


def finish_queries_kernel(dq_ref, query_ref):
    for h in range(HQ):
        cols = slice(h * TILE, (h + 1) * TILE)
        query_ref[:, cols] = (dq_ref[:, cols].astype(jnp.float32).T * SCALE).astype(jnp.bfloat16)


def finish_keys_kernel(over_y_ref, key_ref, value_ref):
    sums = over_y_ref[0].astype(jnp.float32)
    for n in range(1, NY):
        sums += over_y_ref[n].astype(jnp.float32)
    key_ref[...] = (sums[:, :HD] * SCALE).astype(jnp.bfloat16)
    value_ref[...] = sums[:, HD:].astype(jnp.bfloat16)


def vmem():
    return pl.BlockSpec(memory_space=pltpu.VMEM)


def smem():
    return pl.BlockSpec(memory_space=pltpu.SMEM)


def anywhere():
    return pl.BlockSpec(memory_space=pl.ANY)


def params(mib=50):
    return pltpu.CompilerParams(vmem_limit_bytes=mib * 1024 * 1024)


def cost(mib):
    return pl.CostEstimate(flops=10_000_000_000, bytes_accessed=mib << 20, transcendentals=0)


def loaded():
    return [
        pltpu.VMEM((NQ, QPAD, ROWS), jnp.bfloat16),
        pltpu.VMEM((NK, TILE, HD), jnp.bfloat16),
        pltpu.VMEM((NK, TILE, HD), jnp.bfloat16),
    ]


def call_prepare(q, g, o, k, v, mask):
    return pl.pallas_call(
        prepare_kernel,
        out_shape=(
            jax.ShapeDtypeStruct((QPAD, ROWS), jnp.bfloat16),
            jax.ShapeDtypeStruct((NY, KPAD, 2 * HD), jnp.bfloat16),
        ),
        in_specs=[anywhere()] * 6,
        out_specs=(anywhere(), anywhere()),
        scratch_shapes=[
            pltpu.VMEM((TILE, ROWS), jnp.bfloat16),
            pltpu.VMEM((TILE, ROWS), jnp.bfloat16),
            pltpu.VMEM((TILE, ROWS), jnp.bfloat16),
            pltpu.VMEM((2 * NZ, NK), jnp.int32),
            pltpu.VMEM((KPAD, 2 * HD), jnp.bfloat16),
            pltpu.VMEM((QPAD - 2 * TILE, ROWS), jnp.bfloat16),
            pltpu.SemaphoreType.DMA((9 + NY,)),
        ],
        compiler_params=params(60),
        name="prepare",
    )(q, g, o, k, v, mask)


def call_finish_queries(dq):
    return pl.pallas_call(
        finish_queries_kernel,
        out_shape=jax.ShapeDtypeStruct((TILE, ROWS), jnp.bfloat16),
        in_specs=[vmem()],
        out_specs=vmem(),
        compiler_params=params(8),
        name="finish_queries",
    )(dq)


def call_finish_keys(over_y):
    tile = jax.ShapeDtypeStruct((TILE, HD), jnp.bfloat16)
    return pl.pallas_call(
        finish_keys_kernel,
        out_shape=(tile, tile),
        in_specs=[vmem()],
        out_specs=(vmem(),) * 2,
        compiler_params=params(8),
        name="finish_keys",
    )(over_y)


def call_stats(info, q, k):
    return pl.pallas_call(
        stats_kernel,
        out_shape=(
            jax.ShapeDtypeStruct((NQ, 1, ROWS), jnp.float32),
            jax.ShapeDtypeStruct((NQ, NQ * HQ, TILE), jnp.float32),
        ),
        in_specs=[smem()] + [anywhere()] * 2,
        out_specs=(vmem(), anywhere()),
        scratch_shapes=[
            pltpu.VMEM((NQ, TILE, ROWS), jnp.bfloat16),
            pltpu.VMEM((NK, TILE, HD), jnp.bfloat16),
            pltpu.VMEM((NQ + 1, 1, ROWS), jnp.float32),
            pltpu.VMEM((NQ + 1, 1, ROWS), jnp.float32),
            pltpu.VMEM((NQ * HQ, TILE), jnp.float32),
            pltpu.SemaphoreType.DMA((NQ,)),
        ],
        compiler_params=params(),
        cost_estimate=cost(4),
        name="row_statistics",
    )(info, q, k)


def call_query(info, q, k, values, part):
    half = jax.ShapeDtypeStruct((NZ, HD, ROWS), jnp.bfloat16)
    return pl.pallas_call(
        query_kernel,
        out_shape=(half, half),
        in_specs=[smem()] + [anywhere()] * 6 + [vmem()],
        out_specs=(vmem(), vmem()),
        scratch_shapes=loaded()
        + [
            pltpu.VMEM((NQ + 1, HD, ROWS), jnp.float32),
            pltpu.VMEM((STEP, TILE, ROWS), jnp.bfloat16),
            pltpu.SemaphoreType.DMA((6,)),
        ],
        compiler_params=params(),
        cost_estimate=cost(8),
        name="query_gradient",
    )(info, q, k, *values, part)


def call_combine(info, parts):
    rows = jax.ShapeDtypeStruct((NQ * HQ, TILE), jnp.float32)
    return pl.pallas_call(
        combine_kernel,
        out_shape=(jax.ShapeDtypeStruct((NQ, 1, ROWS), jnp.float32), rows, rows),
        in_specs=[smem(), vmem()],
        out_specs=(vmem(),) * 3,
        compiler_params=params(8),
        cost_estimate=cost(8),
        name="combine_statistics",
    )(info, parts)


def call_weigh(info, own, far, kept, got):
    return pl.pallas_call(
        weigh_kernel,
        out_shape=jax.ShapeDtypeStruct((NZ, HD, ROWS), jnp.bfloat16),
        in_specs=[smem()] + [vmem()] * 4,
        out_specs=vmem(),
        compiler_params=params(8),
        name="weigh_queries",
    )(info, own, far, kept, got)


def call_key(info, q, k, values, total):
    quarter = jax.ShapeDtypeStruct((NY, TILE, 2 * HD), jnp.bfloat16)
    return pl.pallas_call(
        key_kernel,
        out_shape=(quarter,) * 4,
        in_specs=[smem()] + [anywhere()] * 6 + [vmem()],
        out_specs=(vmem(),) * 4,
        scratch_shapes=[
            *loaded(),
            pltpu.VMEM((NK + 1, TILE, HD), jnp.float32),
            pltpu.VMEM((NK + 1, TILE, HD), jnp.float32),
            pltpu.VMEM((STEP, TILE, ROWS), jnp.bfloat16),
            pltpu.VMEM((STEP, TILE, ROWS), jnp.bfloat16),
            pltpu.SemaphoreType.DMA((6,)),
        ],
        compiler_params=params(),
        cost_estimate=cost(8),
        name="key_gradient",
    )(info, q, k, *values, total)


def to_everyone(value, axis):
    peers = lax.axis_size(axis)
    return lax.all_to_all(
        jnp.broadcast_to(value[None], (peers, *value.shape)), axis, 0, 0, tiled=True
    )


def along_x(value, by):
    return lax.ppermute(value, "x", [(n, (n + by) % 4) for n in range(4)])


def swap_cores(value):
    return lax.ppermute(value, "c", [(0, 1), (1, 0)])


def sum_over_keys(here, ahead, across, back):
    arrived = (here, along_x(across, 2), along_x(ahead, 1), along_x(back, -1))
    over_x = sum(p.astype(jnp.float32) for p in arrived).astype(jnp.bfloat16)
    return lax.all_to_all(over_x, Y, 0, 0, tiled=True)


def list_pairs(tile_mask):
    flat = tile_mask.reshape(-1) > 0
    number = flat.shape[0]
    place = jnp.arange(number, dtype=jnp.int32)
    ones = flat.astype(jnp.int32)
    before = jnp.sum(
        jnp.where(place[None, :] < place[:, None], ones[None, :], 0), axis=1
    )
    here = (before[None, :] == place[:, None]) & flat[None, :]
    spare = jnp.where(place < jnp.sum(ones), 0, NQ * 64 + NK)
    code = place // NK * 64 + place % NK
    pairs = jnp.sum(jnp.where(here, code[None, :], 0), axis=1) + spare
    return jnp.pad(pairs, (0, STEP), constant_values=NQ * 64 + NK), jnp.sum(ones)


def body(query_states, out_grad, forward_out, key_states, value_states, block_mask):
    core, x, z = (lax.axis_index(a) for a in ("c", "x", "z"))
    y_hi = lax.axis_index("yh")
    y_lo = lax.axis_index("yl")
    q_own, kv_own = call_prepare(
        query_states, out_grad, forward_out, key_states, value_states, block_mask
    )
    q_all = lax.all_gather(q_own, ("c", "z"), axis=0, tiled=False)
    kv_y = lax.all_to_all(kv_own, Y, 0, 0, tiled=True)
    k_all = to_everyone(kv_y[:, :TILE, :HD], "x").reshape(NK, TILE, HD)
    mine = lax.dynamic_slice_in_dim(kv_y[:, TILE:, :NK], y_lo * 2, 2, 0)
    other = swap_cores(mine)
    v_y, other = lax.optimization_barrier((kv_y[:, :TILE, HD:], other))
    v_all = (v_y, along_x(v_y, -1), along_x(v_y, 2), along_x(v_y, 1))
    first = jnp.where(core == 0, mine, other)
    second = jnp.where(core == 0, other, mine)
    both = jnp.stack([first, second])
    both = lax.dynamic_slice_in_dim(both, y_hi * 8, 8, 2)
    both = both.reshape(2, 2, 8, 16, 2)
    both = jnp.where(core == 0, both[..., 0], both[..., 1])
    mask = both.transpose(0, 2, 3, 1).reshape(NQ, NK)
    pairs, count = list_pairs(mask)
    info = jnp.concatenate([jnp.stack([count, core, x, z]), pairs])

    part, parts = call_stats(info, q_all, k_all)
    parts = lax.all_to_all(parts, ("c", "z"), 0, 0, tiled=True)
    kept, sent = call_query(info, q_all, k_all, v_all, part)
    got = swap_cores(sent)

    total, own, far = call_combine(info, parts)
    chip = call_weigh(info, own, far, kept, got)
    parts = call_key(info, q_all, k_all, v_all, total)

    dq_own = lax.psum_scatter(chip, "z", scatter_dimension=0, tiled=True)[0]
    query_grad, over_y = lax.optimization_barrier(
        (call_finish_queries(dq_own), sum_over_keys(*parts))
    )
    return query_grad, *call_finish_keys(over_y)


def solution(mesh):
    torus = Mesh(mesh.devices.reshape(4, 4, 2, 2, 8), ("x", "yl", "c", "yh", "z"))
    queries = P(("x", "yl", "c", "yh", "z"), None)
    keys = P(("yh", "z", "x", "yl", "c"), None)
    return jax.shard_map(
        body,
        mesh=torus,
        in_specs=(queries, queries, queries, keys, keys, P(("x", "yl", "c"), ("yh", "z"))),
        out_specs=(queries, keys, keys),
        check_vma=False,
    )
```

```python
import math

import jax
import jax.numpy as jnp
from jax import lax
from jax.experimental import pallas as pl
from jax.experimental.pallas import tpu as pltpu
from jax.sharding import Mesh
from jax.sharding import PartitionSpec as P

TILE = 128
HD = 128
HQ = 4
ROWS = TILE * HQ
NQ = 16
NK = 32
NY = 8
NZ = 8
QPAD = 272
KPAD = 144
LOW = -1e30
SCALE = 1.0 / math.sqrt(HD)
LOG2E = 1.0 / math.log(2.0)
Y = ("yl", "yh")
SCALARS = 4
STEP = 4


def dot(a, b, dims):
    return lax.dot_general(a, b, (dims, ((), ())), preferred_element_type=jnp.float32)


def heads(ref, r, first):
    return jnp.concatenate(
        [ref[r, first : first + TILE, h * HD : (h + 1) * HD] for h in range(HQ)], axis=0
    )


def unpack(info_ref, s):
    pair = info_ref[SCALARS + s]
    r, j = pair >> 6, pair & 63
    return r, j, jnp.minimum(r, NQ - 1), jnp.minimum(j, NK - 1)


def steps_of(info_ref):
    return (info_ref[0] + (STEP - 1)) // STEP


def stats_kernel(
    info_ref, q_hbm, k_hbm, out_ref, sent_hbm, q_ref, k_ref, m_ref, l_ref, sent_ref, sems
):
    copies = (
        pltpu.make_async_copy(q_hbm.at[:, pl.ds(0, TILE), :], q_ref, sems.at[0]),
        pltpu.make_async_copy(k_hbm, k_ref, sems.at[1]),
    )
    for copy in copies:
        copy.start()
    m_ref[...] = jnp.full(m_ref.shape, LOW, jnp.float32)
    l_ref[...] = jnp.zeros(l_ref.shape, jnp.float32)
    for copy in copies:
        copy.wait()

    def visit(i, carry):
        found = []
        for u in range(STEP):
            r, _, rq, jk = unpack(info_ref, i * STEP + u)
            scores = dot(k_ref[jk], heads(q_ref, rq, 0), ((1,), (1,))) * (SCALE * LOG2E)
            top = jnp.max(scores, axis=0, keepdims=True)
            found.append((r, top, jnp.sum(jnp.exp2(scores - top), axis=0, keepdims=True)))
        for r, top, total in found:
            old = m_ref[r]
            new = jnp.maximum(old, top)
            m_ref[r] = new
            l_ref[r] = l_ref[r] * jnp.exp2(old - new) + total * jnp.exp2(top - new)
        return carry

    lax.fori_loop(0, steps_of(info_ref), visit, 0)
    total = l_ref[...][:NQ]
    out_ref[...] = jnp.where(
        total > 0.0, m_ref[...][:NQ] + jnp.log2(jnp.maximum(total, 1e-30)), LOW
    )
    for n in range(NQ * HQ):
        sent_ref[n : n + 1] = out_ref[n // HQ, :, n % HQ * TILE : (n % HQ + 1) * TILE]
    copies = [pltpu.make_async_copy(sent_ref, sent_hbm.at[n], sems.at[n]) for n in range(NQ)]
    for copy in copies:
        copy.start()
    for copy in copies:
        copy.wait()


def weights_of(q_ref, k_ref, v_ref, total_ref, rq, jk):
    scores = dot(k_ref[jk], heads(q_ref, rq, 0), ((1,), (1,))) * (SCALE * LOG2E)
    probs = jnp.exp2(scores - total_ref[rq])
    grad_probs = dot(v_ref[jk], heads(q_ref, rq, TILE), ((1,), (1,)))
    delta = q_ref[rq, 2 * TILE : 2 * TILE + 16, :].astype(jnp.float32)[0:1, :]
    return probs, (probs * (grad_probs - delta)).astype(jnp.bfloat16)


def of_x(info_ref, by):
    return pl.ds(pl.multiple_of(((info_ref[2] + by) & 3) * NY, NY), NY)


def load(info_ref, q_hbm, k_hbm, values, q_ref, k_ref, v_ref, sems):
    copies = [
        pltpu.make_async_copy(q_hbm, q_ref, sems.at[0]),
        pltpu.make_async_copy(k_hbm, k_ref, sems.at[1]),
    ]
    for n, piece in enumerate(values):
        copies.append(pltpu.make_async_copy(piece, v_ref.at[of_x(info_ref, n)], sems.at[2 + n]))
    for copy in copies:
        copy.start()
    return copies


def query_kernel(
    info_ref, q_hbm, k_hbm, v0, v1, v2, v3, total_ref,
    kept_ref, sent_ref, q_ref, k_ref, v_ref, acc, ds_ref, sems,
):
    copies = load(info_ref, q_hbm, k_hbm, (v0, v1, v2, v3), q_ref, k_ref, v_ref, sems)
    acc[...] = jnp.zeros(acc.shape, jnp.float32)
    for copy in copies:
        copy.wait()

    def visit(i, carry):
        where = [unpack(info_ref, i * STEP + u) for u in range(STEP)]
        for u, (_, _, rq, jk) in enumerate(where):
            ds_ref[u] = weights_of(q_ref, k_ref, v_ref, total_ref, rq, jk)[1]
        parts = [dot(k_ref[w[3]], ds_ref[u], ((0,), (0,))) for u, w in enumerate(where)]
        for (r, _, _, _), part in zip(where, parts):
            acc[r] += part
        return carry

    lax.fori_loop(0, steps_of(info_ref), visit, 0)
    mine = info_ref[1] * NZ
    for n in range(NZ):
        kept_ref[n] = acc[mine + n].astype(jnp.bfloat16)
        sent_ref[n] = acc[NZ - mine + n].astype(jnp.bfloat16)


def combine_kernel(info_ref, parts_ref, total_ref, own_ref, far_ref):
    top = parts_ref[0]
    for n in range(1, NQ):
        top = jnp.maximum(top, parts_ref[n])
    summed = jnp.exp2(parts_ref[0] - top)
    for n in range(1, NQ):
        summed += jnp.exp2(parts_ref[n] - top)
    total = top + jnp.log2(summed)
    for n in range(NQ * HQ):
        total_ref[n // HQ, :, n % HQ * TILE : (n % HQ + 1) * TILE] = total[n : n + 1]
    own_ref[...] = jnp.exp2(parts_ref[info_ref[1] * NZ + info_ref[3]] - total)
    far_ref[...] = jnp.exp2(parts_ref[(1 - info_ref[1]) * NZ + info_ref[3]] - total)


def key_kernel(
    info_ref, q_hbm, k_hbm, v0, v1, v2, v3, total_ref, own_ref, far_ref, kept_hbm, got_hbm,
    chip_hbm, out0, out1, out2, out3,
    q_ref, k_ref, v_ref, k_acc, v_acc, p_ref, ds_ref, kept_ref, got_ref, chip_ref, sems,
):
    two = (
        pltpu.make_async_copy(kept_hbm, kept_ref, sems.at[6]),
        pltpu.make_async_copy(got_hbm, got_ref, sems.at[7]),
    )
    for copy in two:
        copy.start()
    copies = load(info_ref, q_hbm, k_hbm, (v0, v1, v2, v3), q_ref, k_ref, v_ref, sems)
    k_acc[...] = jnp.zeros(k_acc.shape, jnp.float32)
    v_acc[...] = jnp.zeros(v_acc.shape, jnp.float32)
    for copy in two:
        copy.wait()
    for n in range(NZ):
        for h in range(HQ):
            row = pl.ds((info_ref[1] * NZ + n) * HQ + h, 1)
            cols = slice(h * TILE, (h + 1) * TILE)
            chip_ref[n, :, cols] = (
                kept_ref[n, :, cols].astype(jnp.float32) * own_ref[row]
                + got_ref[n, :, cols].astype(jnp.float32) * far_ref[row]
            ).astype(jnp.bfloat16)
    leave = pltpu.make_async_copy(chip_ref, chip_hbm, sems.at[8])
    leave.start()
    for copy in copies:
        copy.wait()

    def visit(i, carry):
        where = [unpack(info_ref, i * STEP + u) for u in range(STEP)]
        for u, (_, _, rq, jk) in enumerate(where):
            probs, grad_scores = weights_of(q_ref, k_ref, v_ref, total_ref, rq, jk)
            p_ref[u] = probs.astype(jnp.bfloat16)
            ds_ref[u] = grad_scores
        parts = [
            (
                dot(ds_ref[u], heads(q_ref, w[2], 0), ((1,), (0,))),
                dot(p_ref[u], heads(q_ref, w[2], TILE), ((1,), (0,))),
            )
            for u, w in enumerate(where)
        ]
        for (_, j, _, _), (of_key, of_value) in zip(where, parts):
            k_acc[j] += of_key
            v_acc[j] += of_value
        return carry

    lax.fori_loop(0, steps_of(info_ref), visit, 0)
    for n, out_ref in enumerate((out0, out1, out2, out3)):
        out_ref[:, :, :HD] = k_acc[of_x(info_ref, n)].astype(jnp.bfloat16)
        out_ref[:, :, HD:] = v_acc[of_x(info_ref, n)].astype(jnp.bfloat16)
    leave.wait()


def prepare_kernel(
    q_in, g_in, o_in, k_in, v_in, mask_in, q_hbm, kv_hbm,
    q_ref, g_ref, o_ref, mask_ref, kv_ref, delta_ref, sems,
):
    k_part, v_part = (kv_ref.at[pl.ds(0, TILE), pl.ds(n * HD, HD)] for n in range(2))
    ends = (q_ref, g_ref, o_ref, k_part, v_part, mask_ref)
    starts = (q_in, g_in, o_in, k_in, v_in, mask_in)
    q_get, g_get, o_get, k_get, v_get, mask_get = (
        pltpu.make_async_copy(start, end, sems.at[n])
        for n, (start, end) in enumerate(zip(starts, ends))
    )
    for copy in (g_get, o_get, q_get, k_get, v_get, mask_get):
        copy.start()
    kv_ref[TILE:, :] = jnp.zeros((KPAD - TILE, 2 * HD), jnp.bfloat16)
    rows = (pl.ds(0, TILE), pl.ds(TILE, TILE), pl.ds(2 * TILE, QPAD - 2 * TILE))
    q_put, g_put, delta_put = (
        pltpu.make_async_copy(start, q_hbm.at[row], sems.at[6 + n])
        for n, (start, row) in enumerate(zip((q_ref, g_ref, delta_ref), rows))
    )
    g_get.wait()
    g_put.start()
    o_get.wait()
    for h in range(HQ):
        cols = slice(h * HD, (h + 1) * HD)
        product = g_ref[:, cols].astype(jnp.float32) * o_ref[:, cols].astype(jnp.float32)
        delta = jnp.sum(product.T, axis=0, keepdims=True).astype(jnp.bfloat16)
        delta_ref[:, cols] = jnp.broadcast_to(delta, (QPAD - 2 * TILE, HD))
    delta_put.start()
    q_get.wait()
    q_put.start()
    k_get.wait()
    v_get.wait()
    mask_get.wait()
    kv_ref[TILE:, :NK] = mask_ref[...].astype(jnp.float32).astype(jnp.bfloat16)
    puts = [pltpu.make_async_copy(kv_ref, kv_hbm.at[n], sems.at[9 + n]) for n in range(NY)]
    for copy in puts:
        copy.start()
    for copy in (g_put, q_put, delta_put, *puts):
        copy.wait()


def finish_queries_kernel(dq_ref, query_ref):
    for h in range(HQ):
        cols = slice(h * TILE, (h + 1) * TILE)
        query_ref[:, cols] = (dq_ref[:, cols].astype(jnp.float32).T * SCALE).astype(jnp.bfloat16)


def finish_keys_kernel(over_y_ref, key_ref, value_ref):
    sums = over_y_ref[0].astype(jnp.float32)
    for n in range(1, NY):
        sums += over_y_ref[n].astype(jnp.float32)
    key_ref[...] = (sums[:, :HD] * SCALE).astype(jnp.bfloat16)
    value_ref[...] = sums[:, HD:].astype(jnp.bfloat16)


def vmem():
    return pl.BlockSpec(memory_space=pltpu.VMEM)


def smem():
    return pl.BlockSpec(memory_space=pltpu.SMEM)


def anywhere():
    return pl.BlockSpec(memory_space=pl.ANY)


def params(mib=50):
    return pltpu.CompilerParams(vmem_limit_bytes=mib * 1024 * 1024)


def cost(mib):
    return pl.CostEstimate(flops=10_000_000_000, bytes_accessed=mib << 20, transcendentals=0)


def loaded():
    return [
        pltpu.VMEM((NQ, QPAD, ROWS), jnp.bfloat16),
        pltpu.VMEM((NK, TILE, HD), jnp.bfloat16),
        pltpu.VMEM((NK, TILE, HD), jnp.bfloat16),
    ]


def call_prepare(q, g, o, k, v, mask):
    return pl.pallas_call(
        prepare_kernel,
        out_shape=(
            jax.ShapeDtypeStruct((QPAD, ROWS), jnp.bfloat16),
            jax.ShapeDtypeStruct((NY, KPAD, 2 * HD), jnp.bfloat16),
        ),
        in_specs=[anywhere()] * 6,
        out_specs=(anywhere(), anywhere()),
        scratch_shapes=[
            pltpu.VMEM((TILE, ROWS), jnp.bfloat16),
            pltpu.VMEM((TILE, ROWS), jnp.bfloat16),
            pltpu.VMEM((TILE, ROWS), jnp.bfloat16),
            pltpu.VMEM((2 * NZ, NK), jnp.int32),
            pltpu.VMEM((KPAD, 2 * HD), jnp.bfloat16),
            pltpu.VMEM((QPAD - 2 * TILE, ROWS), jnp.bfloat16),
            pltpu.SemaphoreType.DMA((9 + NY,)),
        ],
        compiler_params=params(60),
        name="prepare",
    )(q, g, o, k, v, mask)


def call_finish_queries(dq):
    return pl.pallas_call(
        finish_queries_kernel,
        out_shape=jax.ShapeDtypeStruct((TILE, ROWS), jnp.bfloat16),
        in_specs=[vmem()],
        out_specs=vmem(),
        compiler_params=params(8),
        name="finish_queries",
    )(dq)


def call_finish_keys(over_y):
    tile = jax.ShapeDtypeStruct((TILE, HD), jnp.bfloat16)
    return pl.pallas_call(
        finish_keys_kernel,
        out_shape=(tile, tile),
        in_specs=[vmem()],
        out_specs=(vmem(),) * 2,
        compiler_params=params(8),
        name="finish_keys",
    )(over_y)


def call_stats(info, q, k):
    return pl.pallas_call(
        stats_kernel,
        out_shape=(
            jax.ShapeDtypeStruct((NQ, 1, ROWS), jnp.float32),
            jax.ShapeDtypeStruct((NQ, NQ * HQ, TILE), jnp.float32),
        ),
        in_specs=[smem()] + [anywhere()] * 2,
        out_specs=(vmem(), anywhere()),
        scratch_shapes=[
            pltpu.VMEM((NQ, TILE, ROWS), jnp.bfloat16),
            pltpu.VMEM((NK, TILE, HD), jnp.bfloat16),
            pltpu.VMEM((NQ + 1, 1, ROWS), jnp.float32),
            pltpu.VMEM((NQ + 1, 1, ROWS), jnp.float32),
            pltpu.VMEM((NQ * HQ, TILE), jnp.float32),
            pltpu.SemaphoreType.DMA((NQ,)),
        ],
        compiler_params=params(),
        cost_estimate=cost(4),
        name="row_statistics",
    )(info, q, k)


def call_query(info, q, k, values, part):
    half = jax.ShapeDtypeStruct((NZ, HD, ROWS), jnp.bfloat16)
    return pl.pallas_call(
        query_kernel,
        out_shape=(half, half),
        in_specs=[smem()] + [anywhere()] * 6 + [vmem()],
        out_specs=(vmem(), vmem()),
        scratch_shapes=loaded()
        + [
            pltpu.VMEM((NQ + 1, HD, ROWS), jnp.float32),
            pltpu.VMEM((STEP, TILE, ROWS), jnp.bfloat16),
            pltpu.SemaphoreType.DMA((6,)),
        ],
        compiler_params=params(),
        cost_estimate=cost(8),
        name="query_gradient",
    )(info, q, k, *values, part)


def call_combine(info, parts):
    rows = jax.ShapeDtypeStruct((NQ * HQ, TILE), jnp.float32)
    return pl.pallas_call(
        combine_kernel,
        out_shape=(jax.ShapeDtypeStruct((NQ, 1, ROWS), jnp.float32), rows, rows),
        in_specs=[smem(), vmem()],
        out_specs=(vmem(),) * 3,
        compiler_params=params(8),
        cost_estimate=cost(8),
        name="combine_statistics",
    )(info, parts)


def call_key(info, q, k, values, statistics, kept, got):
    quarter = jax.ShapeDtypeStruct((NY, TILE, 2 * HD), jnp.bfloat16)
    half = pltpu.VMEM((NZ, HD, ROWS), jnp.bfloat16)
    return pl.pallas_call(
        key_kernel,
        out_shape=(jax.ShapeDtypeStruct((NZ, HD, ROWS), jnp.bfloat16),) + (quarter,) * 4,
        in_specs=[smem()] + [anywhere()] * 6 + [vmem()] * 3 + [anywhere()] * 2,
        out_specs=(anywhere(),) + (vmem(),) * 4,
        scratch_shapes=[
            *loaded(),
            pltpu.VMEM((NK + 1, TILE, HD), jnp.float32),
            pltpu.VMEM((NK + 1, TILE, HD), jnp.float32),
            pltpu.VMEM((STEP, TILE, ROWS), jnp.bfloat16),
            pltpu.VMEM((STEP, TILE, ROWS), jnp.bfloat16),
            half,
            half,
            half,
            pltpu.SemaphoreType.DMA((9,)),
        ],
        compiler_params=params(),
        cost_estimate=cost(8),
        name="key_gradient",
    )(info, q, k, *values, *statistics, kept, got)


def to_everyone(value, axis):
    peers = lax.axis_size(axis)
    return lax.all_to_all(
        jnp.broadcast_to(value[None], (peers, *value.shape)), axis, 0, 0, tiled=True
    )


def along_x(value, by):
    return lax.ppermute(value, "x", [(n, (n + by) % 4) for n in range(4)])


def swap_cores(value):
    return lax.ppermute(value, "c", [(0, 1), (1, 0)])


def sum_over_keys(here, ahead, across, back):
    arrived = (here, along_x(across, 2), along_x(ahead, 1), along_x(back, -1))
    over_x = sum(p.astype(jnp.float32) for p in arrived).astype(jnp.bfloat16)
    return lax.all_to_all(over_x, Y, 0, 0, tiled=True)


def list_pairs(tile_mask):
    flat = tile_mask.reshape(-1) > 0
    number = flat.shape[0]
    place = jnp.arange(number, dtype=jnp.int32)
    ones = flat.astype(jnp.int32)
    before = jnp.sum(
        jnp.where(place[None, :] < place[:, None], ones[None, :], 0), axis=1
    )
    here = (before[None, :] == place[:, None]) & flat[None, :]
    spare = jnp.where(place < jnp.sum(ones), 0, NQ * 64 + NK)
    code = place // NK * 64 + place % NK
    pairs = jnp.sum(jnp.where(here, code[None, :], 0), axis=1) + spare
    return jnp.pad(pairs, (0, STEP), constant_values=NQ * 64 + NK), jnp.sum(ones)


def body(query_states, out_grad, forward_out, key_states, value_states, block_mask):
    core, x, z = (lax.axis_index(a) for a in ("c", "x", "z"))
    y_hi = lax.axis_index("yh")
    y_lo = lax.axis_index("yl")
    q_own, kv_own = call_prepare(
        query_states, out_grad, forward_out, key_states, value_states, block_mask
    )
    q_all = lax.all_gather(q_own, ("c", "z"), axis=0, tiled=False)
    kv_y = lax.all_to_all(kv_own, Y, 0, 0, tiled=True)
    k_all = to_everyone(kv_y[:, :TILE, :HD], "x").reshape(NK, TILE, HD)
    mine = lax.dynamic_slice_in_dim(kv_y[:, TILE:, :NK], y_lo * 2, 2, 0)
    other = swap_cores(mine)
    v_y, other = lax.optimization_barrier((kv_y[:, :TILE, HD:], other))
    v_all = (v_y, along_x(v_y, -1), along_x(v_y, 2), along_x(v_y, 1))
    first = jnp.where(core == 0, mine, other)
    second = jnp.where(core == 0, other, mine)
    both = jnp.stack([first, second])
    both = lax.dynamic_slice_in_dim(both, y_hi * 8, 8, 2)
    both = both.reshape(2, 2, 8, 16, 2)
    both = jnp.where(core == 0, both[..., 0], both[..., 1])
    mask = both.transpose(0, 2, 3, 1).reshape(NQ, NK)
    pairs, count = list_pairs(mask)
    info = jnp.concatenate([jnp.stack([count, core, x, z]), pairs])

    part, parts = call_stats(info, q_all, k_all)
    parts = lax.all_to_all(parts, ("c", "z"), 0, 0, tiled=True)
    kept, sent = call_query(info, q_all, k_all, v_all, part)
    got = swap_cores(sent)

    statistics = call_combine(info, parts)
    chip, *parts = call_key(info, q_all, k_all, v_all, statistics, kept, got)

    dq_own = lax.psum_scatter(chip, "z", scatter_dimension=0, tiled=True)[0]
    query_grad, over_y = lax.optimization_barrier(
        (call_finish_queries(dq_own), sum_over_keys(*parts))
    )
    return query_grad, *call_finish_keys(over_y)


def solution(mesh):
    torus = Mesh(mesh.devices.reshape(4, 4, 2, 2, 8), ("x", "yl", "c", "yh", "z"))
    queries = P(("x", "yl", "c", "yh", "z"), None)
    keys = P(("yh", "z", "x", "yl", "c"), None)
    return jax.shard_map(
        body,
        mesh=torus,
        in_specs=(queries, queries, queries, keys, keys, P(("x", "yl", "c"), ("yh", "z"))),
        out_specs=(queries, keys, keys),
        check_vma=False,
    )
```

```python
import math

import jax
import jax.numpy as jnp
from jax import lax
from jax.experimental import pallas as pl
from jax.experimental.pallas import tpu as pltpu
from jax.sharding import Mesh
from jax.sharding import PartitionSpec as P

TILE = 128
HD = 128
HQ = 4
ROWS = TILE * HQ
NQ = 16
NK = 32
NY = 8
NZ = 8
QPAD = 272
KPAD = 144
LOW = -1e30
SCALE = 1.0 / math.sqrt(HD)
LOG2E = 1.0 / math.log(2.0)
Y = ("yl", "yh")
SCALARS = 4
STEP = 4


def dot(a, b, dims):
    return lax.dot_general(a, b, (dims, ((), ())), preferred_element_type=jnp.float32)


def heads(ref, r, first):
    return jnp.concatenate(
        [ref[r, first : first + TILE, h * HD : (h + 1) * HD] for h in range(HQ)], axis=0
    )


def unpack(info_ref, s):
    pair = info_ref[SCALARS + s]
    r, j = pair >> 6, pair & 63
    return r, j, jnp.minimum(r, NQ - 1), jnp.minimum(j, NK - 1)


def steps_of(info_ref):
    return (info_ref[0] + (STEP - 1)) // STEP


def stats_kernel(
    info_ref, q_hbm, k_hbm, sent_hbm, q_ref, k_ref, m_ref, l_ref, sent_ref, sems
):
    copies = (
        pltpu.make_async_copy(q_hbm.at[:, pl.ds(0, TILE), :], q_ref, sems.at[0]),
        pltpu.make_async_copy(k_hbm, k_ref, sems.at[1]),
    )
    for copy in copies:
        copy.start()
    m_ref[...] = jnp.full(m_ref.shape, LOW, jnp.float32)
    l_ref[...] = jnp.zeros(l_ref.shape, jnp.float32)
    for copy in copies:
        copy.wait()

    def visit(i, carry):
        found = []
        for u in range(STEP):
            r, _, rq, jk = unpack(info_ref, i * STEP + u)
            scores = dot(k_ref[jk], heads(q_ref, rq, 0), ((1,), (1,))) * (SCALE * LOG2E)
            top = jnp.max(scores, axis=0, keepdims=True)
            found.append((r, top, jnp.sum(jnp.exp2(scores - top), axis=0, keepdims=True)))
        for r, top, total in found:
            old = m_ref[r]
            new = jnp.maximum(old, top)
            m_ref[r] = new
            l_ref[r] = l_ref[r] * jnp.exp2(old - new) + total * jnp.exp2(top - new)
        return carry

    lax.fori_loop(0, steps_of(info_ref), visit, 0)
    total = l_ref[...][:NQ]
    part = jnp.where(
        total > 0.0, m_ref[...][:NQ] + jnp.log2(jnp.maximum(total, 1e-30)), LOW
    )
    for n in range(NQ * HQ):
        sent_ref[n : n + 1] = part[n // HQ, :, n % HQ * TILE : (n % HQ + 1) * TILE]
    copies = [pltpu.make_async_copy(sent_ref, sent_hbm.at[n], sems.at[n]) for n in range(NQ)]
    for copy in copies:
        copy.start()
    for copy in copies:
        copy.wait()


def weights_of(q_ref, k_ref, v_ref, total_ref, rq, jk):
    scores = dot(k_ref[jk], heads(q_ref, rq, 0), ((1,), (1,))) * (SCALE * LOG2E)
    probs = jnp.exp2(scores - total_ref[rq])
    grad_probs = dot(v_ref[jk], heads(q_ref, rq, TILE), ((1,), (1,)))
    delta = q_ref[rq, 2 * TILE : 2 * TILE + 16, :].astype(jnp.float32)[0:1, :]
    return probs, (probs * (grad_probs - delta)).astype(jnp.bfloat16)


def of_x(info_ref, by):
    return pl.ds(pl.multiple_of(((info_ref[2] + by) & 3) * NY, NY), NY)


def load(info_ref, q_hbm, k_hbm, values, q_ref, k_ref, v_ref, sems):
    copies = [
        pltpu.make_async_copy(q_hbm, q_ref, sems.at[0]),
        pltpu.make_async_copy(k_hbm, k_ref, sems.at[1]),
    ]
    for n, piece in enumerate(values):
        copies.append(pltpu.make_async_copy(piece, v_ref.at[of_x(info_ref, n)], sems.at[2 + n]))
    for copy in copies:
        copy.start()
    return copies


def query_kernel(
    info_ref, q_hbm, k_hbm, v0, v1, v2, v3, parts_hbm,
    kept_ref, sent_ref, q_ref, k_ref, v_ref, acc, ds_ref, part_ref, total_ref, sems,
):
    copies = load(info_ref, q_hbm, k_hbm, (v0, v1, v2, v3), q_ref, k_ref, v_ref, sems)
    copies.append(pltpu.make_async_copy(parts_hbm.at[0], part_ref, sems.at[6]))
    copies[-1].start()
    acc[...] = jnp.zeros(acc.shape, jnp.float32)
    for copy in copies:
        copy.wait()
    for n in range(NQ * HQ):
        total_ref[n // HQ, :, n % HQ * TILE : (n % HQ + 1) * TILE] = part_ref[n : n + 1]

    def visit(i, carry):
        where = [unpack(info_ref, i * STEP + u) for u in range(STEP)]
        for u, (_, _, rq, jk) in enumerate(where):
            ds_ref[u] = weights_of(q_ref, k_ref, v_ref, total_ref, rq, jk)[1]
        parts = [dot(k_ref[w[3]], ds_ref[u], ((0,), (0,))) for u, w in enumerate(where)]
        for (r, _, _, _), part in zip(where, parts):
            acc[r] += part
        return carry

    lax.fori_loop(0, steps_of(info_ref), visit, 0)
    mine = info_ref[1] * NZ
    for n in range(NZ):
        kept_ref[n] = acc[mine + n].astype(jnp.bfloat16)
        sent_ref[n] = acc[NZ - mine + n].astype(jnp.bfloat16)


def combine_kernel(info_ref, parts_ref, total_ref, own_ref, far_ref):
    top = parts_ref[0]
    for n in range(1, NQ):
        top = jnp.maximum(top, parts_ref[n])
    summed = jnp.exp2(parts_ref[0] - top)
    for n in range(1, NQ):
        summed += jnp.exp2(parts_ref[n] - top)
    total = top + jnp.log2(summed)
    for n in range(NQ * HQ):
        total_ref[n // HQ, :, n % HQ * TILE : (n % HQ + 1) * TILE] = total[n : n + 1]
    own_ref[...] = jnp.exp2(parts_ref[info_ref[1] * NZ + info_ref[3]] - total)
    far_ref[...] = jnp.exp2(parts_ref[(1 - info_ref[1]) * NZ + info_ref[3]] - total)


def key_kernel(
    info_ref, q_hbm, k_hbm, v0, v1, v2, v3, total_ref, own_ref, far_ref, kept_hbm, got_hbm,
    chip_hbm, out0, out1, out2, out3,
    q_ref, k_ref, v_ref, k_acc, v_acc, p_ref, ds_ref, kept_ref, got_ref, chip_ref, sems,
):
    two = (
        pltpu.make_async_copy(kept_hbm, kept_ref, sems.at[6]),
        pltpu.make_async_copy(got_hbm, got_ref, sems.at[7]),
    )
    for copy in two:
        copy.start()
    copies = load(info_ref, q_hbm, k_hbm, (v0, v1, v2, v3), q_ref, k_ref, v_ref, sems)
    k_acc[...] = jnp.zeros(k_acc.shape, jnp.float32)
    v_acc[...] = jnp.zeros(v_acc.shape, jnp.float32)
    for copy in two:
        copy.wait()
    for n in range(NZ):
        for h in range(HQ):
            row = pl.ds((info_ref[1] * NZ + n) * HQ + h, 1)
            cols = slice(h * TILE, (h + 1) * TILE)
            chip_ref[n, :, cols] = (
                kept_ref[n, :, cols].astype(jnp.float32) * own_ref[row]
                + got_ref[n, :, cols].astype(jnp.float32) * far_ref[row]
            ).astype(jnp.bfloat16)
    leave = pltpu.make_async_copy(chip_ref, chip_hbm, sems.at[8])
    leave.start()
    for copy in copies:
        copy.wait()

    def visit(i, carry):
        where = [unpack(info_ref, i * STEP + u) for u in range(STEP)]
        for u, (_, _, rq, jk) in enumerate(where):
            probs, grad_scores = weights_of(q_ref, k_ref, v_ref, total_ref, rq, jk)
            p_ref[u] = probs.astype(jnp.bfloat16)
            ds_ref[u] = grad_scores
        parts = [
            (
                dot(ds_ref[u], heads(q_ref, w[2], 0), ((1,), (0,))),
                dot(p_ref[u], heads(q_ref, w[2], TILE), ((1,), (0,))),
            )
            for u, w in enumerate(where)
        ]
        for (_, j, _, _), (of_key, of_value) in zip(where, parts):
            k_acc[j] += of_key
            v_acc[j] += of_value
        return carry

    lax.fori_loop(0, steps_of(info_ref), visit, 0)
    for n, out_ref in enumerate((out0, out1, out2, out3)):
        out_ref[:, :, :HD] = k_acc[of_x(info_ref, n)].astype(jnp.bfloat16)
        out_ref[:, :, HD:] = v_acc[of_x(info_ref, n)].astype(jnp.bfloat16)
    leave.wait()


def prepare_kernel(
    q_in, g_in, o_in, k_in, v_in, mask_in, q_hbm, kv_hbm,
    q_ref, g_ref, o_ref, mask_ref, kv_ref, delta_ref, sems,
):
    k_part, v_part = (kv_ref.at[pl.ds(0, TILE), pl.ds(n * HD, HD)] for n in range(2))
    ends = (q_ref, g_ref, o_ref, k_part, v_part, mask_ref)
    starts = (q_in, g_in, o_in, k_in, v_in, mask_in)
    q_get, g_get, o_get, k_get, v_get, mask_get = (
        pltpu.make_async_copy(start, end, sems.at[n])
        for n, (start, end) in enumerate(zip(starts, ends))
    )
    for copy in (g_get, o_get, q_get, k_get, v_get, mask_get):
        copy.start()
    kv_ref[TILE:, :] = jnp.zeros((KPAD - TILE, 2 * HD), jnp.bfloat16)
    rows = (pl.ds(0, TILE), pl.ds(TILE, TILE), pl.ds(2 * TILE, QPAD - 2 * TILE))
    q_put, g_put, delta_put = (
        pltpu.make_async_copy(start, q_hbm.at[row], sems.at[6 + n])
        for n, (start, row) in enumerate(zip((q_ref, g_ref, delta_ref), rows))
    )
    g_get.wait()
    g_put.start()
    o_get.wait()
    for h in range(HQ):
        cols = slice(h * HD, (h + 1) * HD)
        product = g_ref[:, cols].astype(jnp.float32) * o_ref[:, cols].astype(jnp.float32)
        delta = jnp.sum(product.T, axis=0, keepdims=True).astype(jnp.bfloat16)
        delta_ref[:, cols] = jnp.broadcast_to(delta, (QPAD - 2 * TILE, HD))
    delta_put.start()
    q_get.wait()
    q_put.start()
    k_get.wait()
    v_get.wait()
    mask_get.wait()
    kv_ref[TILE:, :NK] = mask_ref[...].astype(jnp.float32).astype(jnp.bfloat16)
    puts = [pltpu.make_async_copy(kv_ref, kv_hbm.at[n], sems.at[9 + n]) for n in range(NY)]
    for copy in puts:
        copy.start()
    for copy in (g_put, q_put, delta_put, *puts):
        copy.wait()


def split_kernel(kv_ref, k_hbm, v_hbm, sems):
    keys = kv_ref.at[:, pl.ds(0, TILE), pl.ds(0, HD)]
    values = kv_ref.at[:, pl.ds(0, TILE), pl.ds(HD, HD)]
    copies = [pltpu.make_async_copy(keys, k_hbm.at[n], sems.at[n]) for n in range(4)]
    copies.append(pltpu.make_async_copy(values, v_hbm, sems.at[4]))
    for copy in copies:
        copy.start()
    for copy in copies:
        copy.wait()


def finish_queries_kernel(dq_ref, query_ref):
    for h in range(HQ):
        cols = slice(h * TILE, (h + 1) * TILE)
        query_ref[:, cols] = (dq_ref[:, cols].astype(jnp.float32).T * SCALE).astype(jnp.bfloat16)


def finish_keys_kernel(over_y_ref, key_ref, value_ref):
    sums = over_y_ref[0].astype(jnp.float32)
    for n in range(1, NY):
        sums += over_y_ref[n].astype(jnp.float32)
    key_ref[...] = (sums[:, :HD] * SCALE).astype(jnp.bfloat16)
    value_ref[...] = sums[:, HD:].astype(jnp.bfloat16)


def vmem():
    return pl.BlockSpec(memory_space=pltpu.VMEM)


def smem():
    return pl.BlockSpec(memory_space=pltpu.SMEM)


def anywhere():
    return pl.BlockSpec(memory_space=pl.ANY)


def params(mib=50):
    return pltpu.CompilerParams(vmem_limit_bytes=mib * 1024 * 1024)


def cost(mib):
    return pl.CostEstimate(flops=10_000_000_000, bytes_accessed=mib << 20, transcendentals=0)


def loaded():
    return [
        pltpu.VMEM((NQ, QPAD, ROWS), jnp.bfloat16),
        pltpu.VMEM((NK, TILE, HD), jnp.bfloat16),
        pltpu.VMEM((NK, TILE, HD), jnp.bfloat16),
    ]


def call_prepare(q, g, o, k, v, mask):
    return pl.pallas_call(
        prepare_kernel,
        out_shape=(
            jax.ShapeDtypeStruct((QPAD, ROWS), jnp.bfloat16),
            jax.ShapeDtypeStruct((NY, KPAD, 2 * HD), jnp.bfloat16),
        ),
        in_specs=[anywhere()] * 6,
        out_specs=(anywhere(), anywhere()),
        scratch_shapes=[
            pltpu.VMEM((TILE, ROWS), jnp.bfloat16),
            pltpu.VMEM((TILE, ROWS), jnp.bfloat16),
            pltpu.VMEM((TILE, ROWS), jnp.bfloat16),
            pltpu.VMEM((2 * NZ, NK), jnp.int32),
            pltpu.VMEM((KPAD, 2 * HD), jnp.bfloat16),
            pltpu.VMEM((QPAD - 2 * TILE, ROWS), jnp.bfloat16),
            pltpu.SemaphoreType.DMA((9 + NY,)),
        ],
        compiler_params=params(60),
        name="prepare",
    )(q, g, o, k, v, mask)


def call_split(kv):
    return pl.pallas_call(
        split_kernel,
        out_shape=(
            jax.ShapeDtypeStruct((4, NY, TILE, HD), jnp.bfloat16),
            jax.ShapeDtypeStruct((NY, TILE, HD), jnp.bfloat16),
        ),
        in_specs=[vmem()],
        out_specs=(anywhere(), anywhere()),
        scratch_shapes=[pltpu.SemaphoreType.DMA((5,))],
        compiler_params=params(8),
        name="split_keys",
    )(kv)


def call_finish_queries(dq):
    return pl.pallas_call(
        finish_queries_kernel,
        out_shape=jax.ShapeDtypeStruct((TILE, ROWS), jnp.bfloat16),
        in_specs=[vmem()],
        out_specs=vmem(),
        compiler_params=params(8),
        name="finish_queries",
    )(dq)


def call_finish_keys(over_y):
    tile = jax.ShapeDtypeStruct((TILE, HD), jnp.bfloat16)
    return pl.pallas_call(
        finish_keys_kernel,
        out_shape=(tile, tile),
        in_specs=[vmem()],
        out_specs=(vmem(),) * 2,
        compiler_params=params(8),
        name="finish_keys",
    )(over_y)


def call_stats(info, q, k):
    return pl.pallas_call(
        stats_kernel,
        out_shape=jax.ShapeDtypeStruct((NQ, NQ * HQ, TILE), jnp.float32),
        in_specs=[smem()] + [anywhere()] * 2,
        out_specs=anywhere(),
        scratch_shapes=[
            pltpu.VMEM((NQ, TILE, ROWS), jnp.bfloat16),
            pltpu.VMEM((NK, TILE, HD), jnp.bfloat16),
            pltpu.VMEM((NQ + 1, 1, ROWS), jnp.float32),
            pltpu.VMEM((NQ + 1, 1, ROWS), jnp.float32),
            pltpu.VMEM((NQ * HQ, TILE), jnp.float32),
            pltpu.SemaphoreType.DMA((NQ,)),
        ],
        compiler_params=params(),
        cost_estimate=cost(4),
        name="row_statistics",
    )(info, q, k)


def call_query(info, q, k, values, parts):
    half = jax.ShapeDtypeStruct((NZ, HD, ROWS), jnp.bfloat16)
    return pl.pallas_call(
        query_kernel,
        out_shape=(half, half),
        in_specs=[smem()] + [anywhere()] * 7,
        out_specs=(vmem(), vmem()),
        scratch_shapes=loaded()
        + [
            pltpu.VMEM((NQ + 1, HD, ROWS), jnp.float32),
            pltpu.VMEM((STEP, TILE, ROWS), jnp.bfloat16),
            pltpu.VMEM((NQ * HQ, TILE), jnp.float32),
            pltpu.VMEM((NQ, 1, ROWS), jnp.float32),
            pltpu.SemaphoreType.DMA((7,)),
        ],
        compiler_params=params(),
        cost_estimate=cost(8),
        name="query_gradient",
    )(info, q, k, *values, parts)


def call_combine(info, parts):
    rows = jax.ShapeDtypeStruct((NQ * HQ, TILE), jnp.float32)
    return pl.pallas_call(
        combine_kernel,
        out_shape=(jax.ShapeDtypeStruct((NQ, 1, ROWS), jnp.float32), rows, rows),
        in_specs=[smem(), vmem()],
        out_specs=(vmem(),) * 3,
        compiler_params=params(8),
        cost_estimate=cost(8),
        name="combine_statistics",
    )(info, parts)


def call_key(info, q, k, values, statistics, kept, got):
    quarter = jax.ShapeDtypeStruct((NY, TILE, 2 * HD), jnp.bfloat16)
    half = pltpu.VMEM((NZ, HD, ROWS), jnp.bfloat16)
    return pl.pallas_call(
        key_kernel,
        out_shape=(jax.ShapeDtypeStruct((NZ, HD, ROWS), jnp.bfloat16),) + (quarter,) * 4,
        in_specs=[smem()] + [anywhere()] * 6 + [vmem()] * 3 + [anywhere()] * 2,
        out_specs=(anywhere(),) + (vmem(),) * 4,
        scratch_shapes=[
            *loaded(),
            pltpu.VMEM((NK + 1, TILE, HD), jnp.float32),
            pltpu.VMEM((NK + 1, TILE, HD), jnp.float32),
            pltpu.VMEM((STEP, TILE, ROWS), jnp.bfloat16),
            pltpu.VMEM((STEP, TILE, ROWS), jnp.bfloat16),
            half,
            half,
            half,
            pltpu.SemaphoreType.DMA((9,)),
        ],
        compiler_params=params(),
        cost_estimate=cost(8),
        name="key_gradient",
    )(info, q, k, *values, *statistics, kept, got)


def along_x(value, by):
    return lax.ppermute(value, "x", [(n, (n + by) % 4) for n in range(4)])


def swap_cores(value):
    return lax.ppermute(value, "c", [(0, 1), (1, 0)])


def sum_over_keys(here, ahead, across, back):
    arrived = (here, along_x(across, 2), along_x(ahead, 1), along_x(back, -1))
    over_x = sum(p.astype(jnp.float32) for p in arrived).astype(jnp.bfloat16)
    return lax.all_to_all(over_x, Y, 0, 0, tiled=True)


def list_pairs(tile_mask):
    flat = tile_mask.reshape(-1) > 0
    number = flat.shape[0]
    place = jnp.arange(number, dtype=jnp.int32)
    ones = flat.astype(jnp.int32)
    before = jnp.sum(
        jnp.where(place[None, :] < place[:, None], ones[None, :], 0), axis=1
    )
    here = (before[None, :] == place[:, None]) & flat[None, :]
    spare = jnp.where(place < jnp.sum(ones), 0, NQ * 64 + NK)
    code = place // NK * 64 + place % NK
    pairs = jnp.sum(jnp.where(here, code[None, :], 0), axis=1) + spare
    return jnp.pad(pairs, (0, STEP), constant_values=NQ * 64 + NK), jnp.sum(ones)


def body(query_states, out_grad, forward_out, key_states, value_states, block_mask):
    core, x, z = (lax.axis_index(a) for a in ("c", "x", "z"))
    y_hi = lax.axis_index("yh")
    y_lo = lax.axis_index("yl")
    q_own, kv_own = call_prepare(
        query_states, out_grad, forward_out, key_states, value_states, block_mask
    )
    q_all = lax.all_gather(q_own, ("c", "z"), axis=0, tiled=False)
    kv_y = lax.all_to_all(kv_own, Y, 0, 0, tiled=True)
    k_copies, v_y = call_split(kv_y)
    k_all = lax.all_to_all(k_copies, "x", 0, 0, tiled=True).reshape(NK, TILE, HD)
    mine = lax.dynamic_slice_in_dim(kv_y[:, TILE:, :NK], y_lo * 2, 2, 0)
    v_y, mine = lax.optimization_barrier((v_y, mine))
    other = swap_cores(mine)
    v_y, other = lax.optimization_barrier((v_y, other))
    v_all = (v_y, along_x(v_y, -1), along_x(v_y, 2), along_x(v_y, 1))
    first = jnp.where(core == 0, mine, other)
    second = jnp.where(core == 0, other, mine)
    both = jnp.stack([first, second])
    both = lax.dynamic_slice_in_dim(both, y_hi * 8, 8, 2)
    both = both.reshape(2, 2, 8, 16, 2)
    both = jnp.where(core == 0, both[..., 0], both[..., 1])
    mask = both.transpose(0, 2, 3, 1).reshape(NQ, NK)
    pairs, count = list_pairs(mask)
    info = jnp.concatenate([jnp.stack([count, core, x, z]), pairs])

    sent_parts = call_stats(info, q_all, k_all)
    parts = lax.all_to_all(sent_parts, ("c", "z"), 0, 0, tiled=True)
    kept, sent = call_query(info, q_all, k_all, v_all, sent_parts)
    got = swap_cores(sent)

    statistics = call_combine(info, parts)
    chip, *parts = call_key(info, q_all, k_all, v_all, statistics, kept, got)

    dq_own = lax.psum_scatter(chip, "z", scatter_dimension=0, tiled=True)[0]
    query_grad, over_y = lax.optimization_barrier(
        (call_finish_queries(dq_own), sum_over_keys(*parts))
    )
    return query_grad, *call_finish_keys(over_y)


def solution(mesh):
    torus = Mesh(mesh.devices.reshape(4, 4, 2, 2, 8), ("x", "yl", "c", "yh", "z"))
    queries = P(("x", "yl", "c", "yh", "z"), None)
    keys = P(("yh", "z", "x", "yl", "c"), None)
    return jax.shard_map(
        body,
        mesh=torus,
        in_specs=(queries, queries, queries, keys, keys, P(("x", "yl", "c"), ("yh", "z"))),
        out_specs=(queries, keys, keys),
        check_vma=False,
    )
```

```python
import math

import jax
import jax.numpy as jnp
from jax import lax
from jax.experimental import pallas as pl
from jax.experimental.pallas import tpu as pltpu
from jax.sharding import Mesh
from jax.sharding import PartitionSpec as P

TILE = 128
HD = 128
HQ = 4
ROWS = TILE * HQ
NQ = 16
NK = 32
NY = 8
NZ = 8
QPAD = 272
KPAD = 144
LOW = -1e30
SCALE = 1.0 / math.sqrt(HD)
LOG2E = 1.0 / math.log(2.0)
Y = ("yl", "yh")
SCALARS = 4
STEP = 6


def dot(a, b, dims):
    return lax.dot_general(a, b, (dims, ((), ())), preferred_element_type=jnp.float32)


def heads(ref, r, first):
    return jnp.concatenate(
        [ref[r, first : first + TILE, h * HD : (h + 1) * HD] for h in range(HQ)], axis=0
    )


def unpack(info_ref, s):
    pair = info_ref[SCALARS + s]
    r, j = pair >> 6, pair & 63
    return r, j, jnp.minimum(r, NQ - 1), jnp.minimum(j, NK - 1)


def steps_of(info_ref):
    return (info_ref[0] + (STEP - 1)) // STEP


def stats_kernel(
    info_ref, q_hbm, k_hbm, sent_hbm, q_ref, k_ref, m_ref, l_ref, sent_ref, sems
):
    copies = (
        pltpu.make_async_copy(q_hbm.at[:, pl.ds(0, TILE), :], q_ref, sems.at[0]),
        pltpu.make_async_copy(k_hbm, k_ref, sems.at[1]),
    )
    for copy in copies:
        copy.start()
    m_ref[...] = jnp.full(m_ref.shape, LOW, jnp.float32)
    l_ref[...] = jnp.zeros(l_ref.shape, jnp.float32)
    for copy in copies:
        copy.wait()

    def visit(i, carry):
        found = []
        for u in range(STEP):
            r, _, rq, jk = unpack(info_ref, i * STEP + u)
            scores = dot(k_ref[jk], heads(q_ref, rq, 0), ((1,), (1,))) * (SCALE * LOG2E)
            top = jnp.max(scores, axis=0, keepdims=True)
            found.append((r, top, jnp.sum(jnp.exp2(scores - top), axis=0, keepdims=True)))
        for r, top, total in found:
            old = m_ref[r]
            new = jnp.maximum(old, top)
            m_ref[r] = new
            l_ref[r] = l_ref[r] * jnp.exp2(old - new) + total * jnp.exp2(top - new)
        return carry

    lax.fori_loop(0, steps_of(info_ref), visit, 0)
    total = l_ref[...][:NQ]
    part = jnp.where(
        total > 0.0, m_ref[...][:NQ] + jnp.log2(jnp.maximum(total, 1e-30)), LOW
    )
    for n in range(NQ * HQ):
        sent_ref[n : n + 1] = part[n // HQ, :, n % HQ * TILE : (n % HQ + 1) * TILE]
    copies = [pltpu.make_async_copy(sent_ref, sent_hbm.at[n], sems.at[n]) for n in range(NQ)]
    for copy in copies:
        copy.start()
    for copy in copies:
        copy.wait()


def weights_of(q_ref, k_ref, v_ref, total_ref, rq, jk):
    scores = dot(k_ref[jk], heads(q_ref, rq, 0), ((1,), (1,))) * (SCALE * LOG2E)
    probs = jnp.exp2(scores - total_ref[rq])
    grad_probs = dot(v_ref[jk], heads(q_ref, rq, TILE), ((1,), (1,)))
    delta = q_ref[rq, 2 * TILE : 2 * TILE + 16, :].astype(jnp.float32)[0:1, :]
    return probs, (probs * (grad_probs - delta)).astype(jnp.bfloat16)


def of_x(info_ref, by):
    return pl.ds(pl.multiple_of(((info_ref[2] + by) & 3) * NY, NY), NY)


def load(info_ref, q_hbm, k_hbm, values, q_ref, k_ref, v_ref, sems):
    copies = [
        pltpu.make_async_copy(q_hbm, q_ref, sems.at[0]),
        pltpu.make_async_copy(k_hbm, k_ref, sems.at[1]),
    ]
    for n, piece in enumerate(values):
        copies.append(pltpu.make_async_copy(piece, v_ref.at[of_x(info_ref, n)], sems.at[2 + n]))
    for copy in copies:
        copy.start()
    return copies


def query_kernel(
    info_ref, q_hbm, k_hbm, v0, v1, v2, v3, parts_hbm,
    kept_ref, sent_ref, q_ref, k_ref, v_ref, acc, ds_ref, part_ref, total_ref, sems,
):
    copies = load(info_ref, q_hbm, k_hbm, (v0, v1, v2, v3), q_ref, k_ref, v_ref, sems)
    copies.append(pltpu.make_async_copy(parts_hbm.at[0], part_ref, sems.at[6]))
    copies[-1].start()
    acc[...] = jnp.zeros(acc.shape, jnp.float32)
    for copy in copies:
        copy.wait()
    for n in range(NQ * HQ):
        total_ref[n // HQ, :, n % HQ * TILE : (n % HQ + 1) * TILE] = part_ref[n : n + 1]

    def visit(i, carry):
        where = [unpack(info_ref, i * STEP + u) for u in range(STEP)]
        for u, (_, _, rq, jk) in enumerate(where):
            ds_ref[u] = weights_of(q_ref, k_ref, v_ref, total_ref, rq, jk)[1]
        parts = [dot(k_ref[w[3]], ds_ref[u], ((0,), (0,))) for u, w in enumerate(where)]
        for (r, _, _, _), part in zip(where, parts):
            acc[r] += part
        return carry

    lax.fori_loop(0, steps_of(info_ref), visit, 0)
    mine = info_ref[1] * NZ
    for n in range(NZ):
        kept_ref[n] = acc[mine + n].astype(jnp.bfloat16)
        sent_ref[n] = acc[NZ - mine + n].astype(jnp.bfloat16)


def combine_kernel(info_ref, parts_ref, total_ref, own_ref, far_ref):
    top = parts_ref[0]
    for n in range(1, NQ):
        top = jnp.maximum(top, parts_ref[n])
    summed = jnp.exp2(parts_ref[0] - top)
    for n in range(1, NQ):
        summed += jnp.exp2(parts_ref[n] - top)
    total = top + jnp.log2(summed)
    for n in range(NQ * HQ):
        total_ref[n // HQ, :, n % HQ * TILE : (n % HQ + 1) * TILE] = total[n : n + 1]
    own_ref[...] = jnp.exp2(parts_ref[info_ref[1] * NZ + info_ref[3]] - total)
    far_ref[...] = jnp.exp2(parts_ref[(1 - info_ref[1]) * NZ + info_ref[3]] - total)


def key_kernel(
    info_ref, q_hbm, k_hbm, v0, v1, v2, v3, total_ref, own_ref, far_ref, kept_hbm, got_hbm,
    chip_hbm, out0, out1, out2, out3,
    q_ref, k_ref, v_ref, k_acc, v_acc, p_ref, ds_ref, kept_ref, got_ref, chip_ref, sems,
):
    two = (
        pltpu.make_async_copy(kept_hbm, kept_ref, sems.at[6]),
        pltpu.make_async_copy(got_hbm, got_ref, sems.at[7]),
    )
    for copy in two:
        copy.start()
    copies = load(info_ref, q_hbm, k_hbm, (v0, v1, v2, v3), q_ref, k_ref, v_ref, sems)
    k_acc[...] = jnp.zeros(k_acc.shape, jnp.float32)
    v_acc[...] = jnp.zeros(v_acc.shape, jnp.float32)
    for copy in two:
        copy.wait()
    for n in range(NZ):
        for h in range(HQ):
            row = pl.ds((info_ref[1] * NZ + n) * HQ + h, 1)
            cols = slice(h * TILE, (h + 1) * TILE)
            chip_ref[n, :, cols] = (
                kept_ref[n, :, cols].astype(jnp.float32) * own_ref[row]
                + got_ref[n, :, cols].astype(jnp.float32) * far_ref[row]
            ).astype(jnp.bfloat16)
    leave = pltpu.make_async_copy(chip_ref, chip_hbm, sems.at[8])
    leave.start()
    for copy in copies:
        copy.wait()

    def visit(i, carry):
        where = [unpack(info_ref, i * STEP + u) for u in range(STEP)]
        for u, (_, _, rq, jk) in enumerate(where):
            probs, grad_scores = weights_of(q_ref, k_ref, v_ref, total_ref, rq, jk)
            p_ref[u] = probs.astype(jnp.bfloat16)
            ds_ref[u] = grad_scores
        parts = [
            (
                dot(ds_ref[u], heads(q_ref, w[2], 0), ((1,), (0,))),
                dot(p_ref[u], heads(q_ref, w[2], TILE), ((1,), (0,))),
            )
            for u, w in enumerate(where)
        ]
        for (_, j, _, _), (of_key, of_value) in zip(where, parts):
            k_acc[j] += of_key
            v_acc[j] += of_value
        return carry

    lax.fori_loop(0, steps_of(info_ref), visit, 0)
    for n, out_ref in enumerate((out0, out1, out2, out3)):
        out_ref[:, :, :HD] = k_acc[of_x(info_ref, n)].astype(jnp.bfloat16)
        out_ref[:, :, HD:] = v_acc[of_x(info_ref, n)].astype(jnp.bfloat16)
    leave.wait()


def prepare_kernel(
    q_in, g_in, o_in, k_in, v_in, mask_in, q_hbm, kv_hbm,
    q_ref, g_ref, o_ref, mask_ref, kv_ref, delta_ref, sems,
):
    k_part, v_part = (kv_ref.at[pl.ds(0, TILE), pl.ds(n * HD, HD)] for n in range(2))
    ends = (q_ref, g_ref, o_ref, k_part, v_part, mask_ref)
    starts = (q_in, g_in, o_in, k_in, v_in, mask_in)
    q_get, g_get, o_get, k_get, v_get, mask_get = (
        pltpu.make_async_copy(start, end, sems.at[n])
        for n, (start, end) in enumerate(zip(starts, ends))
    )
    for copy in (g_get, o_get, q_get, k_get, v_get, mask_get):
        copy.start()
    kv_ref[TILE:, :] = jnp.zeros((KPAD - TILE, 2 * HD), jnp.bfloat16)
    rows = (pl.ds(0, TILE), pl.ds(TILE, TILE), pl.ds(2 * TILE, QPAD - 2 * TILE))
    q_put, g_put, delta_put = (
        pltpu.make_async_copy(start, q_hbm.at[row], sems.at[6 + n])
        for n, (start, row) in enumerate(zip((q_ref, g_ref, delta_ref), rows))
    )
    g_get.wait()
    g_put.start()
    o_get.wait()
    for h in range(HQ):
        cols = slice(h * HD, (h + 1) * HD)
        product = g_ref[:, cols].astype(jnp.float32) * o_ref[:, cols].astype(jnp.float32)
        delta = jnp.sum(product.T, axis=0, keepdims=True).astype(jnp.bfloat16)
        delta_ref[:, cols] = jnp.broadcast_to(delta, (QPAD - 2 * TILE, HD))
    delta_put.start()
    q_get.wait()
    q_put.start()
    k_get.wait()
    v_get.wait()
    mask_get.wait()
    kv_ref[TILE:, :NK] = mask_ref[...].astype(jnp.float32).astype(jnp.bfloat16)
    puts = [pltpu.make_async_copy(kv_ref, kv_hbm.at[n], sems.at[9 + n]) for n in range(NY)]
    for copy in puts:
        copy.start()
    for copy in (g_put, q_put, delta_put, *puts):
        copy.wait()


def split_kernel(kv_ref, k_hbm, v_hbm, sems):
    keys = kv_ref.at[:, pl.ds(0, TILE), pl.ds(0, HD)]
    values = kv_ref.at[:, pl.ds(0, TILE), pl.ds(HD, HD)]
    copies = [pltpu.make_async_copy(keys, k_hbm.at[n], sems.at[n]) for n in range(4)]
    copies.append(pltpu.make_async_copy(values, v_hbm, sems.at[4]))
    for copy in copies:
        copy.start()
    for copy in copies:
        copy.wait()


def finish_queries_kernel(dq_ref, query_ref):
    for h in range(HQ):
        cols = slice(h * TILE, (h + 1) * TILE)
        query_ref[:, cols] = (dq_ref[:, cols].astype(jnp.float32).T * SCALE).astype(jnp.bfloat16)


def finish_keys_kernel(over_y_ref, key_ref, value_ref):
    sums = over_y_ref[0].astype(jnp.float32)
    for n in range(1, NY):
        sums += over_y_ref[n].astype(jnp.float32)
    key_ref[...] = (sums[:, :HD] * SCALE).astype(jnp.bfloat16)
    value_ref[...] = sums[:, HD:].astype(jnp.bfloat16)


def vmem():
    return pl.BlockSpec(memory_space=pltpu.VMEM)


def smem():
    return pl.BlockSpec(memory_space=pltpu.SMEM)


def anywhere():
    return pl.BlockSpec(memory_space=pl.ANY)


def params(mib=50):
    return pltpu.CompilerParams(vmem_limit_bytes=mib * 1024 * 1024)


def cost(mib):
    return pl.CostEstimate(flops=10_000_000_000, bytes_accessed=mib << 20, transcendentals=0)


def loaded():
    return [
        pltpu.VMEM((NQ, QPAD, ROWS), jnp.bfloat16),
        pltpu.VMEM((NK, TILE, HD), jnp.bfloat16),
        pltpu.VMEM((NK, TILE, HD), jnp.bfloat16),
    ]


def call_prepare(q, g, o, k, v, mask):
    return pl.pallas_call(
        prepare_kernel,
        out_shape=(
            jax.ShapeDtypeStruct((QPAD, ROWS), jnp.bfloat16),
            jax.ShapeDtypeStruct((NY, KPAD, 2 * HD), jnp.bfloat16),
        ),
        in_specs=[anywhere()] * 6,
        out_specs=(anywhere(), anywhere()),
        scratch_shapes=[
            pltpu.VMEM((TILE, ROWS), jnp.bfloat16),
            pltpu.VMEM((TILE, ROWS), jnp.bfloat16),
            pltpu.VMEM((TILE, ROWS), jnp.bfloat16),
            pltpu.VMEM((2 * NZ, NK), jnp.int32),
            pltpu.VMEM((KPAD, 2 * HD), jnp.bfloat16),
            pltpu.VMEM((QPAD - 2 * TILE, ROWS), jnp.bfloat16),
            pltpu.SemaphoreType.DMA((9 + NY,)),
        ],
        compiler_params=params(60),
        name="prepare",
    )(q, g, o, k, v, mask)


def call_split(kv):
    return pl.pallas_call(
        split_kernel,
        out_shape=(
            jax.ShapeDtypeStruct((4, NY, TILE, HD), jnp.bfloat16),
            jax.ShapeDtypeStruct((NY, TILE, HD), jnp.bfloat16),
        ),
        in_specs=[vmem()],
        out_specs=(anywhere(), anywhere()),
        scratch_shapes=[pltpu.SemaphoreType.DMA((5,))],
        compiler_params=params(8),
        name="split_keys",
    )(kv)


def call_finish_queries(dq):
    return pl.pallas_call(
        finish_queries_kernel,
        out_shape=jax.ShapeDtypeStruct((TILE, ROWS), jnp.bfloat16),
        in_specs=[vmem()],
        out_specs=vmem(),
        compiler_params=params(8),
        name="finish_queries",
    )(dq)


def call_finish_keys(over_y):
    tile = jax.ShapeDtypeStruct((TILE, HD), jnp.bfloat16)
    return pl.pallas_call(
        finish_keys_kernel,
        out_shape=(tile, tile),
        in_specs=[vmem()],
        out_specs=(vmem(),) * 2,
        compiler_params=params(8),
        name="finish_keys",
    )(over_y)


def call_stats(info, q, k):
    return pl.pallas_call(
        stats_kernel,
        out_shape=jax.ShapeDtypeStruct((NQ, NQ * HQ, TILE), jnp.float32),
        in_specs=[smem()] + [anywhere()] * 2,
        out_specs=anywhere(),
        scratch_shapes=[
            pltpu.VMEM((NQ, TILE, ROWS), jnp.bfloat16),
            pltpu.VMEM((NK, TILE, HD), jnp.bfloat16),
            pltpu.VMEM((NQ + 1, 1, ROWS), jnp.float32),
            pltpu.VMEM((NQ + 1, 1, ROWS), jnp.float32),
            pltpu.VMEM((NQ * HQ, TILE), jnp.float32),
            pltpu.SemaphoreType.DMA((NQ,)),
        ],
        compiler_params=params(),
        cost_estimate=cost(4),
        name="row_statistics",
    )(info, q, k)


def call_query(info, q, k, values, parts):
    half = jax.ShapeDtypeStruct((NZ, HD, ROWS), jnp.bfloat16)
    return pl.pallas_call(
        query_kernel,
        out_shape=(half, half),
        in_specs=[smem()] + [anywhere()] * 7,
        out_specs=(vmem(), vmem()),
        scratch_shapes=loaded()
        + [
            pltpu.VMEM((NQ + 1, HD, ROWS), jnp.float32),
            pltpu.VMEM((STEP, TILE, ROWS), jnp.bfloat16),
            pltpu.VMEM((NQ * HQ, TILE), jnp.float32),
            pltpu.VMEM((NQ, 1, ROWS), jnp.float32),
            pltpu.SemaphoreType.DMA((7,)),
        ],
        compiler_params=params(),
        cost_estimate=cost(8),
        name="query_gradient",
    )(info, q, k, *values, parts)


def call_combine(info, parts):
    rows = jax.ShapeDtypeStruct((NQ * HQ, TILE), jnp.float32)
    return pl.pallas_call(
        combine_kernel,
        out_shape=(jax.ShapeDtypeStruct((NQ, 1, ROWS), jnp.float32), rows, rows),
        in_specs=[smem(), vmem()],
        out_specs=(vmem(),) * 3,
        compiler_params=params(8),
        cost_estimate=cost(8),
        name="combine_statistics",
    )(info, parts)


def call_key(info, q, k, values, statistics, kept, got):
    quarter = jax.ShapeDtypeStruct((NY, TILE, 2 * HD), jnp.bfloat16)
    half = pltpu.VMEM((NZ, HD, ROWS), jnp.bfloat16)
    return pl.pallas_call(
        key_kernel,
        out_shape=(jax.ShapeDtypeStruct((NZ, HD, ROWS), jnp.bfloat16),) + (quarter,) * 4,
        in_specs=[smem()] + [anywhere()] * 6 + [vmem()] * 3 + [anywhere()] * 2,
        out_specs=(anywhere(),) + (vmem(),) * 4,
        scratch_shapes=[
            *loaded(),
            pltpu.VMEM((NK + 1, TILE, HD), jnp.float32),
            pltpu.VMEM((NK + 1, TILE, HD), jnp.float32),
            pltpu.VMEM((STEP, TILE, ROWS), jnp.bfloat16),
            pltpu.VMEM((STEP, TILE, ROWS), jnp.bfloat16),
            half,
            half,
            half,
            pltpu.SemaphoreType.DMA((9,)),
        ],
        compiler_params=params(),
        cost_estimate=cost(8),
        name="key_gradient",
    )(info, q, k, *values, *statistics, kept, got)


def along_x(value, by):
    return lax.ppermute(value, "x", [(n, (n + by) % 4) for n in range(4)])


def swap_cores(value):
    return lax.ppermute(value, "c", [(0, 1), (1, 0)])


def sum_over_keys(here, ahead, across, back):
    arrived = (here, along_x(across, 2), along_x(ahead, 1), along_x(back, -1))
    over_x = sum(p.astype(jnp.float32) for p in arrived).astype(jnp.bfloat16)
    return lax.all_to_all(over_x, Y, 0, 0, tiled=True)


def list_pairs(tile_mask):
    flat = tile_mask.reshape(-1) > 0
    number = flat.shape[0]
    place = jnp.arange(number, dtype=jnp.int32)
    ones = flat.astype(jnp.int32)
    before = jnp.sum(
        jnp.where(place[None, :] < place[:, None], ones[None, :], 0), axis=1
    )
    here = (before[None, :] == place[:, None]) & flat[None, :]
    spare = jnp.where(place < jnp.sum(ones), 0, NQ * 64 + NK)
    code = place // NK * 64 + place % NK
    pairs = jnp.sum(jnp.where(here, code[None, :], 0), axis=1) + spare
    return jnp.pad(pairs, (0, STEP), constant_values=NQ * 64 + NK), jnp.sum(ones)


def body(query_states, out_grad, forward_out, key_states, value_states, block_mask):
    core, x, z = (lax.axis_index(a) for a in ("c", "x", "z"))
    y_hi = lax.axis_index("yh")
    y_lo = lax.axis_index("yl")
    q_own, kv_own = call_prepare(
        query_states, out_grad, forward_out, key_states, value_states, block_mask
    )
    q_all = lax.all_gather(q_own, ("c", "z"), axis=0, tiled=False)
    kv_y = lax.all_to_all(kv_own, Y, 0, 0, tiled=True)
    k_copies, v_y = call_split(kv_y)
    k_all = lax.all_to_all(k_copies, "x", 0, 0, tiled=True).reshape(NK, TILE, HD)
    mine = lax.dynamic_slice_in_dim(kv_y[:, TILE:, :NK], y_lo * 2, 2, 0)
    v_y, mine = lax.optimization_barrier((v_y, mine))
    other = swap_cores(mine)
    v_y, other = lax.optimization_barrier((v_y, other))
    v_all = (v_y, along_x(v_y, -1), along_x(v_y, 2), along_x(v_y, 1))
    first = jnp.where(core == 0, mine, other)
    second = jnp.where(core == 0, other, mine)
    both = jnp.stack([first, second])
    both = lax.dynamic_slice_in_dim(both, y_hi * 8, 8, 2)
    both = both.reshape(2, 2, 8, 16, 2)
    both = jnp.where(core == 0, both[..., 0], both[..., 1])
    mask = both.transpose(0, 2, 3, 1).reshape(NQ, NK)
    pairs, count = list_pairs(mask)
    info = jnp.concatenate([jnp.stack([count, core, x, z]), pairs])

    sent_parts = call_stats(info, q_all, k_all)
    parts = lax.all_to_all(sent_parts, ("c", "z"), 0, 0, tiled=True)
    kept, sent = call_query(info, q_all, k_all, v_all, sent_parts)
    got = swap_cores(sent)

    statistics = call_combine(info, parts)
    chip, *parts = call_key(info, q_all, k_all, v_all, statistics, kept, got)

    dq_own = lax.psum_scatter(chip, "z", scatter_dimension=0, tiled=True)[0]
    query_grad, over_y = lax.optimization_barrier(
        (call_finish_queries(dq_own), sum_over_keys(*parts))
    )
    return query_grad, *call_finish_keys(over_y)


def solution(mesh):
    torus = Mesh(mesh.devices.reshape(4, 4, 2, 2, 8), ("x", "yl", "c", "yh", "z"))
    queries = P(("x", "yl", "c", "yh", "z"), None)
    keys = P(("yh", "z", "x", "yl", "c"), None)
    return jax.shard_map(
        body,
        mesh=torus,
        in_specs=(queries, queries, queries, keys, keys, P(("x", "yl", "c"), ("yh", "z"))),
        out_specs=(queries, keys, keys),
        check_vma=False,
    )
```
